32 devices in a mesh: dp: 8 (over z, x), tensor: 4 (over y, core).
Axes of the slice: x: 2, y: 2, z: 4, core: 2. Of those that a mesh axis runs over, the one named last changes fastest.
Arguments:
- tokens: bfloat16 [24576, 768], P('dp'), may hold values from -6 to 6
- cotangent: bfloat16 [24576, 768], P('dp'), may hold values from -6 to 6
- documents: int32 [24, 1024], P('dp'), may hold values from 0 to 7, never falling along the last dimension, each value on 1 to 512 neighbouring positions
- w_qkv: float32 [768, 3, 768], P('dp', None, 'tensor'), may hold values from -0.21875 to 0.21875
- w_out: float32 [768, 768], P('tensor', 'dp'), may hold values from -0.625 to 0.625
- w_fc: float32 [768, 3072], P('dp', 'tensor'), may hold values from -0.21875 to 0.21875
- w_proj: float32 [3072, 768], P('tensor', 'dp'), may hold values from -0.109375 to 0.109375
- vectors: float32 [12, 768], P(None, 'dp'), may hold values from -4 to 4, as said below
- first_qkv: float32 [768, 3, 768], P('dp', None, 'tensor'), may hold values from -0.00025017266 to 0.00025017266
- first_out: float32 [768, 768], P('tensor', 'dp'), may hold values from -0.00025017266 to 0.00025017266
- first_fc: float32 [768, 3072], P('dp', 'tensor'), may hold values from -0.00025017266 to 0.00025017266
- first_proj: float32 [3072, 768], P('tensor', 'dp'), may hold values from -0.00025017266 to 0.00025017266
- first_vec: float32 [12, 768], P(None, 'dp'), may hold values from -0.00090152305 to 0.00090152305
- second_qkv: float32 [768, 3, 768], P('dp', None, 'tensor'), may hold values from 7.0550676e-11 to 1.1288108e-09
- second_out: float32 [768, 768], P('tensor', 'dp'), may hold values from 7.0550676e-11 to 1.1288108e-09
- second_fc: float32 [768, 3072], P('dp', 'tensor'), may hold values from 7.0550676e-11 to 1.1288108e-09
- second_proj: float32 [3072, 768], P('tensor', 'dp'), may hold values from 7.0550676e-11 to 1.1288108e-09
- second_vec: float32 [12, 768], P(None, 'dp'), may hold values from 1.1288108e-09 to 1.8060973e-08
Outputs:
- output: bfloat16 [24576, 768], P('dp')
- input_grad: bfloat16 [24576, 768], P('dp')
- grad_norm: float32 [], replicated
- new_qkv: float32 [768, 3, 768], P('dp', None, 'tensor')
- new_out: float32 [768, 768], P('tensor', 'dp')
- new_fc: float32 [768, 3072], P('dp', 'tensor')
- new_proj: float32 [3072, 768], P('tensor', 'dp')
- new_vectors: float32 [12, 768], P(None, 'dp')
- mean_qkv: float32 [768, 3, 768], P('dp', None, 'tensor')
- mean_out: float32 [768, 768], P('tensor', 'dp')
- mean_fc: float32 [768, 3072], P('dp', 'tensor')
- mean_proj: float32 [3072, 768], P('tensor', 'dp')
- mean_vectors: float32 [12, 768], P(None, 'dp')
- square_qkv: float32 [768, 3, 768], P('dp', None, 'tensor')
- square_out: float32 [768, 768], P('tensor', 'dp')
- square_fc: float32 [768, 3072], P('dp', 'tensor')
- square_proj: float32 [3072, 768], P('tensor', 'dp')
- square_vectors: float32 [12, 768], P(None, 'dp')
The draws below stay inside these ranges and needn't reach their ends.
Inputs may be any that keep to these rules, and one draw needn't show every extreme that they name: `documents`: document numbers never fall along a row; each document has 1 to 512 tokens, and some document of each row has exactly 512. `vectors`: gains near one and biases of order one.
All inputs are finite; a program needn't handle non-finite values.
Results may differ from the reference program's by a relative error of at most 0.02.
Values may be sent and summed in bfloat16 or wider, within the bound.
A program may use at most 192 MiB of HBM per device.

```python
import math
import jax
import jax.numpy as jnp
import numpy as np
from jax import lax

D = 768
H = 12
HD = 64
FF = 3072
LEN = 1024
DOCS = 8
STEP = 10
MOST = 512
NV = 12
SEQS = 24
TOKENS = 24576
NPARAM = 7087104


def draw_vectors(key, part):
    key = jax.random.fold_in(key, 7)
    key_one, key_two, key_three = jax.random.split(key, 3)
    across = jnp.arange(D, dtype=jnp.float32) / (D - 1)
    rough = jax.random.uniform(key_one, (2, D), jnp.float32, 0.8, 1.25)
    gains = (0.6 + 1.2 * across) * rough
    spread = 0.3
    noise = jax.random.truncated_normal(key_two, -3.0, 3.0, (6, D), jnp.float32)
    value_bias = noise[3] * (0.2 + across)
    hidden_ramp = jnp.arange(FF, dtype=jnp.float32) / (FF - 1)
    fc_bias = 1.5 * hidden_ramp - 0.5 + 0.3 * jax.random.truncated_normal(key_three, -3.0, 3.0, (FF,), jnp.float32)
    first_rows = jnp.stack([gains[0], spread * noise[0], spread * noise[1], value_bias, spread * noise[2], gains[1], spread * noise[4], spread * noise[5]])
    return jnp.concatenate([first_rows, fc_bias.reshape(FF // D, D)], 0)


def block_levels(stream_key, dims, cuts, low, high):
    level, own = 1.0, jax.random.fold_in(stream_key, 6)
    for axis_at, shards_of in cuts:
        draws = jnp.exp(jax.random.uniform(jax.random.fold_in(own, axis_at), (shards_of,), jnp.float32, low / len(cuts), high / len(cuts)))
        level = level * jnp.repeat(draws, dims[axis_at] // shards_of).reshape([-1 if axis == axis_at else 1 for axis in range(len(dims))])
    return level


def length_profile(number_of, total, reach, slope):
    weights = [(1 << 20) // math.isqrt(rank ** slope) + 1 for rank in range(2, number_of + 1)]
    spare, given = total - reach - (number_of - 1), [1] * (number_of - 1)
    while spare > 0:
        movable = [i for i in range(number_of - 1) if given[i] < reach]
        mass, budget = sum([weights[i] for i in movable]), spare
        for i in movable:
            more = min(reach - given[i], max(1, budget * weights[i] // mass), spare)
            given[i] = given[i] + more
            spare = spare - more
    return np.array([reach] + given)


def uneven_parts(stream_key, amount, total, bound, lean):
    if amount == 2:
        one = jax.random.randint(stream_key, (), max(1, total - bound), min(bound, total - 1) + 1)
        return jnp.stack([one, total - one])
    lengths = jnp.asarray(length_profile(amount, total, bound, lean), jnp.int32)
    couples = (amount - 1) // 2
    source_of, taker = lengths[1:1 + 2 * couples:2], lengths[2:2 + 2 * couples:2]
    margin = jnp.minimum(source_of - 1, bound - taker)
    moved = jax.random.randint(jax.random.fold_in(stream_key, 1), (couples,), 0, 1 << 20) % (margin + 1)
    lengths = lengths.at[1:1 + 2 * couples:2].set(source_of - moved).at[2:2 + 2 * couples:2].set(taker + moved)
    return lengths[jax.random.permutation(jax.random.fold_in(stream_key, 2), amount)]


def bell_draw(stream_key, dims, scale, reach, shards=(), kind=jnp.bfloat16):
    entries = scale * jax.random.normal(stream_key, dims, jnp.float32)
    if shards:
        entries = entries * block_levels(stream_key, dims, shards, -0.22, 0.18)
    return jnp.clip(entries, -reach, reach).astype(kind)


def setup_inputs(seed: int = 0) -> dict:
    seeds = jax.random.split(jax.random.key(seed), 19)
    tokens = bell_draw(seeds[0], (TOKENS, D), 1.0, 6.0, ((0, 8),))
    cotangent = bell_draw(seeds[1], (TOKENS, D), 1.0, 6.0, ((0, 8),))
    documents = jax.vmap(lambda own: jnp.searchsorted(jnp.cumsum(uneven_parts(own, DOCS, LEN, MOST, 0)), jnp.arange(LEN), side="right"))(jax.random.split(seeds[2], SEQS)).reshape((SEQS, LEN)).astype(jnp.int32)
    w_qkv = bell_draw(seeds[3], (D, 3, D), D ** -0.5, 0.21875, ((0, 8), (2, 4)), jnp.float32)
    w_out = bell_draw(seeds[4], (D, D), (D // 8) ** -0.5, 0.625, ((0, 4), (1, 8)), jnp.float32)
    w_fc = bell_draw(seeds[5], (D, FF), D ** -0.5, 0.21875, ((0, 8), (1, 4)), jnp.float32)
    w_proj = bell_draw(seeds[6], (FF, D), FF ** -0.5, 0.109375, ((0, 4), (1, 8)), jnp.float32)
    vectors = draw_vectors(jax.random.fold_in(seeds[18], 71), 0)
    first_qkv = bell_draw(seeds[8], (D, 3, D), (0.111 / NPARAM ** 0.5), 0.00025017266, ((0, 8), (2, 4)), jnp.float32)
    first_out = bell_draw(seeds[9], (D, D), (0.111 / NPARAM ** 0.5), 0.00025017266, ((0, 4), (1, 8)), jnp.float32)
    first_fc = bell_draw(seeds[10], (D, FF), (0.111 / NPARAM ** 0.5), 0.00025017266, ((0, 8), (1, 4)), jnp.float32)
    first_proj = bell_draw(seeds[11], (FF, D), (0.111 / NPARAM ** 0.5), 0.00025017266, ((0, 4), (1, 8)), jnp.float32)
    first_vec = bell_draw(seeds[12], (NV, D), (0.4 / NPARAM ** 0.5), 0.00090152305, ((1, 8),), jnp.float32)
    second_qkv = jnp.clip(jnp.exp(math.log(1.1288108225926408e-09) - 2.7725887 * jax.random.uniform(seeds[13], (D, 3, D), jnp.float32) ** block_levels(seeds[13], (D, 3, D), ((0, 8), (2, 4)), -0.2, 0.2)), 7.055067641204005e-11, 1.1288108225926408e-09)
    second_out = jnp.clip(jnp.exp(math.log(1.1288108225926408e-09) - 2.7725887 * jax.random.uniform(seeds[14], (D, D), jnp.float32) ** block_levels(seeds[14], (D, D), ((0, 4), (1, 8)), -0.2, 0.2)), 7.055067641204005e-11, 1.1288108225926408e-09)
    second_fc = jnp.clip(jnp.exp(math.log(1.1288108225926408e-09) - 2.7725887 * jax.random.uniform(seeds[15], (D, FF), jnp.float32) ** block_levels(seeds[15], (D, FF), ((0, 8), (1, 4)), -0.2, 0.2)), 7.055067641204005e-11, 1.1288108225926408e-09)
    second_proj = jnp.clip(jnp.exp(math.log(1.1288108225926408e-09) - 2.7725887 * jax.random.uniform(seeds[16], (FF, D), jnp.float32) ** block_levels(seeds[16], (FF, D), ((0, 4), (1, 8)), -0.2, 0.2)), 7.055067641204005e-11, 1.1288108225926408e-09)
    second_vec = jnp.clip(jnp.exp(math.log(1.8060973161482252e-08) - 2.7725887 * jax.random.uniform(seeds[17], (NV, D), jnp.float32) ** block_levels(seeds[17], (NV, D), ((1, 8),), -0.2, 0.2)), 1.1288108225926408e-09, 1.8060973161482252e-08)
    return {"tokens": tokens, "cotangent": cotangent, "documents": documents, "w_qkv": w_qkv, "w_out": w_out, "w_fc": w_fc, "w_proj": w_proj, "vectors": vectors, "first_qkv": first_qkv, "first_out": first_out, "first_fc": first_fc, "first_proj": first_proj, "first_vec": first_vec, "second_qkv": second_qkv, "second_out": second_out, "second_fc": second_fc, "second_proj": second_proj, "second_vec": second_vec}


@jax.custom_vjp
def low(v):
    return lax.optimization_barrier(v.astype(jnp.bfloat16)).astype(jnp.float32)

@jax.custom_vjp
def low_back(v):
    return v

def low_keep(v):
    return (low(v), None)

def low_pass(kept, grad):
    return (grad,)

def back_keep(v):
    return (v, None)

def back_low(kept, grad):
    return (low(grad),)
low.defvjp(low_keep, low_pass)
low_back.defvjp(back_keep, back_low)
beta_one = 0.9
beta_two = 0.999
rate_qkv = 0.03
rate_out = 0.08
rate_fc = 0.03
rate_proj = 0.02
rate_vec = 0.6
decay_rate = 0.01
epsilon = 1e-08
max_norm = 1.0

def normalize(hidden, gain_row, bias_row):
    average = lax.optimization_barrier(jnp.mean(hidden, -1, keepdims=True))
    centred = hidden - average
    variance = lax.optimization_barrier(jnp.mean(centred * centred, -1, keepdims=True))
    return centred * lax.rsqrt(variance + 1e-05) * gain_row + bias_row

def product(left, right):
    return jnp.dot(left, right, precision=lax.Precision.HIGHEST)

def attend(pieces):
    queries, key_rows, value_rows, doc_ids = pieces
    raw_scores = jnp.einsum('qhe,khe->hqk', queries, key_rows, precision=lax.Precision.HIGHEST)
    scores = low_back(raw_scores * (1.0 / math.sqrt(HD)))
    places = jnp.arange(LEN)
    allowed = (doc_ids[:, None] == doc_ids[None, :]) & (places[:, None] >= places[None, :])
    scores = jnp.where(allowed[None], scores, -1e+30)
    highest = lax.optimization_barrier(jnp.max(scores, -1, keepdims=True))
    exponent = jnp.exp(scores - highest)
    attention_weights = low(exponent / lax.optimization_barrier(jnp.sum(exponent, -1, keepdims=True)))
    return jnp.einsum('hqk,khe->qhe', attention_weights, value_rows, precision=lax.Precision.HIGHEST)

def forward(inputs, w_qkv, w_out, w_fc, w_proj, vectors, documents):
    tok_count = inputs.shape[0]
    normed = low(normalize(inputs, vectors[0], vectors[1]))
    joined_rows = product(normed, w_qkv.reshape(D, 3 * D))
    queries = low(low_back(joined_rows[:, :D] + vectors[2]))
    key_rows = low(low_back(joined_rows[:, D:2 * D]))
    value_rows = low(low_back(joined_rows[:, 2 * D:] + vectors[3]))
    split_shape = (tok_count // LEN, LEN, H, HD)
    context = lax.map(jax.checkpoint(attend), (queries.reshape(split_shape), key_rows.reshape(split_shape), value_rows.reshape(split_shape), documents))
    context = low(low_back(context.reshape(tok_count, D)))
    middle = inputs + low_back(product(context, w_out)) + vectors[4]
    normed_two = low(normalize(middle, vectors[5], vectors[6]))
    pre_act = low_back(product(normed_two, w_fc) + vectors[8:].reshape(FF))
    activated = low(low_back(jax.nn.gelu(pre_act, approximate=True)))
    return middle + low_back(product(activated, w_proj)) + vectors[7]

def adam_step(weight, gradient, first, second, rate, decay):
    first = beta_one * first + (1.0 - beta_one) * gradient
    second = beta_two * second + (1.0 - beta_two) * gradient * gradient
    first_hat = first / (1.0 - beta_one ** STEP)
    second_hat = second / (1.0 - beta_two ** STEP)
    weight = weight - rate * (first_hat / (jnp.sqrt(second_hat) + epsilon) + decay * weight)
    return (weight, first, second)

def reference(tokens, cotangent, documents, w_qkv, w_out, w_fc, w_proj, vectors, first_qkv, first_out, first_fc, first_proj, first_vec, second_qkv, second_out, second_fc, second_proj, second_vec):
    inputs = tokens.astype(jnp.float32)
    low_qkv = w_qkv.astype(jnp.bfloat16).astype(jnp.float32)
    low_out = w_out.astype(jnp.bfloat16).astype(jnp.float32)
    low_fc = w_fc.astype(jnp.bfloat16).astype(jnp.float32)
    low_proj = w_proj.astype(jnp.bfloat16).astype(jnp.float32)
    low_vec = vectors.astype(jnp.bfloat16).astype(jnp.float32)

    def wrapped(inputs_in, qkv_in, out_in, fc_in, proj_in, vec_in):
        return forward(inputs_in, qkv_in, out_in, fc_in, proj_in, vec_in, documents)
    result, pull_back = jax.vjp(wrapped, inputs, low_qkv, low_out, low_fc, low_proj, low_vec)
    gradients = pull_back(cotangent.astype(jnp.float32))
    squares = jnp.float32(0.0)
    for gradient in gradients[1:]:
        squares = squares + jnp.sum(gradient * gradient)
    global_norm = jnp.sqrt(squares)
    clip_factor = max_norm / jnp.maximum(global_norm, max_norm)
    new_qkv, mean_qkv, square_qkv = adam_step(w_qkv, gradients[1] * clip_factor, first_qkv, second_qkv, rate_qkv, decay_rate)
    new_out, mean_out, square_out = adam_step(w_out, gradients[2] * clip_factor, first_out, second_out, rate_out, decay_rate)
    new_fc, mean_fc, square_fc = adam_step(w_fc, gradients[3] * clip_factor, first_fc, second_fc, rate_fc, decay_rate)
    new_proj, mean_proj, square_proj = adam_step(w_proj, gradients[4] * clip_factor, first_proj, second_proj, rate_proj, decay_rate)
    new_vec, mean_vec, square_vec = adam_step(vectors, gradients[5] * clip_factor, first_vec, second_vec, rate_vec, 0.0)
    return (result.astype(jnp.bfloat16), gradients[0].astype(jnp.bfloat16), global_norm, new_qkv, new_out, new_fc, new_proj, new_vec, mean_qkv, mean_out, mean_fc, mean_proj, mean_vec, square_qkv, square_out, square_fc, square_proj, square_vec)
```

```python
import functools
import math

import jax
import jax.numpy as jnp
from jax import lax
from jax.experimental import pallas as pl
from jax.experimental.pallas import tpu as pltpu
from jax.sharding import PartitionSpec as P

D = 768
HD = 64
FF = 3072
STEP = 10
PREV = 512
BLK = 256
LANES = 128

beta_one = 0.9
beta_two = 0.999
rate_qkv = 0.03
rate_out = 0.08
rate_fc = 0.03
rate_proj = 0.02
rate_vec = 0.6
decay_rate = 0.01
epsilon = 1e-08
max_norm = 1.0

BF = jnp.bfloat16
F32 = jnp.float32
VMEM_LIMIT = 62 * 2**20
ANY = pl.BlockSpec(memory_space=pl.ANY)
VM = pl.BlockSpec(memory_space=pltpu.VMEM)
GELU_C = math.sqrt(2.0 / math.pi)


def nn(a, b):
    return lax.dot_general(a, b, (((1,), (0,)), ((), ())), preferred_element_type=F32)


def nt(a, b):
    return lax.dot_general(a, b, (((1,), (1,)), ((), ())), preferred_element_type=F32)


MESH = pl.DeviceIdType.MESH


def wait_bytes(ref, sem):
    pltpu.make_async_copy(ref, ref, sem).wait()


def positions():
    d, t = lax.axis_index("dp"), lax.axis_index("tensor")
    return d, t, lax.rem(d, 2), d // 2, t // 2, lax.rem(t, 2)


class Gather:
    Z, X0, Y1, Y0, X1, X1U, C, CU = range(8)

    def __init__(self, n_dp, blk, vecb, w, vecg, send, recv, loc, vsend, vrecv):
        self.n_dp, self.blk, self.vecb, self.w, self.vecg = n_dp, blk, vecb, w, vecg
        self.send, self.recv, self.loc, self.vsend, self.vrecv = send, recv, loc, vsend, vrecv
        self.rows = blk.shape[1]
        self.nz = n_dp // 2
        self.d, self.t, self.x, self.z, self.y, self.c = positions()
        self.to_x = (self.d + 1 - 2 * self.x, self.t)
        self.to_y = (self.d, self.t + 2 - 4 * self.y)
        self.to_c = (self.d, self.t + 1 - 2 * self.c)
        self.u = self.t + 2 - 4 * self.y
        self.half = D // 2

    def dp_peers(self):
        return [(lax.rem(self.d + k, self.n_dp), self.t) for k in range(1, self.n_dp)]

    def at(self, m, t, block, lanes):
        return self.w.at[m, t, pl.ds(pl.multiple_of(block * self.rows, self.rows), self.rows), lanes]

    def copy(self, m, stage, src, dst, dev):
        pltpu.make_async_remote_copy(
            src_ref=src, dst_ref=dst, send_sem=self.send.at[m, stage], recv_sem=self.recv.at[m, stage],
            device_id=dev, device_id_type=MESH,
        ).start()

    def size(self, m, stage):
        rows = (self.nz - 1) * self.rows if stage == self.Z else self.nz * self.rows
        if stage in (self.Y0, self.C, self.CU):
            rows = D
        lanes = self.half if stage in (self.X0, self.Y1, self.Y0, self.X1, self.X1U) else D
        return self.w.at[m, 0, pl.ds(0, rows), pl.ds(0, lanes)]

    def got(self, m, stage):
        wait_bytes(self.size(m, stage), self.recv.at[m, stage])

    def begin(self):
        barrier = pltpu.get_barrier_semaphore()
        peers = self.dp_peers() + [self.to_y, self.to_c]
        for dev in peers:
            pl.semaphore_signal(barrier, inc=1, device_id=dev, device_id_type=MESH)
        for m in range(3):
            pltpu.make_async_copy(self.blk.at[m], self.at(m, self.t, self.d, pl.ds(0, D)), self.loc.at[m]).start()
        pl.semaphore_wait(barrier, len(peers))
        for dev in self.dp_peers():
            pltpu.make_async_remote_copy(
                src_ref=self.vecb, dst_ref=self.vecg.at[self.d], send_sem=self.vsend, recv_sem=self.vrecv,
                device_id=dev, device_id_type=MESH,
            ).start()
        self.vecg[self.d] = self.vecb[...]
        self.along_z(0)

    def vectors(self):
        wait_bytes(self.vecg.at[pl.ds(0, self.n_dp - 1)], self.vrecv)
        width = D // self.n_dp
        lane = lax.broadcasted_iota(jnp.int32, (LANES, D), 0)
        col = lax.broadcasted_iota(jnp.int32, (LANES, D), 1)
        total = jnp.zeros((16, D), F32)
        for p in range(self.n_dp):
            pick = jnp.where((col == lane + p * width) & (lane < width), 1.0, 0.0).astype(BF)
            total += nn(self.vecg[p], pick)
        return total

    def along_z(self, m):
        for k in range(1, self.nz):
            dev = (lax.rem(self.d + 2 * k, self.n_dp), self.t)
            self.copy(m, self.Z, self.blk.at[m], self.at(m, self.t, self.d, pl.ds(0, D)), dev)

    def columns(self, m, stage, t, lanes, dev):
        for zz in range(self.nz):
            ref = self.at(m, t, 2 * zz + self.x, lanes)
            self.copy(m, stage, ref, ref, dev)

    def after_z(self, m):
        self.got(m, self.Z)
        pltpu.make_async_copy(self.blk.at[m], self.blk.at[m], self.loc.at[m]).wait()
        low, high = pl.ds(0, self.half), pl.ds(self.half, self.half)
        self.columns(m, self.Y1, self.t, high, self.to_y)
        self.columns(m, self.X0, self.t, low, self.to_x)
        self.columns(m, self.X1, self.t, high, self.to_x)

    def after_y1(self, m):
        self.got(m, self.Y1)
        self.columns(m, self.X1U, self.u, pl.ds(self.half, self.half), self.to_x)

    def after_x0(self, m):
        self.got(m, self.X0)
        ref = self.w.at[m, self.t, :, pl.ds(0, self.half)]
        self.copy(m, self.Y0, ref, ref, self.to_y)

    def after_x1(self, m):
        self.got(m, self.X1)
        ref = self.w.at[m, self.t]
        self.copy(m, self.C, ref, ref, self.to_c)

    def after_last(self, m):
        self.got(m, self.Y0)
        self.got(m, self.X1U)
        ref = self.w.at[m, self.u]
        self.copy(m, self.CU, ref, ref, self.to_c)

    def complete(self, m):
        self.got(m, self.C)
        self.got(m, self.CU)

    def finish(self):
        for m in range(3):
            for stage in range(8):
                wait_bytes(self.size(m, stage), self.send.at[m, stage])
        wait_bytes(self.vecg.at[pl.ds(0, self.n_dp - 1)], self.vsend)


def ln_parts(x):
    mean = jnp.mean(x, -1, keepdims=True)
    centred = x - mean
    inv = lax.rsqrt(jnp.mean(centred * centred, -1, keepdims=True) + 1e-05)
    return centred * inv, inv


def ln_back(e, u, inv):
    return inv * (
        e - jnp.mean(e, -1, keepdims=True) - u * jnp.mean(e * u, -1, keepdims=True)
    )


def group_tiles(rows, group):
    base = (group // 2) * 384
    low = lax.broadcasted_iota(jnp.int32, (rows.shape[0], LANES), 1) < HD
    first = rows[:, base : base + 128]
    second = rows[:, base + 128 : base + 256]
    third = rows[:, base + 256 : base + 384]
    if group % 2 == 0:
        return first, second
    second, third = pltpu.roll(second, HD, 1), pltpu.roll(third, HD, 1)
    return jnp.where(low, second, third), third


def ungroup_tiles(even, odd):
    low = lax.broadcasted_iota(jnp.int32, even[0].shape, 1) < HD
    pair = pltpu.roll(odd[0], HD, 1)
    single = pltpu.roll(odd[1], HD, 1)
    return even[0], jnp.where(low, even[1], pair), jnp.where(low, pair, single)


def fwd_kernel(
    n_dp, w_in, vec_in, tok_hbm, gcol, grow,
    w_hbm, nrm_out, q_out, k_out, v_out, kT_out, ctx_out, mid_out, n2_out, act_out, slope_out, probs_out, out_out,
    xw, nrm, wa, wf, wp, qm, kt, vt, ktT, vtT, ctxT, ctx, mb, mid, n2, acc, act, slope, pst,
    in_sem, w_sem, out_sem, p_sem, *gather_refs,
):
    gather = Gather(n_dp, w_in, vec_in, w_hbm, *gather_refs) if n_dp else None
    if gather:
        gather.begin()
    else:
        w_hbm = w_in
    rank = lax.axis_index("tensor")
    own = xw.shape[0] - PREV
    start = jnp.maximum(rank * own - PREV, 0)
    cp_prev = pltpu.make_async_copy(tok_hbm.at[pl.ds(pl.multiple_of(start, 256), PREV)], xw.at[pl.ds(0, PREV)], in_sem.at[0])
    cp_own = pltpu.make_async_copy(tok_hbm.at[pl.ds(pl.multiple_of(rank * own, 256), own)], xw.at[pl.ds(PREV, own)], in_sem.at[1])
    cp_prev.start()
    cp_own.start()
    outs = []

    def load(m, dst):
        if gather:
            gather.complete(m)
        cps = [pltpu.make_async_copy(w_hbm.at[m, t], dst.at[t], w_sem.at[m, t]) for t in range(4)]
        for cp in cps:
            cp.start()
        return cps

    def put(src, dst):
        cp = pltpu.make_async_copy(src, dst, out_sem.at[len(outs)])
        cp.start()
        outs.append(cp)

    for i in range(3):
        keys = gcol[pl.ds(i * BLK, 3 * BLK), :]
        same = keys == grow[0:1, pl.ds(i * BLK, BLK)]
        row = lax.broadcasted_iota(jnp.int32, (3 * BLK, BLK), 0)
        col = lax.broadcasted_iota(jnp.int32, (3 * BLK, BLK), 1)
        mb[i] = jnp.where(same & (row <= col + PREV), 0.0, -1e30).astype(F32)
    cp_prev.wait()
    cp_own.wait()
    vec = gather.vectors() if gather else vec_in[...]

    def ln_one(r, _):
        rows = pl.ds(pl.multiple_of(r * 128, 128), 128)
        u, _inv = ln_parts(xw[rows, :].astype(F32))
        nrm[rows, :] = (u * vec[0:1] + vec[1:2]).astype(BF)
        return 0

    lax.fori_loop(0, xw.shape[0] // 128, ln_one, 0)
    put(nrm, nrm_out)
    if gather:
        gather.after_z(0)
        gather.along_z(1)
        gather.after_y1(0)
        gather.after_x0(0)
        gather.after_z(1)
        gather.along_z(2)
        gather.after_x1(0)
        gather.after_last(0)
        gather.after_y1(1)
        gather.after_x0(1)
    loads = load(0, wa)
    low = lax.broadcasted_iota(jnp.int32, (BLK, LANES), 1) < HD
    for g in range(4):
        loads[g].wait()
        pair, single = group_tiles(vec[0:8], g)
        bq_pair, bq_single, bv_pair, bv_single = pair[2:3], single[2:3], pair[3:4], single[3:4]

        def qkv(rc, _):
            rows = pl.ds(pl.multiple_of(rc * BLK, BLK), BLK)
            x = nrm[rows, :]
            one = nn(x, wa[g, :, 0:384])
            two = nn(x, wa[g, :, 512:768])
            k_pair = one[:, 128:256].astype(BF)
            v_pair = (one[:, 256:384] + bv_pair).astype(BF)
            kt[2 * g, rows, :] = k_pair
            vt[2 * g, rows, :] = v_pair
            ktT[2 * g, :, rows] = k_pair.T
            vtT[2 * g, :, rows] = v_pair.T
            qk, vo = two[:, 0:128], two[:, 128:256]
            k_single = jnp.where(low, pltpu.roll(qk, HD, 1), 0.0).astype(BF)
            v_single = jnp.where(low, vo + bv_single, 0.0)
            kt[2 * g + 1, rows, :] = k_single
            vt[2 * g + 1, rows, :] = pltpu.roll(v_single, HD, 1).astype(BF)
            ktT[2 * g + 1, :, rows] = k_single.T
            vtT[2 * g + 1, :, rows] = v_single.astype(BF).T

            @pl.when(rc >= PREV // BLK)
            def _():
                orows = pl.ds(pl.multiple_of(rc * BLK - PREV, BLK), BLK)
                q_pair = (one[:, 0:128] + bq_pair).astype(BF).astype(F32) * 0.125
                q_single = (qk + bq_single).astype(BF).astype(F32) * 0.125
                qm[3 * g, orows, :] = jnp.where(low, q_pair, 0.0).astype(BF)
                qm[3 * g + 1, orows, :] = jnp.where(low, 0.0, q_pair).astype(BF)
                qm[3 * g + 2, orows, :] = jnp.where(low, q_single, 0.0).astype(BF)

            return 0

        lax.fori_loop(0, nrm.shape[0] // BLK, qkv, 0)
    put(qm, q_out)
    put(kt, k_out)
    put(vt, v_out)
    put(ktT, kT_out)

    def attend(h, _):
        g, hh = h // 3, lax.rem(h, 3)
        tile = 2 * g + hh // 2
        src_half = pl.multiple_of(jnp.where(hh == 1, HD, 0), HD)
        dst_half = pl.multiple_of(jnp.where(hh == 0, 0, HD), HD)
        slot = lax.rem(h, 2)

        @pl.when(h >= 2)
        def _():
            pltpu.make_async_copy(pst.at[slot], probs_out.at[h - 2], p_sem.at[slot]).wait()

        for i in range(3):
            keys = pl.ds(i * BLK, 3 * BLK)
            mine = pl.ds(i * BLK, BLK)
            s = nt(kt[tile, keys, :], qm[h, mine, :]) + mb[i]
            p = jnp.exp(s - jnp.max(s, 0, keepdims=True))
            pb = (p * (1.0 / jnp.sum(p, 0, keepdims=True))).astype(BF)
            pst[slot, i] = pb
            o = nn(vtT[tile, pl.ds(src_half, HD), keys], pb)
            ctxT[tile, pl.ds(dst_half, HD), mine] = o.astype(BF)
        pltpu.make_async_copy(pst.at[slot], probs_out.at[h], p_sem.at[slot]).start()
        return 0

    if gather:
        gather.after_z(2)
        gather.after_x1(1)
        gather.after_last(1)
        gather.after_y1(2)
        gather.after_x0(2)
    for g in range(4):
        ctxT[2 * g + 1, 0:HD, :] = jnp.zeros((HD, own), BF)
    lax.fori_loop(0, 12, attend, 0)
    for t in range(8):
        ctx[t] = ctxT[t].T
    put(ctx, ctx_out)

    def out_proj(rc, _):
        rows = pl.ds(pl.multiple_of(rc * BLK, BLK), BLK)
        total = xw[pl.ds(pl.multiple_of(rc * BLK + PREV, BLK), BLK), :].astype(F32) + vec[4:5]
        for g in range(4):
            total += nt(ctx[2 * g, rows, :], wa[g, :, 384:512])
            total += nt(ctx[2 * g + 1, rows, :], wa[g, :, 640:768])
        mid[rows, :] = total
        u, _inv = ln_parts(total)
        n2[rows, :] = (u * vec[5:6] + vec[6:7]).astype(BF)
        acc[rows, :] = total + vec[7:8]
        return 0

    lax.fori_loop(0, own // BLK, out_proj, 0)
    put(mid, mid_out)
    put(n2, n2_out)
    loads = load(1, wf)
    if gather:
        gather.after_x1(2)
        gather.after_last(2)
    loads += load(2, wp)
    for t in range(4):
        loads[t].wait()
        loads[4 + t].wait()
        bias = vec[8 + t : 9 + t]

        def mlp(rc, _):
            rows = pl.ds(pl.multiple_of(rc * BLK, BLK), BLK)
            z = nn(n2[rows, :], wf[t]) + bias
            th = jnp.tanh(GELU_C * (z + 0.044715 * z * z * z))
            half = 0.5 * (1.0 + th)
            low_act = (z * half).astype(BF)
            act[t, rows, :] = low_act
            slope[t, rows, :] = (
                half + 0.5 * z * (1.0 - th * th) * (GELU_C * (1.0 + 3 * 0.044715 * z * z))
            ).astype(BF)
            acc[rows, :] += nt(low_act, wp[t])
            return 0

        lax.fori_loop(0, own // BLK, mlp, 0)
        put(act.at[t], act_out.at[t])
        put(slope.at[t], slope_out.at[t])
    xw[0:own, :] = acc[...].astype(BF)
    put(xw.at[pl.ds(0, own)], out_out)
    for slot in range(2):
        pltpu.make_async_copy(pst.at[slot], probs_out.at[0], p_sem.at[slot]).wait()
    for cp in outs:
        cp.wait()
    if gather:
        gather.finish()


def forward(n_dp, w_in, vec, tokens, gcol, grow, own):
    win = own + PREV
    sds = jax.ShapeDtypeStruct
    out_shape = [
        sds((3, 4, D, D) if n_dp else (8, LANES), BF),
        sds((win, D), BF), sds((12, own, LANES), BF), sds((8, win, LANES), BF), sds((8, win, LANES), BF),
        sds((8, LANES, win), BF), sds((8, own, LANES), BF), sds((own, D), F32), sds((own, D), BF),
        sds((4, own, D), BF), sds((4, own, D), BF), sds((12, 3, 3 * BLK, BLK), BF), sds((own, D), BF),
    ]
    scratch = [
        pltpu.VMEM((win, D), BF), pltpu.VMEM((win, D), BF),
        pltpu.VMEM((4, D, D), BF), pltpu.VMEM((4, D, D), BF), pltpu.VMEM((4, D, D), BF),
        pltpu.VMEM((12, own, LANES), BF), pltpu.VMEM((8, win, LANES), BF), pltpu.VMEM((8, win, LANES), BF),
        pltpu.VMEM((8, LANES, win), BF), pltpu.VMEM((8, LANES, win), BF),
        pltpu.VMEM((8, LANES, own), BF), pltpu.VMEM((8, own, LANES), BF),
        pltpu.VMEM((3, 3 * BLK, BLK), F32), pltpu.VMEM((own, D), F32), pltpu.VMEM((own, D), BF),
        pltpu.VMEM((own, D), F32), pltpu.VMEM((4, own, D), BF), pltpu.VMEM((4, own, D), BF),
        pltpu.VMEM((2, 3, 3 * BLK, BLK), BF),
        pltpu.SemaphoreType.DMA((2,)), pltpu.SemaphoreType.DMA((3, 4)), pltpu.SemaphoreType.DMA((24,)),
        pltpu.SemaphoreType.DMA((2,)),
    ]
    params = {}
    if n_dp:
        scratch += [
            pltpu.VMEM((n_dp, 16, LANES), BF), pltpu.SemaphoreType.DMA((3, 8)), pltpu.SemaphoreType.DMA((3, 8)),
            pltpu.SemaphoreType.DMA((3,)), pltpu.SemaphoreType.DMA, pltpu.SemaphoreType.DMA,
        ]
        params = dict(collective_id=1, has_side_effects=True)
    return pl.pallas_call(
        functools.partial(fwd_kernel, n_dp),
        out_shape=out_shape,
        in_specs=[ANY, VM, ANY, VM, VM],
        out_specs=[ANY] * len(out_shape),
        scratch_shapes=scratch,
        compiler_params=pltpu.CompilerParams(vmem_limit_bytes=VMEM_LIMIT, **params),
        name="forward",
    )(w_in, vec, tokens, gcol, grow)


def pack_blocks(w_qkv, w_out, w_fc, w_proj):
    q, k, v, o = w_qkv[:, 0], w_qkv[:, 1], w_qkv[:, 2], w_out.T
    pairs = [a[:, :128] for a in (q, k, v, o)]
    singles = [a[:, 128:] for a in (q, k, v, o)]
    return jnp.stack([jnp.concatenate(pairs + singles, 1), w_fc, w_proj.T]).astype(BF)


def doc_inputs(documents, own):
    rank = lax.axis_index("tensor")
    rows = documents.shape[0]
    gid = (documents + 8 * jnp.arange(rows, dtype=jnp.int32)[:, None]).reshape(-1)
    padded = jnp.concatenate([jnp.full((PREV,), -1, jnp.int32), gid])
    win = lax.dynamic_slice_in_dim(padded, rank * own, own + PREV)
    mine = lax.dynamic_slice_in_dim(gid, rank * own, own)
    return win[:, None], jnp.broadcast_to(mine[None], (8, own))


def normalize(hidden, gain_row, bias_row):
    average = jnp.mean(hidden, -1, keepdims=True)
    centred = hidden - average
    inverse = lax.rsqrt(jnp.mean(centred * centred, -1, keepdims=True) + 1e-05)
    normed_unit = centred * inverse
    return (normed_unit * gain_row + bias_row, normed_unit, inverse)


def normalize_back(grad_rows, normed_unit, inverse, gain_row):
    scaled = grad_rows * gain_row
    return inverse * (
        scaled
        - jnp.mean(scaled, -1, keepdims=True)
        - normed_unit * jnp.mean(scaled * normed_unit, -1, keepdims=True)
    )


def gelu_tanh(values):
    return jax.nn.gelu(values, approximate=True)


def masked_scores(queries, key_rows, doc_ids):
    raw_scores = jnp.einsum("qhe,khe->hqk", queries, key_rows, preferred_element_type=jnp.float32)
    places = jnp.arange(doc_ids.shape[0])
    allowed = (doc_ids[:, None] == doc_ids[None, :]) & (places[:, None] >= places[None, :])
    return jnp.where(allowed[None], raw_scores * (1.0 / math.sqrt(HD)), -1e30)


def attend_forward(pieces):
    queries, key_rows, value_rows, doc_ids = pieces
    scores = masked_scores(queries, key_rows, doc_ids)
    highest = jnp.max(scores, -1, keepdims=True)
    exponent = jnp.exp(scores - highest)
    totals = jnp.sum(exponent, -1, keepdims=True)
    attention_weights = (exponent / totals).astype(jnp.bfloat16)
    context = jnp.einsum(
        "hqk,khe->qhe", attention_weights, value_rows, preferred_element_type=jnp.float32
    )
    return (context, (highest + jnp.log(totals))[..., 0])


def attend_backward(pieces):
    queries, key_rows, value_rows, grad_context, doc_ids, log_sums = pieces
    scores = masked_scores(queries, key_rows, doc_ids)
    exact_weights = jnp.exp(scores - log_sums[..., None])
    grad_weights = jnp.einsum(
        "qhe,khe->hqk", grad_context, value_rows, preferred_element_type=jnp.float32
    )
    centre = jnp.sum(exact_weights * grad_weights, -1, keepdims=True)
    grad_scores = (exact_weights * (grad_weights - centre)).astype(jnp.bfloat16)
    grad_values = jnp.einsum(
        "hqk,qhe->khe",
        exact_weights.astype(jnp.bfloat16),
        grad_context,
        preferred_element_type=jnp.float32,
    ).astype(jnp.bfloat16)
    grad_queries = (
        jnp.einsum("hqk,khe->qhe", grad_scores, key_rows, preferred_element_type=jnp.float32)
        * (1.0 / math.sqrt(HD))
    ).astype(jnp.bfloat16)
    grad_keys = (
        jnp.einsum("hqk,qhe->khe", grad_scores, queries, preferred_element_type=jnp.float32)
        * (1.0 / math.sqrt(HD))
    ).astype(jnp.bfloat16)
    return (grad_queries, grad_keys, grad_values)


def adam_step(weight, gradient, first, second, rate, decay):
    first = beta_one * first + (1.0 - beta_one) * gradient
    second = beta_two * second + (1.0 - beta_two) * gradient * gradient
    first_hat = first / (1.0 - beta_one**STEP)
    second_hat = second / (1.0 - beta_two**STEP)
    weight = weight - rate * (first_hat / (jnp.sqrt(second_hat) + epsilon) + decay * weight)
    return (weight, first, second)


def body(
    tokens,
    cotangent,
    documents,
    w_qkv,
    w_out,
    w_fc,
    w_proj,
    vectors,
    first_qkv,
    first_out,
    first_fc,
    first_proj,
    first_vec,
    second_qkv,
    second_out,
    second_fc,
    second_proj,
    second_vec,
):
    tensor_rank = lax.axis_index("tensor")
    head_only = jnp.where(tensor_rank == 0, 1.0, 0.0).astype(jnp.float32)
    full_qkv, full_out, full_fc, full_proj, full_vec = (
        lax.all_gather(w_qkv.astype(jnp.bfloat16), "dp", axis=0, tiled=True),
        lax.all_gather(w_out.astype(jnp.bfloat16), "dp", axis=1, tiled=True),
        lax.all_gather(w_fc.astype(jnp.bfloat16), "dp", axis=0, tiled=True),
        lax.all_gather(w_proj.astype(jnp.bfloat16), "dp", axis=1, tiled=True),
        lax.all_gather(vectors.astype(jnp.bfloat16), "dp", axis=1, tiled=True),
    )
    local_width = full_qkv.shape[2]
    hidden_width = full_fc.shape[1]
    row_count = tokens.shape[0]
    split_shape = (documents.shape[0], documents.shape[1], local_width // HD, HD)
    params = full_vec.astype(jnp.float32)
    query_bias = lax.dynamic_slice_in_dim(params[2], tensor_rank * local_width, local_width)
    value_bias = lax.dynamic_slice_in_dim(params[3], tensor_rank * local_width, local_width)
    fc_bias = lax.dynamic_slice_in_dim(
        params[8:].reshape(FF), tensor_rank * hidden_width, hidden_width
    )
    qkv_matrix = full_qkv.reshape(D, 3 * local_width)
    inputs = tokens.astype(jnp.float32)
    grad_output = cotangent.astype(jnp.float32)
    normed, unit_one, inverse_one = normalize(inputs, params[0], params[1])
    normed_low = normed.astype(jnp.bfloat16)
    joined_rows = jnp.dot(normed_low, qkv_matrix, preferred_element_type=jnp.float32)
    queries = (joined_rows[:, :local_width] + query_bias).astype(jnp.bfloat16).reshape(split_shape)
    key_rows = (
        joined_rows[:, local_width : 2 * local_width].astype(jnp.bfloat16).reshape(split_shape)
    )
    value_rows = (
        (joined_rows[:, 2 * local_width :] + value_bias).astype(jnp.bfloat16).reshape(split_shape)
    )
    context, log_sums = lax.map(attend_forward, (queries, key_rows, value_rows, documents))
    context_low = context.reshape(row_count, local_width).astype(jnp.bfloat16)
    attn_partial = jnp.dot(context_low, full_out, preferred_element_type=jnp.float32)
    middle = (
        inputs
        + lax.psum(attn_partial.astype(jnp.bfloat16), "tensor").astype(jnp.float32)
        + params[4]
    )
    normed_two, unit_two, inverse_two = normalize(middle, params[5], params[6])
    normed_two_low = normed_two.astype(jnp.bfloat16)
    pre_act = jnp.dot(normed_two_low, full_fc, preferred_element_type=jnp.float32) + fc_bias
    activated, gelu_pull = jax.vjp(gelu_tanh, pre_act)
    activated_low = activated.astype(jnp.bfloat16)
    mlp_partial = jnp.dot(activated_low, full_proj, preferred_element_type=jnp.float32)
    output = (
        middle
        + lax.psum(mlp_partial.astype(jnp.bfloat16), "tensor").astype(jnp.float32)
        + params[7]
    ).astype(jnp.bfloat16)
    grad_proj = jnp.dot(activated_low.T, cotangent, preferred_element_type=jnp.float32)
    grad_act = jnp.dot(cotangent, full_proj.T, preferred_element_type=jnp.float32).astype(
        jnp.bfloat16
    )
    grad_pre = gelu_pull(grad_act.astype(jnp.float32))[0].astype(jnp.bfloat16)
    grad_fc = jnp.dot(normed_two_low.T, grad_pre, preferred_element_type=jnp.float32)
    back_two_partial = jnp.dot(grad_pre, full_fc.T, preferred_element_type=jnp.float32)
    grad_normed_two = lax.psum(back_two_partial.astype(jnp.bfloat16), "tensor").astype(jnp.float32)
    grad_middle = grad_output + normalize_back(grad_normed_two, unit_two, inverse_two, params[5])
    grad_attn = grad_middle.astype(jnp.bfloat16)
    grad_wout = jnp.dot(context_low.T, grad_attn, preferred_element_type=jnp.float32)
    grad_context = jnp.dot(grad_attn, full_out.T, preferred_element_type=jnp.float32).astype(
        jnp.bfloat16
    )
    grad_q, grad_k, grad_v = lax.map(
        attend_backward,
        (queries, key_rows, value_rows, grad_context.reshape(split_shape), documents, log_sums),
    )
    grad_q = grad_q.reshape(row_count, local_width)
    grad_v = grad_v.reshape(row_count, local_width)
    grad_joined = jnp.concatenate([grad_q, grad_k.reshape(row_count, local_width), grad_v], 1)
    grad_wqkv = jnp.dot(normed_low.T, grad_joined, preferred_element_type=jnp.float32).reshape(
        D, 3, local_width
    )
    back_one_partial = jnp.dot(grad_joined, qkv_matrix.T, preferred_element_type=jnp.float32)
    grad_normed = lax.psum(back_one_partial.astype(jnp.bfloat16), "tensor").astype(jnp.float32)
    input_grad = (
        grad_middle + normalize_back(grad_normed, unit_one, inverse_one, params[0])
    ).astype(jnp.bfloat16)

    def place_slice(share, total):
        return lax.dynamic_update_slice_in_dim(
            jnp.zeros((total,), jnp.float32), share, tensor_rank * share.shape[0], 0
        )

    first_rows = jnp.stack(
        [
            head_only * jnp.sum(grad_normed * unit_one, 0),
            head_only * jnp.sum(grad_normed, 0),
            place_slice(jnp.sum(grad_q.astype(jnp.float32), 0), D),
            place_slice(jnp.sum(grad_v.astype(jnp.float32), 0), D),
            head_only * jnp.sum(grad_middle, 0),
            head_only * jnp.sum(grad_normed_two * unit_two, 0),
            head_only * jnp.sum(grad_normed_two, 0),
            head_only * jnp.sum(grad_output, 0),
        ]
    )
    vector_grad = jnp.concatenate(
        [first_rows, place_slice(jnp.sum(grad_pre.astype(jnp.float32), 0), FF).reshape(FF // D, D)],
        0,
    )
    reduced_qkv, reduced_out, reduced_fc, reduced_proj, reduced_vec = (
        lax.psum_scatter(
            grad_wqkv.astype(jnp.bfloat16), "dp", scatter_dimension=0, tiled=True
        ).astype(jnp.float32),
        lax.psum_scatter(
            grad_wout.astype(jnp.bfloat16), "dp", scatter_dimension=1, tiled=True
        ).astype(jnp.float32),
        lax.psum_scatter(
            grad_fc.astype(jnp.bfloat16), "dp", scatter_dimension=0, tiled=True
        ).astype(jnp.float32),
        lax.psum_scatter(
            grad_proj.astype(jnp.bfloat16), "dp", scatter_dimension=1, tiled=True
        ).astype(jnp.float32),
        lax.psum_scatter(
            vector_grad.astype(jnp.bfloat16), "dp", scatter_dimension=1, tiled=True
        ).astype(jnp.float32),
    )
    matrix_squares = (
        jnp.sum(reduced_qkv * reduced_qkv)
        + jnp.sum(reduced_out * reduced_out)
        + jnp.sum(reduced_fc * reduced_fc)
        + jnp.sum(reduced_proj * reduced_proj)
    )
    reduced_vec = lax.psum(reduced_vec, "tensor")
    squares = lax.psum(
        matrix_squares + head_only * jnp.sum(reduced_vec * reduced_vec), ("dp", "tensor")
    )
    global_norm = jnp.sqrt(squares)
    clip_factor = max_norm / jnp.maximum(global_norm, max_norm)
    new_qkv, mean_qkv, square_qkv = adam_step(
        w_qkv, reduced_qkv * clip_factor, first_qkv, second_qkv, rate_qkv, decay_rate
    )
    new_out, mean_out, square_out = adam_step(
        w_out, reduced_out * clip_factor, first_out, second_out, rate_out, decay_rate
    )
    new_fc, mean_fc, square_fc = adam_step(
        w_fc, reduced_fc * clip_factor, first_fc, second_fc, rate_fc, decay_rate
    )
    new_proj, mean_proj, square_proj = adam_step(
        w_proj, reduced_proj * clip_factor, first_proj, second_proj, rate_proj, decay_rate
    )
    new_vec, mean_vec, square_vec = adam_step(
        vectors, reduced_vec * clip_factor, first_vec, second_vec, rate_vec, 0.0
    )
    own = tokens.shape[0] // 4
    n_dp = lax.axis_size("dp")
    rows = D // n_dp
    if rows % 16 == 0:
        blk = pack_blocks(w_qkv, w_out, w_fc, w_proj)
        vecb = jnp.pad(vectors.astype(jnp.bfloat16), ((0, 4), (0, LANES - rows)))
        gcol, grow = doc_inputs(documents, own)
        output = lax.all_gather(forward(n_dp, blk, vecb, tokens, gcol, grow, own)[-1], "tensor", axis=0, tiled=True)
    return (
        output,
        input_grad,
        global_norm,
        new_qkv,
        new_out,
        new_fc,
        new_proj,
        new_vec,
        mean_qkv,
        mean_out,
        mean_fc,
        mean_proj,
        mean_vec,
        square_qkv,
        square_out,
        square_fc,
        square_proj,
        square_vec,
    )


def solution(mesh):
    in_specs = (
        P("dp", None),
        P("dp", None),
        P("dp", None),
        P("dp", None, "tensor"),
        P("tensor", "dp"),
        P("dp", "tensor"),
        P("tensor", "dp"),
        P(None, "dp"),
        P("dp", None, "tensor"),
        P("tensor", "dp"),
        P("dp", "tensor"),
        P("tensor", "dp"),
        P(None, "dp"),
        P("dp", None, "tensor"),
        P("tensor", "dp"),
        P("dp", "tensor"),
        P("tensor", "dp"),
        P(None, "dp"),
    )
    out_specs = (
        P("dp", None),
        P("dp", None),
        P(),
        P("dp", None, "tensor"),
        P("tensor", "dp"),
        P("dp", "tensor"),
        P("tensor", "dp"),
        P(None, "dp"),
        P("dp", None, "tensor"),
        P("tensor", "dp"),
        P("dp", "tensor"),
        P("tensor", "dp"),
        P(None, "dp"),
        P("dp", None, "tensor"),
        P("tensor", "dp"),
        P("dp", "tensor"),
        P("tensor", "dp"),
        P(None, "dp"),
    )
    return jax.shard_map(body, mesh=mesh, in_specs=in_specs, out_specs=out_specs, check_vma=False)
```

```python
import functools
import math

import jax
import jax.numpy as jnp
from jax import lax
from jax.experimental import pallas as pl
from jax.experimental.pallas import tpu as pltpu
from jax.sharding import PartitionSpec as P

D = 768
HD = 64
FF = 3072
STEP = 10
PREV = 512
BLK = 256
LANES = 128

beta_one = 0.9
beta_two = 0.999
rate_qkv = 0.03
rate_out = 0.08
rate_fc = 0.03
rate_proj = 0.02
rate_vec = 0.6
decay_rate = 0.01
epsilon = 1e-08
max_norm = 1.0

BF = jnp.bfloat16
F32 = jnp.float32
VMEM_LIMIT = 62 * 2**20
ANY = pl.BlockSpec(memory_space=pl.ANY)
VM = pl.BlockSpec(memory_space=pltpu.VMEM)
GELU_C = math.sqrt(2.0 / math.pi)


def nn(a, b):
    return lax.dot_general(a, b, (((1,), (0,)), ((), ())), preferred_element_type=F32)


def nt(a, b):
    return lax.dot_general(a, b, (((1,), (1,)), ((), ())), preferred_element_type=F32)


MESH = pl.DeviceIdType.MESH


def wait_bytes(ref, sem):
    pltpu.make_async_copy(ref, ref, sem).wait()


def positions():
    d, t = lax.axis_index("dp"), lax.axis_index("tensor")
    return d, t, lax.rem(d, 2), d // 2, t // 2, lax.rem(t, 2)


class Gather:
    Z, X0, Y1, Y0, X1, X1U, C, CU = range(8)

    def __init__(self, n_dp, blk, vecb, w, vecg, send, recv, loc, vsend, vrecv):
        self.n_dp, self.blk, self.vecb, self.w, self.vecg = n_dp, blk, vecb, w, vecg
        self.send, self.recv, self.loc, self.vsend, self.vrecv = send, recv, loc, vsend, vrecv
        self.rows = blk.shape[1]
        self.nz = n_dp // 2
        self.d, self.t, self.x, self.z, self.y, self.c = positions()
        self.to_x = (self.d + 1 - 2 * self.x, self.t)
        self.to_y = (self.d, self.t + 2 - 4 * self.y)
        self.to_c = (self.d, self.t + 1 - 2 * self.c)
        self.u = self.t + 2 - 4 * self.y
        self.half = D // 2

    def dp_peers(self):
        return [(lax.rem(self.d + k, self.n_dp), self.t) for k in range(1, self.n_dp)]

    def at(self, m, t, block, lanes):
        return self.w.at[m, t, pl.ds(pl.multiple_of(block * self.rows, self.rows), self.rows), lanes]

    def copy(self, m, stage, src, dst, dev):
        pltpu.make_async_remote_copy(
            src_ref=src, dst_ref=dst, send_sem=self.send.at[m, stage], recv_sem=self.recv.at[m, stage],
            device_id=dev, device_id_type=MESH,
        ).start()

    def size(self, m, stage):
        rows = (self.nz - 1) * self.rows if stage == self.Z else self.nz * self.rows
        if stage in (self.Y0, self.C, self.CU):
            rows = D
        lanes = self.half if stage in (self.X0, self.Y1, self.Y0, self.X1, self.X1U) else D
        return self.w.at[m, 0, pl.ds(0, rows), pl.ds(0, lanes)]

    def got(self, m, stage):
        wait_bytes(self.size(m, stage), self.recv.at[m, stage])

    def begin(self):
        barrier = pltpu.get_barrier_semaphore()
        peers = self.dp_peers() + [self.to_y, self.to_c]
        for dev in peers:
            pl.semaphore_signal(barrier, inc=1, device_id=dev, device_id_type=MESH)
        for m in range(3):
            pltpu.make_async_copy(self.blk.at[m], self.at(m, self.t, self.d, pl.ds(0, D)), self.loc.at[m]).start()
        pl.semaphore_wait(barrier, len(peers))
        for dev in self.dp_peers():
            pltpu.make_async_remote_copy(
                src_ref=self.vecb, dst_ref=self.vecg.at[self.d], send_sem=self.vsend, recv_sem=self.vrecv,
                device_id=dev, device_id_type=MESH,
            ).start()
        self.vecg[self.d] = self.vecb[...]
        self.along_z(0)

    def vectors(self):
        wait_bytes(self.vecg.at[pl.ds(0, self.n_dp - 1)], self.vrecv)
        width = D // self.n_dp
        lane = lax.broadcasted_iota(jnp.int32, (LANES, D), 0)
        col = lax.broadcasted_iota(jnp.int32, (LANES, D), 1)
        total = jnp.zeros((16, D), F32)
        for p in range(self.n_dp):
            pick = jnp.where((col == lane + p * width) & (lane < width), 1.0, 0.0).astype(BF)
            total += nn(self.vecg[p], pick)
        return total

    def along_z(self, m):
        for k in range(1, self.nz):
            dev = (lax.rem(self.d + 2 * k, self.n_dp), self.t)
            self.copy(m, self.Z, self.blk.at[m], self.at(m, self.t, self.d, pl.ds(0, D)), dev)

    def columns(self, m, stage, t, lanes, dev):
        for zz in range(self.nz):
            ref = self.at(m, t, 2 * zz + self.x, lanes)
            self.copy(m, stage, ref, ref, dev)

    def after_z(self, m):
        self.got(m, self.Z)
        pltpu.make_async_copy(self.blk.at[m], self.blk.at[m], self.loc.at[m]).wait()
        low, high = pl.ds(0, self.half), pl.ds(self.half, self.half)
        self.columns(m, self.Y1, self.t, high, self.to_y)
        self.columns(m, self.X0, self.t, low, self.to_x)
        self.columns(m, self.X1, self.t, high, self.to_x)

    def after_y1(self, m):
        self.got(m, self.Y1)
        self.columns(m, self.X1U, self.u, pl.ds(self.half, self.half), self.to_x)

    def after_x0(self, m):
        self.got(m, self.X0)
        ref = self.w.at[m, self.t, :, pl.ds(0, self.half)]
        self.copy(m, self.Y0, ref, ref, self.to_y)

    def after_x1(self, m):
        self.got(m, self.X1)
        ref = self.w.at[m, self.t]
        self.copy(m, self.C, ref, ref, self.to_c)

    def after_last(self, m):
        self.got(m, self.Y0)
        self.got(m, self.X1U)
        ref = self.w.at[m, self.u]
        self.copy(m, self.CU, ref, ref, self.to_c)

    def complete(self, m):
        self.got(m, self.C)
        self.got(m, self.CU)

    def finish(self):
        for m in range(3):
            for stage in range(8):
                wait_bytes(self.size(m, stage), self.send.at[m, stage])
        wait_bytes(self.vecg.at[pl.ds(0, self.n_dp - 1)], self.vsend)


def ln_parts(x):
    mean = jnp.mean(x, -1, keepdims=True)
    centred = x - mean
    inv = lax.rsqrt(jnp.mean(centred * centred, -1, keepdims=True) + 1e-05)
    return centred * inv, inv


def ln_back(e, u, inv):
    return inv * (
        e - jnp.mean(e, -1, keepdims=True) - u * jnp.mean(e * u, -1, keepdims=True)
    )


def group_tiles(rows, group):
    base = (group // 2) * 384
    low = lax.broadcasted_iota(jnp.int32, (rows.shape[0], LANES), 1) < HD
    first = rows[:, base : base + 128]
    second = rows[:, base + 128 : base + 256]
    third = rows[:, base + 256 : base + 384]
    if group % 2 == 0:
        return first, second
    second, third = pltpu.roll(second, HD, 1), pltpu.roll(third, HD, 1)
    return jnp.where(low, second, third), third


def ungroup_tiles(even, odd):
    low = lax.broadcasted_iota(jnp.int32, even[0].shape, 1) < HD
    pair = pltpu.roll(odd[0], HD, 1)
    single = pltpu.roll(odd[1], HD, 1)
    return even[0], jnp.where(low, even[1], pair), jnp.where(low, pair, single)


def fwd_kernel(
    n_dp, w_in, vec_in, tok_hbm, gcol, grow,
    w_hbm, vec_out, nrm_out, q_out, v_out, kT_out, ctx_out, mid_out, n2_out, act_out, slope_out, probs_out, out_out,
    xw, nrm, wa, wf, wp, qm, kt, vt, ktT, vtT, ctxT, ctx, mb, mid, n2, acc, act, slope, pst, vec_ref,
    in_sem, w_sem, out_sem, p_sem, *gather_refs,
):
    gather = Gather(n_dp, w_in, vec_in, w_hbm, *gather_refs) if n_dp else None
    if gather:
        gather.begin()
    else:
        w_hbm = w_in
    rank = lax.axis_index("tensor")
    own = xw.shape[0] - PREV
    start = jnp.maximum(rank * own - PREV, 0)
    cp_prev = pltpu.make_async_copy(tok_hbm.at[pl.ds(pl.multiple_of(start, 256), PREV)], xw.at[pl.ds(0, PREV)], in_sem.at[0])
    cp_own = pltpu.make_async_copy(tok_hbm.at[pl.ds(pl.multiple_of(rank * own, 256), own)], xw.at[pl.ds(PREV, own)], in_sem.at[1])
    cp_prev.start()
    cp_own.start()
    outs = []

    def load(m, dst):
        if gather:
            gather.complete(m)
        cps = [pltpu.make_async_copy(w_hbm.at[m, t], dst.at[t], w_sem.at[m, t]) for t in range(4)]
        for cp in cps:
            cp.start()
        return cps

    def put(src, dst):
        cp = pltpu.make_async_copy(src, dst, out_sem.at[len(outs)])
        cp.start()
        outs.append(cp)

    for i in range(3):
        keys = gcol[pl.ds(i * BLK, 3 * BLK), :]
        same = keys == grow[0:1, pl.ds(i * BLK, BLK)]
        row = lax.broadcasted_iota(jnp.int32, (3 * BLK, BLK), 0)
        col = lax.broadcasted_iota(jnp.int32, (3 * BLK, BLK), 1)
        mb[i] = jnp.where(same & (row <= col + PREV), 0.0, -1e30).astype(F32)
    cp_prev.wait()
    cp_own.wait()
    vec = gather.vectors() if gather else vec_in[...]
    vec_ref[...] = vec
    put(vec_ref, vec_out)

    def ln_one(r, _):
        rows = pl.ds(pl.multiple_of(r * 128, 128), 128)
        u, _inv = ln_parts(xw[rows, :].astype(F32))
        nrm[rows, :] = (u * vec[0:1] + vec[1:2]).astype(BF)
        return 0

    lax.fori_loop(0, xw.shape[0] // 128, ln_one, 0)
    put(nrm, nrm_out)
    if gather:
        gather.after_z(0)
        gather.along_z(1)
        gather.after_y1(0)
        gather.after_x0(0)
        gather.after_z(1)
        gather.along_z(2)
        gather.after_x1(0)
        gather.after_last(0)
        gather.after_y1(1)
        gather.after_x0(1)
    loads = load(0, wa)
    low = lax.broadcasted_iota(jnp.int32, (BLK, LANES), 1) < HD
    for g in range(4):
        loads[g].wait()
        pair, single = group_tiles(vec[0:8], g)
        bq_pair, bq_single, bv_pair, bv_single = pair[2:3], single[2:3], pair[3:4], single[3:4]

        def qkv(rc, _):
            rows = pl.ds(pl.multiple_of(rc * BLK, BLK), BLK)
            x = nrm[rows, :]
            one = nn(x, wa[g, :, 0:384])
            two = nn(x, wa[g, :, 512:768])
            k_pair = one[:, 128:256].astype(BF)
            v_pair = (one[:, 256:384] + bv_pair).astype(BF)
            kt[2 * g, rows, :] = k_pair
            vt[2 * g, rows, :] = v_pair
            ktT[2 * g, :, rows] = k_pair.T
            vtT[2 * g, :, rows] = v_pair.T
            qk, vo = two[:, 0:128], two[:, 128:256]
            k_single = jnp.where(low, pltpu.roll(qk, HD, 1), 0.0).astype(BF)
            v_single = jnp.where(low, vo + bv_single, 0.0)
            kt[2 * g + 1, rows, :] = k_single
            vt[2 * g + 1, rows, :] = pltpu.roll(v_single, HD, 1).astype(BF)
            ktT[2 * g + 1, :, rows] = k_single.T
            vtT[2 * g + 1, :, rows] = v_single.astype(BF).T

            @pl.when(rc >= PREV // BLK)
            def _():
                orows = pl.ds(pl.multiple_of(rc * BLK - PREV, BLK), BLK)
                q_pair = (one[:, 0:128] + bq_pair).astype(BF).astype(F32) * 0.125
                q_single = (qk + bq_single).astype(BF).astype(F32) * 0.125
                qm[3 * g, orows, :] = jnp.where(low, q_pair, 0.0).astype(BF)
                qm[3 * g + 1, orows, :] = jnp.where(low, 0.0, q_pair).astype(BF)
                qm[3 * g + 2, orows, :] = jnp.where(low, q_single, 0.0).astype(BF)

            return 0

        lax.fori_loop(0, nrm.shape[0] // BLK, qkv, 0)
    put(qm, q_out)
    put(vt, v_out)
    put(ktT, kT_out)

    def attend(h, _):
        g, hh = h // 3, lax.rem(h, 3)
        tile = 2 * g + hh // 2
        src_half = pl.multiple_of(jnp.where(hh == 1, HD, 0), HD)
        dst_half = pl.multiple_of(jnp.where(hh == 0, 0, HD), HD)
        slot = lax.rem(h, 2)

        @pl.when(h >= 2)
        def _():
            pltpu.make_async_copy(pst.at[slot], probs_out.at[h - 2], p_sem.at[slot]).wait()

        for i in range(3):
            keys = pl.ds(i * BLK, 3 * BLK)
            mine = pl.ds(i * BLK, BLK)
            s = nt(kt[tile, keys, :], qm[h, mine, :]) + mb[i]
            p = jnp.exp(s - jnp.max(s, 0, keepdims=True))
            pb = (p * (1.0 / jnp.sum(p, 0, keepdims=True))).astype(BF)
            pst[slot, i] = pb
            o = nn(vtT[tile, pl.ds(src_half, HD), keys], pb)
            ctxT[tile, pl.ds(dst_half, HD), mine] = o.astype(BF)
        pltpu.make_async_copy(pst.at[slot], probs_out.at[h], p_sem.at[slot]).start()
        return 0

    if gather:
        gather.after_z(2)
        gather.after_x1(1)
        gather.after_last(1)
        gather.after_y1(2)
        gather.after_x0(2)
    for g in range(4):
        ctxT[2 * g + 1, 0:HD, :] = jnp.zeros((HD, own), BF)
    lax.fori_loop(0, 12, attend, 0)
    for t in range(8):
        ctx[t] = ctxT[t].T
    put(ctx, ctx_out)

    def out_proj(rc, _):
        rows = pl.ds(pl.multiple_of(rc * BLK, BLK), BLK)
        total = xw[pl.ds(pl.multiple_of(rc * BLK + PREV, BLK), BLK), :].astype(F32) + vec[4:5]
        for g in range(4):
            total += nt(ctx[2 * g, rows, :], wa[g, :, 384:512])
            total += nt(ctx[2 * g + 1, rows, :], wa[g, :, 640:768])
        mid[rows, :] = total
        u, _inv = ln_parts(total)
        n2[rows, :] = (u * vec[5:6] + vec[6:7]).astype(BF)
        acc[rows, :] = total + vec[7:8]
        return 0

    lax.fori_loop(0, own // BLK, out_proj, 0)
    put(mid, mid_out)
    put(n2, n2_out)
    loads = load(1, wf)
    if gather:
        gather.after_x1(2)
        gather.after_last(2)
    loads += load(2, wp)
    for t in range(4):
        loads[t].wait()
        loads[4 + t].wait()
        bias = vec[8 + t : 9 + t]

        def mlp(rc, _):
            rows = pl.ds(pl.multiple_of(rc * BLK, BLK), BLK)
            z = nn(n2[rows, :], wf[t]) + bias
            th = jnp.tanh(GELU_C * (z + 0.044715 * z * z * z))
            half = 0.5 * (1.0 + th)
            low_act = (z * half).astype(BF)
            act[t, rows, :] = low_act
            slope[t, rows, :] = (
                half + 0.5 * z * (1.0 - th * th) * (GELU_C * (1.0 + 3 * 0.044715 * z * z))
            ).astype(BF)
            acc[rows, :] += nt(low_act, wp[t])
            return 0

        lax.fori_loop(0, own // BLK, mlp, 0)
        put(act.at[t], act_out.at[t])
        put(slope.at[t], slope_out.at[t])
    xw[0:own, :] = acc[...].astype(BF)
    put(xw.at[pl.ds(0, own)], out_out)
    for slot in range(2):
        pltpu.make_async_copy(pst.at[slot], probs_out.at[0], p_sem.at[slot]).wait()
    for cp in outs:
        cp.wait()
    if gather:
        gather.finish()


def forward(n_dp, w_in, vec, tokens, gcol, grow, own):
    win = own + PREV
    sds = jax.ShapeDtypeStruct
    out_shape = [
        sds((3, 4, D, D) if n_dp else (8, LANES), BF),
        sds((16, D), F32), sds((win, D), BF), sds((12, own, LANES), BF), sds((8, win, LANES), BF),
        sds((8, LANES, win), BF), sds((8, own, LANES), BF), sds((own, D), F32), sds((own, D), BF),
        sds((4, own, D), BF), sds((4, own, D), BF), sds((12, 3, 3 * BLK, BLK), BF), sds((own, D), BF),
    ]
    scratch = [
        pltpu.VMEM((win, D), BF), pltpu.VMEM((win, D), BF),
        pltpu.VMEM((4, D, D), BF), pltpu.VMEM((4, D, D), BF), pltpu.VMEM((4, D, D), BF),
        pltpu.VMEM((12, own, LANES), BF), pltpu.VMEM((8, win, LANES), BF), pltpu.VMEM((8, win, LANES), BF),
        pltpu.VMEM((8, LANES, win), BF), pltpu.VMEM((8, LANES, win), BF),
        pltpu.VMEM((8, LANES, own), BF), pltpu.VMEM((8, own, LANES), BF),
        pltpu.VMEM((3, 3 * BLK, BLK), F32), pltpu.VMEM((own, D), F32), pltpu.VMEM((own, D), BF),
        pltpu.VMEM((own, D), F32), pltpu.VMEM((4, own, D), BF), pltpu.VMEM((4, own, D), BF),
        pltpu.VMEM((2, 3, 3 * BLK, BLK), BF), pltpu.VMEM((16, D), F32),
        pltpu.SemaphoreType.DMA((2,)), pltpu.SemaphoreType.DMA((3, 4)), pltpu.SemaphoreType.DMA((24,)),
        pltpu.SemaphoreType.DMA((2,)),
    ]
    params = {}
    if n_dp:
        scratch += [
            pltpu.VMEM((n_dp, 16, LANES), BF), pltpu.SemaphoreType.DMA((3, 8)), pltpu.SemaphoreType.DMA((3, 8)),
            pltpu.SemaphoreType.DMA((3,)), pltpu.SemaphoreType.DMA, pltpu.SemaphoreType.DMA,
        ]
        params = dict(collective_id=1, has_side_effects=True)
    return pl.pallas_call(
        functools.partial(fwd_kernel, n_dp),
        out_shape=out_shape,
        in_specs=[ANY, VM, ANY, VM, VM],
        out_specs=[ANY] * len(out_shape),
        scratch_shapes=scratch,
        compiler_params=pltpu.CompilerParams(vmem_limit_bytes=VMEM_LIMIT, **params),
        name="forward",
    )(w_in, vec, tokens, gcol, grow)


def pack_blocks(w_qkv, w_out, w_fc, w_proj):
    q, k, v, o = w_qkv[:, 0], w_qkv[:, 1], w_qkv[:, 2], w_out.T
    pairs = [a[:, :128] for a in (q, k, v, o)]
    singles = [a[:, 128:] for a in (q, k, v, o)]
    return jnp.stack([jnp.concatenate(pairs + singles, 1), w_fc, w_proj.T]).astype(BF)


def doc_inputs(documents, own):
    rank = lax.axis_index("tensor")
    rows = documents.shape[0]
    gid = (documents + 8 * jnp.arange(rows, dtype=jnp.int32)[:, None]).reshape(-1)
    padded = jnp.concatenate([jnp.full((PREV,), -1, jnp.int32), gid])
    win = lax.dynamic_slice_in_dim(padded, rank * own, own + PREV)
    mine = lax.dynamic_slice_in_dim(gid, rank * own, own)
    return win[:, None], jnp.broadcast_to(mine[None], (8, own))


class Reduce:
    def __init__(self, n_dp, sb, rc, su, rx, rz, ry, ys, fin, sems):
        self.n_dp, self.nz, self.rows = n_dp, n_dp // 2, D // n_dp
        self.sb, self.rc, self.su, self.rx, self.rz, self.ry, self.ys, self.fin = sb, rc, su, rx, rz, ry, ys, fin
        self.cs, self.cr, self.xs, self.xr, self.zs, self.zr, self.ysem, self.yr = sems
        self.d, self.t, self.x, self.z, self.y, self.c = positions()
        self.to_x = (self.d + 1 - 2 * self.x, self.t)
        self.to_y = (self.d, self.t + 2 - 4 * self.y)
        self.to_c = (self.d, self.t + 1 - 2 * self.c)

    def block(self, ref, index):
        return ref.at[pl.ds(pl.multiple_of(index * self.rows, self.rows), self.rows)]

    def send(self, src, dst, ssem, rsem, dev):
        pltpu.make_async_remote_copy(
            src_ref=src, dst_ref=dst, send_sem=ssem, recv_sem=rsem, device_id=dev, device_id_type=MESH
        ).start()

    def to_core(self, u):
        self.send(self.sb.at[u % 2], self.rc.at[u], self.cs.at[u], self.cr.at[u], self.to_c)

    def core_sent(self, u):
        wait_bytes(self.sb.at[u % 2], self.cs.at[u])

    def core_got(self, u):
        wait_bytes(self.rc.at[u], self.cr.at[u])

    def slot(self, u):
        return u % 4

    def along_x(self, u):
        for zz in range(self.nz):
            src = self.block(self.su.at[self.slot(u)], 2 * zz + 1 - self.x)
            self.send(src, self.rx.at[u, pl.ds(zz * self.rows, self.rows)], self.xs.at[u], self.xr.at[u], self.to_x)

    def after_x(self, u):
        wait_bytes(self.rx.at[u], self.xr.at[u])
        tile = self.su.at[self.slot(u)]
        for zz in range(self.nz):
            mine = self.block(tile, 2 * zz + self.x)
            got = self.rx[u, pl.ds(zz * self.rows, self.rows), :]
            mine[...] = (mine[...].astype(F32) + got.astype(F32)).astype(BF)
        for k in range(1, self.nz):
            zz = lax.rem(self.z + k, self.nz)
            src = self.block(tile, 2 * zz + self.x)
            dev = (2 * zz + self.x, self.t)
            self.send(src, self.rz.at[u, k - 1], self.zs.at[u], self.zr.at[u], dev)

    def after_z(self, u, m, yy):
        wait_bytes(self.rz.at[u], self.zr.at[u])
        total = self.block(self.su.at[self.slot(u)], 2 * self.z + self.x)[...].astype(F32)
        for k in range(self.nz - 1):
            total += self.rz[u, k].astype(F32)

        @pl.when(self.y == yy)
        def _():
            self.fin[m] = total

        @pl.when(self.y != yy)
        def _():
            self.ys[m] = total.astype(BF)
            self.send(self.ys.at[m], self.ry.at[m], self.ysem.at[m], self.yr.at[m], self.to_y)

    def sent(self, u):
        wait_bytes(self.rx.at[u], self.xs.at[u])
        wait_bytes(self.rz.at[u], self.zs.at[u])

    def finish(self, m):
        wait_bytes(self.ry.at[m], self.yr.at[m])
        self.fin[m] += self.ry[m].astype(F32)
        wait_bytes(self.ys.at[m], self.ysem.at[m])


def bwd_kernel(
    n_dp, w_hbm, vec_hbm, tok_hbm, cot_hbm, nrm_hbm, q_hbm, v_hbm, kT_hbm, ctx_hbm, mid_hbm, n2_hbm,
    act_hbm, slope_hbm, probs_hbm, own_out_hbm,
    *rest,
):
    if n_dp:
        fin_out, vgrad_out, ss_out, igr_out, prev_out, all_out = rest[:6]
        rest = rest[6:]
    else:
        tiles_out, vgrad_out, igr_out, prev_out = rest[:4]
        rest = rest[4:]
    (cot, cotT, n2T, gp, gm, w4, pool, gn1, vs, kTs, qs, ctxs, pbuf, gctx, dk, dv, dqT, gj, vec_ref, vg, cs_ref,
     sb, in_sem, tile_sem, ct_sem, p_sem, out_sem) = rest[:27]
    rest = rest[27:]
    d, t, x, z, y, c = positions()
    own = cot.shape[0]
    own_rows = pl.ds(pl.multiple_of(t * own, 256), own)
    red = None
    if n_dp:
        (rc, su, rx, rz, ry, ys, fin, comb, vgx, ssx, *sems) = rest
        red = Reduce(n_dp, sb, rc, su, rx, rz, ry, ys, fin, sems[:8])
        o_send, o_recv, v_send, v_recv, s_send, s_recv = sems[8:]
        to_c, to_y = red.to_c, red.to_y
        diag = (d, t + 2 - 4 * y + 1 - 2 * c)
        dp_peers = [(lax.rem(d + k, n_dp), t) for k in range(1, n_dp)]
        barrier = pltpu.get_barrier_semaphore()
        peers = dp_peers + [to_y, to_c, diag]
        for dev in peers:
            pl.semaphore_signal(barrier, inc=1, device_id=dev, device_id_type=MESH)

    def fetch(src, dst, sem):
        cp = pltpu.make_async_copy(src, dst, sem)
        cp.start()
        return cp

    order = [1 - c, c, 3 - c, 2 + c]

    def fetch_tile(j):
        s = j % 2
        return [
            fetch(w_hbm.at[2, order[j]], w4.at[s], tile_sem.at[j, 0]),
            fetch(act_hbm.at[order[j]], pool.at[s], tile_sem.at[j, 1]),
            fetch(slope_hbm.at[order[j]], pool.at[2 + s], tile_sem.at[j, 2]),
            fetch(w_hbm.at[1, order[j]], w4.at[2 + s], tile_sem.at[j, 3]),
        ]

    cp_cot = fetch(cot_hbm.at[own_rows], cot, in_sem.at[0])
    tiles = {0: fetch_tile(0)}
    cp_n2 = fetch(n2_hbm, gp, in_sem.at[1])
    cp_vec = fetch(vec_hbm, vec_ref, in_sem.at[2])
    tiles[1] = fetch_tile(1)
    cp_mid = fetch(mid_hbm, gn1.at[pl.ds(0, own)], in_sem.at[3])
    local_out = []
    if n_dp:
        local_out.append(fetch(own_out_hbm, all_out.at[t], out_sem.at[0]))
        pl.semaphore_wait(barrier, len(peers))
        red.send(own_out_hbm, all_out.at[t], o_send.at[0], o_recv.at[0], to_y)
        red.send(own_out_hbm, all_out.at[t], o_send.at[1], o_recv.at[1], to_c)
    vg[...] = jnp.zeros_like(vg)
    ones = jnp.ones((16, own), BF)
    cp_cot.wait()
    cotT[...] = cot[...].T
    cp_n2.wait()
    n2T[...] = gp[...].T

    def emit(u, keep, rows, lanes, value):
        if not n_dp or not keep:
            sb[u % 2, rows, lanes] = value.astype(BF)
        else:
            su[red.slot(u), rows, lanes] = (value + rc[u, rows, lanes].astype(F32)).astype(BF)

    def chunk(r, size=BLK):
        return pl.ds(pl.multiple_of(r * size, size), size)

    pending = set()

    def before(u, keep):
        if n_dp:
            if keep:
                red.core_got(u)
                if u >= 4:
                    red.sent(u - 4)
            elif u >= 2:
                red.core_sent(u - 2)
        elif u % 2 in pending:
            wait_bytes(sb.at[u % 2], tile_sem.at[4, u % 2])

    def after(u, keep, m, which):
        if n_dp:
            if keep:
                red.along_x(u)
            else:
                red.to_core(u)
        else:
            pending.add(u % 2)
            pltpu.make_async_copy(sb.at[u % 2], tiles_out.at[m, which], tile_sem.at[4, u % 2]).start()

    for j in range(4):
        yy, keep = j // 2, j % 2 == 1
        s = j % 2
        which = order[j]
        u_p, u_f = 2 * yy, 2 * yy + 1
        for cp in tiles[j]:
            cp.wait()

        def grads(r, _):
            rows = chunk(r)
            ga = nn(cot[rows, :], w4[s]).astype(BF).astype(F32)
            g = (ga * pool[2 + s, rows, :].astype(F32)).astype(BF)
            gp[rows, :] = g
            back = nt(g, w4[2 + s])
            if j == 0:
                gm[rows, :] = back
            else:
                gm[rows, :] += back
            return 0

        lax.fori_loop(0, own // BLK, grads, 0)
        vg[pl.ds(8 + which, 1), :] = nn(ones, gp[...])[0:1]
        before(u_p, keep)

        def grad_p(r, _):
            emit(u_p, keep, chunk(r), slice(None), nn(cotT[chunk(r), :], pool[s]))
            return 0

        lax.fori_loop(0, D // BLK, grad_p, 0)
        after(u_p, keep, 2, which)
        before(u_f, keep)

        def grad_f(r, _):
            emit(u_f, keep, chunk(r), slice(None), nn(n2T[chunk(r), :], gp[...]))
            return 0

        lax.fori_loop(0, D // BLK, grad_f, 0)
        after(u_f, keep, 1, which)
        if j < 2:
            tiles[j + 2] = fetch_tile(j + 2)
    cp_vec.wait()
    cp_mid.wait()
    wa_cps = [fetch(w_hbm.at[0, k], w4.at[k], ct_sem.at[0, k]) for k in range(4)]
    cp_nrm_own = fetch(nrm_hbm.at[pl.ds(PREV, own)], pool.at[0], in_sem.at[1])
    cp_nrm_prev = fetch(nrm_hbm.at[pl.ds(0, PREV)], pool.at[1, pl.ds(0, PREV)], in_sem.at[3])

    def fetch_heads(j):
        s, g = j % 2, order[j]
        return [
            fetch(v_hbm.at[pl.ds(2 * g, 2)], vs.at[s], ct_sem.at[1 + j, 0]),
            fetch(kT_hbm.at[pl.ds(2 * g, 2)], kTs.at[s], ct_sem.at[1 + j, 1]),
            fetch(q_hbm.at[pl.ds(3 * g, 3)], qs.at[s], ct_sem.at[1 + j, 2]),
            fetch(ctx_hbm.at[pl.ds(2 * g, 2)], ctxs.at[s], ct_sem.at[1 + j, 3]),
        ]

    heads = {0: fetch_heads(0), 1: fetch_heads(1)}

    def probs_copy(g, hh, slot):
        return pltpu.make_async_copy(probs_hbm.at[3 * g + hh], pbuf.at[slot], p_sem.at[slot])

    probs_copy(order[0], 0, 0).start()

    def ln_two(r, sums):
        rows = chunk(r, 128)
        u, inv = ln_parts(gn1[rows, :])
        g = gm[rows, :]
        co = cot[rows, :].astype(F32)
        total = co + ln_back(g * vec_ref[5:6, :], u, inv)
        gm[rows, :] = total
        cot[rows, :] = total.astype(BF)
        new = [jnp.sum(v, 0, keepdims=True) for v in (total, g * u, g, co)]
        return tuple(a + b for a, b in zip(sums, new))

    zero = jnp.zeros((1, D), F32)
    sums = lax.fori_loop(0, own // 128, ln_two, (zero,) * 4)
    for k in range(4):
        vg[4 + k : 5 + k, :] = sums[k]
    gattn, gattnT = cot, cotT
    gattnT[...] = gattn[...].T
    cp_nrm_own.wait()
    cp_nrm_prev.wait()
    nrmT, nrmT_prev = pool.at[2], pool.at[3]
    nrmT[...] = pool[0].T
    nrmT_prev[:, 0:PREV] = pool[1, 0:PREV, :].T
    cp_tok_own = fetch(tok_hbm.at[own_rows], pool.at[0], in_sem.at[0])
    tok_start = pl.multiple_of(jnp.maximum(t * own - PREV, 0), 256)
    cp_tok_prev = fetch(tok_hbm.at[pl.ds(tok_start, PREV)], pool.at[1, pl.ds(0, PREV)], in_sem.at[2])
    for cp in wa_cps:
        cp.wait()
    if n_dp:
        red.after_x(0)
    win = own + PREV
    low = lax.broadcasted_iota(jnp.int32, (BLK, LANES), 1) < HD
    ones_win = jnp.ones((16, win), BF)
    for j in range(4):
        yy, keep = j // 2, j % 2 == 1
        s, g = j % 2, order[j]
        u = 4 + yy
        for cp in heads[j]:
            cp.wait()

        def grad_ctx(r, _):
            rows = chunk(r)
            pair = nn(gattn[rows, :], w4[g, :, 384:512])
            single = nn(gattn[rows, :], w4[g, :, 640:768])
            gctx[0, rows, :] = jnp.where(low, pair, 0.0).astype(BF)
            gctx[1, rows, :] = jnp.where(low, 0.0, pair).astype(BF)
            gctx[2, rows, :] = jnp.where(low, 0.0, single).astype(BF)
            return 0

        lax.fori_loop(0, own // BLK, grad_ctx, 0)
        dk[...] = jnp.zeros_like(dk)
        dv[...] = jnp.zeros_like(dv)
        dqT[1, HD:, :] = jnp.zeros((HD, own), F32)

        def head(hh, _):
            tile = hh // 2
            half = pl.multiple_of(jnp.where(hh == 1, HD, 0), HD)
            slot = lax.rem(j * 3 + hh, 2)

            @pl.when(hh < 2)
            def _():
                probs_copy(g, hh + 1, 1 - slot).start()

            if j < 3:

                @pl.when(hh == 2)
                def _():
                    probs_copy(order[j + 1], 0, 1 - slot).start()

            probs_copy(g, hh, slot).wait()
            for i in range(3):
                keys = pl.ds(i * BLK, 3 * BLK)
                mine = pl.ds(i * BLK, BLK)
                p = pbuf[slot, i]
                do = gctx[hh, mine, :]
                dp = nt(vs[s, tile, keys, :], do)
                pf = p.astype(F32)
                ds = (pf * (dp - jnp.sum(pf * dp, 0, keepdims=True))).astype(BF)
                dv[tile, keys, :] += nn(p, do)
                dk[tile, keys, :] += nn(ds, qs[s, hh, mine, :])
                dqT[tile, pl.ds(half, HD), mine] = nn(kTs[s, tile, pl.ds(half, HD), keys], ds)
            return 0

        lax.fori_loop(0, 3, head, 0)
        for r in range(win // BLK):
            rows = pl.ds(r * BLK, BLK)
            k_single = pltpu.roll(dk[1, rows, :], HD, 1)
            if r >= PREV // BLK:
                orows = pl.ds(r * BLK - PREV, BLK)
                gj[rows, 0:128] = (dqT[0, :, orows].T * 0.125).astype(BF)
                k_single += dqT[1, :, orows].T * 0.125
            else:
                gj[rows, 0:128] = jnp.zeros((BLK, LANES), BF)
            gj[rows, 128:256] = dk[0, rows, :].astype(BF)
            gj[rows, 256:384] = dv[0, rows, :].astype(BF)
            gj[rows, 384:512] = k_single.astype(BF)
            gj[rows, 512:640] = pltpu.roll(dv[1, rows, :], HD, 1).astype(BF)
        cs_ref[g] = nn(ones_win, gj[...])[0:8]
        before(u, keep)

        def grad_a(r, _):
            rows = chunk(r)
            a_own, a_prev, b = nrmT[rows, :], nrmT_prev[rows, 0:PREV], gattnT[rows, :]
            emit(u, keep, rows, slice(0, 384), nn(a_own, gj[PREV:, 0:384]) + nn(a_prev, gj[0:PREV, 0:384]))
            emit(u, keep, rows, slice(384, 512), nn(b, ctxs[s, 0]))
            last = nn(a_own, gj[PREV:, 384:640]) + nn(a_prev, gj[0:PREV, 384:640])
            emit(u, keep, rows, slice(512, 640), last[:, 0:128])
            emit(u, keep, rows, slice(640, 768), last[:, 128:256] + nn(b, ctxs[s, 1]))
            return 0

        lax.fori_loop(0, D // BLK, grad_a, 0)
        after(u, keep, 0, g)

        def grad_n1(r, _):
            rows = chunk(r)
            back = nt(gj[rows, 0:384], w4[g, :, 0:384]) + nt(gj[rows, 384:640], w4[g, :, 512:768])
            if j == 0:
                gn1[rows, :] = back
            else:
                gn1[rows, :] += back
            return 0

        lax.fori_loop(0, win // BLK, grad_n1, 0)
        if j < 2:
            heads[j + 2] = fetch_heads(j + 2)
        if n_dp:
            if j == 0:
                red.after_x(1)
                red.after_z(0, 2, 0)
                wait_bytes(all_out.at[t], o_recv.at[0])
                there = all_out.at[t + 2 - 4 * y]
                red.send(there, there, o_send.at[2], o_recv.at[2], to_c)
            if j == 1:
                red.after_x(2)
                red.after_z(1, 1, 0)
            if j == 2:
                red.after_x(3)
                red.after_z(2, 2, 1)
            if j == 3:
                red.after_x(4)
    cp_tok_own.wait()
    cp_tok_prev.wait()
    igr, prev = w4.at[0], w4.at[1]

    def ln_one(base, src, tokens, dst, add):
        def step(r, sums):
            rows = chunk(r, 128)
            g = gn1[pl.ds(pl.multiple_of(base + r * 128, 128), 128), :]
            u, inv = ln_parts(tokens[rows, :].astype(F32))
            total = ln_back(g * vec_ref[0:1, :], u, inv)
            if add:
                total += gm[rows, :]
            dst[rows, :] = total.astype(BF)
            return (sums[0] + jnp.sum(g * u, 0, keepdims=True), sums[1] + jnp.sum(g, 0, keepdims=True))

        return lax.fori_loop(0, src // 128, step, (zero, zero))

    sp = ln_one(0, PREV, pool.at[1], prev, False)
    if n_dp:

        @pl.when(c == 1)
        def _():
            red.send(prev.at[pl.ds(0, PREV)], comb, o_send.at[3], o_recv.at[3], to_c)

    so = ln_one(PREV, own, pool.at[0], igr, True)
    vg[0:1, :] = sp[0] + so[0]
    vg[1:2, :] = sp[1] + so[1]
    for g in (0, 2):
        for row, (a, b) in ((2, (0, 384)), (3, (256, 512))):
            even = (cs_ref[g, :, a : a + 128], cs_ref[g, :, b : b + 128])
            odd = (cs_ref[g + 1, :, a : a + 128], cs_ref[g + 1, :, b : b + 128])
            for k, part in enumerate(ungroup_tiles(even, odd)):
                col = (g // 2) * 384 + 128 * k
                vg[row : row + 1, col : col + 128] = part[0:1]
    if not n_dp:
        last = [fetch(igr, igr_out, out_sem.at[0]), fetch(prev.at[pl.ds(0, PREV)], prev_out, out_sem.at[1]),
                fetch(vg, vgrad_out, out_sem.at[2])]
        for cp in last:
            cp.wait()
        for k in range(2):
            wait_bytes(sb.at[k], tile_sem.at[4, k])
        return

    @pl.when(c == 0)
    def _():
        wait_bytes(comb, o_recv.at[3])
        igr[own - PREV :, :] = (igr[own - PREV :, :].astype(F32) + comb[...].astype(F32)).astype(BF)

    @pl.when(c == 1)
    def _():
        wait_bytes(comb, o_send.at[3])

    there = t + 2 - 4 * y
    local_out.append(fetch(igr, igr_out.at[t], out_sem.at[1]))
    red.send(igr, igr_out.at[t], o_send.at[4], o_recv.at[4], to_y)
    red.send(igr, igr_out.at[t], o_send.at[5], o_recv.at[5], to_c)
    prev_rows = prev.at[pl.ds(0, PREV)]

    @pl.when(t == 2)
    def _():
        red.send(prev_rows, prev_out, o_send.at[6], o_recv.at[6], to_y)
        red.send(prev_rows, prev_out, o_send.at[7], o_recv.at[7], to_c)
        fetch(prev_rows, prev_out, out_sem.at[2]).wait()

    def exchange(buf, own_slot, devs, ssem, rsem):
        for dev in devs:
            red.send(buf.at[own_slot], buf.at[own_slot], ssem, rsem, dev)

    vgx[0, d] = vg[...]
    for dev in dp_peers:
        red.send(vgx.at[0, d], vgx.at[0, d], v_send.at[0], v_recv.at[0], dev)
    red.after_z(3, 1, 1)
    red.after_x(5)
    red.after_z(4, 0, 0)
    wait_bytes(vgx.at[0, pl.ds(0, n_dp - 1)], v_recv.at[0])
    total = vgx[0, 0]
    for k in range(1, n_dp):
        total += vgx[0, k]
    vgx[1, t] = total
    for dev in (to_y, to_c, diag):
        red.send(vgx.at[1, t], vgx.at[1, t], v_send.at[1], v_recv.at[1], dev)
    red.after_z(5, 0, 1)
    for m in range(3):
        red.finish(m)
    part = jnp.zeros((8, LANES), F32)
    for m in range(3):
        sq = fin[m] * fin[m]
        acc = sq[:, 0:LANES]
        for k in range(1, D // LANES):
            acc += sq[:, k * LANES : (k + 1) * LANES]
        part += jnp.sum(acc.reshape(-1, 8, LANES), 0)
    ssx[0, d] = part
    for dev in dp_peers:
        red.send(ssx.at[0, d], ssx.at[0, d], s_send.at[0], s_recv.at[0], dev)
    fin_cp = fetch(fin, fin_out, in_sem.at[0])
    wait_bytes(vgx.at[1, pl.ds(0, 3)], v_recv.at[1])
    total = vgx[1, 0]
    for k in range(1, 4):
        total += vgx[1, k]
    vg[...] = total
    vg_cp = fetch(vg, vgrad_out, in_sem.at[1])
    wait_bytes(ssx.at[0, pl.ds(0, n_dp - 1)], s_recv.at[0])
    total = ssx[0, 0]
    for k in range(1, n_dp):
        total += ssx[0, k]
    ssx[1, t] = total
    for dev in (to_y, to_c, diag):
        red.send(ssx.at[1, t], ssx.at[1, t], s_send.at[1], s_recv.at[1], dev)
    wait_bytes(all_out.at[t], o_recv.at[4])
    red.send(igr_out.at[there], igr_out.at[there], o_send.at[8], o_recv.at[8], to_c)

    @pl.when(t == 0)
    def _():
        wait_bytes(prev_out, o_recv.at[6])
        red.send(prev_out, prev_out, o_send.at[7], o_recv.at[7], to_c)

    wait_bytes(ssx.at[1, pl.ds(0, 3)], s_recv.at[1])
    total = ssx[1, 0]
    for k in range(1, 4):
        total += ssx[1, k]
    part_ref = ssx.at[2, 0]
    part_ref[...] = total
    ss_cp = fetch(part_ref, ss_out, in_sem.at[2])
    for k in (1, 2, 5, 8):
        wait_bytes(all_out.at[t], o_recv.at[k])

    @pl.when(c == 1)
    def _():
        wait_bytes(prev_out, o_recv.at[7])

    for k in (0, 1, 2, 4, 5, 8):
        wait_bytes(all_out.at[t], o_send.at[k])

    @pl.when(t == 2)
    def _():
        wait_bytes(prev_out, o_send.at[6])

    @pl.when(c == 0)
    def _():
        wait_bytes(prev_out, o_send.at[7])

    for u in range(2, 6):
        red.sent(u)
    for u in (4, 5):
        red.core_sent(u)
    wait_bytes(vgx.at[0, pl.ds(0, n_dp - 1)], v_send.at[0])
    wait_bytes(vgx.at[1, pl.ds(0, 3)], v_send.at[1])
    wait_bytes(ssx.at[0, pl.ds(0, n_dp - 1)], s_send.at[0])
    wait_bytes(ssx.at[1, pl.ds(0, 3)], s_send.at[1])
    for cp in local_out + [fin_cp, vg_cp, ss_cp]:
        cp.wait()


def backward(n_dp, w_full, vec, tokens, cot, saved, own_out, own):
    nrm, q, v, kT, ctx, mid, n2, act, slope, probs = saved
    win = own + PREV
    sds = jax.ShapeDtypeStruct
    dma = pltpu.SemaphoreType.DMA
    vm = pltpu.VMEM
    scratch = [
        vm((own, D), BF), vm((D, own), BF), vm((D, own), BF), vm((own, D), BF), vm((own, D), F32),
        vm((4, D, D), BF), vm((4, own, D), BF), vm((win, D), F32),
        vm((2, 2, win, LANES), BF), vm((2, 2, LANES, win), BF), vm((2, 3, own, LANES), BF), vm((2, 2, own, LANES), BF),
        vm((2, 3, 3 * BLK, BLK), BF), vm((3, own, LANES), BF),
        vm((2, win, LANES), F32), vm((2, win, LANES), F32), vm((2, LANES, own), F32), vm((win, 640), BF),
        vm((16, D), F32), vm((16, D), F32), vm((4, 8, 640), F32), vm((2, D, D), BF),
        dma((4,)), dma((5, 4)), dma((5, 4)), dma((2,)), dma((4,)),
    ]
    params = {}
    if n_dp:
        rows = D // n_dp
        out_shape = [
            sds((3, rows, D), F32), sds((16, D), F32), sds((8, LANES), F32),
            sds((4, own, D), BF), sds((PREV, D), BF), sds((4, own, D), BF),
        ]
        scratch += [
            vm((6, D, D), BF), vm((4, D, D), BF), vm((6, D // 2, D), BF), vm((6, n_dp // 2 - 1, rows, D), BF),
            vm((3, rows, D), BF), vm((3, rows, D), BF), vm((3, rows, D), F32), vm((PREV, D), BF),
            vm((2, n_dp, 16, D), F32), vm((3, n_dp, 8, LANES), F32),
            dma((6,)), dma((6,)), dma((6,)), dma((6,)), dma((6,)), dma((6,)), dma((3,)), dma((3,)),
            dma((9,)), dma((9,)), dma((2,)), dma((2,)), dma((2,)), dma((2,)),
        ]
        params = dict(collective_id=2, has_side_effects=True)
    else:
        out_shape = [sds((3, 4, D, D), BF), sds((16, D), F32), sds((own, D), BF), sds((PREV, D), BF)]
    return pl.pallas_call(
        functools.partial(bwd_kernel, n_dp),
        out_shape=out_shape,
        in_specs=[ANY] * 15,
        out_specs=[ANY] * len(out_shape),
        scratch_shapes=scratch,
        compiler_params=pltpu.CompilerParams(vmem_limit_bytes=VMEM_LIMIT, **params),
        name="backward",
    )(w_full, vec, tokens, cot, nrm, q, v, kT, ctx, mid, n2, act, slope, probs, own_out)


def unpack_block(block):
    parts = []
    for k in range(4):
        second = 512 + 64 * k
        parts.append(jnp.concatenate([block[:, 128 * k : 128 * k + 128], block[:, second : second + 64]], 1))
    return jnp.stack(parts[:3], 1), parts[3].T


def adam_step(weight, gradient, first, second, rate, decay):
    first = beta_one * first + (1.0 - beta_one) * gradient
    second = beta_two * second + (1.0 - beta_two) * gradient * gradient
    first_hat = first / (1.0 - beta_one**STEP)
    second_hat = second / (1.0 - beta_two**STEP)
    weight = weight - rate * (first_hat / (jnp.sqrt(second_hat) + epsilon) + decay * weight)
    return (weight, first, second)


def body(
    tokens, cotangent, documents, w_qkv, w_out, w_fc, w_proj, vectors,
    first_qkv, first_out, first_fc, first_proj, first_vec,
    second_qkv, second_out, second_fc, second_proj, second_vec,
):
    n_dp = lax.axis_size("dp")
    n_t = lax.axis_size("tensor")
    own = tokens.shape[0] // n_t
    rows = D // n_dp
    d = lax.axis_index("dp")
    direct = rows % 16 == 0
    kernel_dp = n_dp if direct else 0
    blk = pack_blocks(w_qkv, w_out, w_fc, w_proj)
    gcol, grow = doc_inputs(documents, own)
    if direct:
        w_in = blk
        vec_in = jnp.pad(vectors.astype(BF), ((0, 4), (0, LANES - rows)))
    else:
        w_in = lax.all_gather(blk, ("dp", "tensor"), axis=0).reshape(n_dp, n_t, 3, rows, D)
        w_in = w_in.transpose(2, 1, 0, 3, 4).reshape(3, n_t, D, D)
        vec_in = jnp.pad(lax.all_gather(vectors.astype(BF), "dp", axis=1, tiled=True).astype(F32), ((0, 4), (0, 0)))
    w_full, vec, *saved, own_out = forward(kernel_dp, w_in, vec_in, tokens, gcol, grow, own)
    if not direct:
        w_full = w_in
    grads = backward(kernel_dp, w_full, vec, tokens, cotangent, saved, own_out, own)
    if direct:
        fin, vgrad, squares, own_grads, prev, all_out = grads
        output = all_out.reshape(-1, D)
        whole = own_grads.reshape(-1, D)
        first_row = 2 * own - PREV
        mid_rows = (whole[first_row : 2 * own].astype(F32) + prev.astype(F32)).astype(BF)
        input_grad = jnp.concatenate([whole[:first_row], mid_rows, whole[2 * own :]], 0)
        squares = jnp.sum(squares)
    else:
        tiles, vgrad, own_grad, prev = grads
        output = lax.all_gather(own_out, "tensor", axis=0, tiled=True)
        whole = lax.all_gather(own_grad, "tensor", axis=0, tiled=True).astype(F32)
        prevs = lax.all_gather(prev, "tensor", axis=0).astype(F32)
        for k in range(1, n_t):
            whole = whole.at[k * own - PREV : k * own].add(prevs[k])
        input_grad = whole.astype(BF)
        fin = tiles.reshape(3, n_t, n_dp, rows, D).transpose(2, 1, 0, 3, 4).reshape(-1, D)
        fin = lax.psum_scatter(fin, ("dp", "tensor"), scatter_dimension=0, tiled=True)
        fin = fin.reshape(3, rows, D).astype(F32)
        vgrad = lax.psum(vgrad, ("dp", "tensor"))
        squares = lax.psum(jnp.sum(fin * fin), ("dp", "tensor"))
    vgrad = vgrad[0:12]
    global_norm = jnp.sqrt(squares + jnp.sum(vgrad * vgrad))
    clip = max_norm / jnp.maximum(global_norm, max_norm)
    g_qkv, g_out = unpack_block(fin[0])
    g_vec = lax.dynamic_slice_in_dim(vgrad, d * rows, rows, 1)
    new_qkv, mean_qkv, square_qkv = adam_step(w_qkv, g_qkv * clip, first_qkv, second_qkv, rate_qkv, decay_rate)
    new_out, mean_out, square_out = adam_step(w_out, g_out * clip, first_out, second_out, rate_out, decay_rate)
    new_fc, mean_fc, square_fc = adam_step(w_fc, fin[1] * clip, first_fc, second_fc, rate_fc, decay_rate)
    new_proj, mean_proj, square_proj = adam_step(w_proj, fin[2].T * clip, first_proj, second_proj, rate_proj, decay_rate)
    new_vec, mean_vec, square_vec = adam_step(vectors, g_vec * clip, first_vec, second_vec, rate_vec, 0.0)
    return (
        output, input_grad, global_norm,
        new_qkv, new_out, new_fc, new_proj, new_vec,
        mean_qkv, mean_out, mean_fc, mean_proj, mean_vec,
        square_qkv, square_out, square_fc, square_proj, square_vec,
    )


def solution(mesh):
    rows = P("dp", None)
    weights = (P("dp", None, "tensor"), P("tensor", "dp"), P("dp", "tensor"), P("tensor", "dp"), P(None, "dp"))
    return jax.shard_map(
        body, mesh=mesh, in_specs=(rows, rows, rows) + weights * 3,
        out_specs=(rows, rows, P()) + weights * 3, check_vma=False,
    )
```

```python
import functools
import math

import jax
import jax.numpy as jnp
from jax import lax
from jax.experimental import pallas as pl
from jax.experimental.pallas import tpu as pltpu
from jax.sharding import PartitionSpec as P

D = 768
HD = 64
FF = 3072
STEP = 10
PREV = 512
BLK = 256
LANES = 128
PARTS = 4

beta_one = 0.9
beta_two = 0.999
rate_qkv = 0.03
rate_out = 0.08
rate_fc = 0.03
rate_proj = 0.02
rate_vec = 0.6
decay_rate = 0.01
epsilon = 1e-08
max_norm = 1.0

BF = jnp.bfloat16
F32 = jnp.float32
VMEM_LIMIT = 62 * 2**20
ANY = pl.BlockSpec(memory_space=pl.ANY)
VM = pl.BlockSpec(memory_space=pltpu.VMEM)
GELU_C = math.sqrt(2.0 / math.pi)


def nn(a, b):
    return lax.dot_general(a, b, (((1,), (0,)), ((), ())), preferred_element_type=F32)


def nt(a, b):
    return lax.dot_general(a, b, (((1,), (1,)), ((), ())), preferred_element_type=F32)


MESH = pl.DeviceIdType.MESH


def wait_bytes(ref, sem):
    pltpu.make_async_copy(ref, ref, sem).wait()


def positions():
    d, t = lax.axis_index("dp"), lax.axis_index("tensor")
    return d, t, lax.rem(d, 2), d // 2, t // 2, lax.rem(t, 2)


GATHER = (
    {6: [("after_last", 0), ("spread", 1)]},
    {5: [("after_first", 1)]},
    {3: [("after_x1", 1)]},
    {3: [("after_last", 1), ("last",)]},
)


class Gather:
    Z, X0, Y1, Y0, X1, X1U, C, CU = range(8)

    def __init__(self, n_dp, blk, vecb, w, vecg, send, recv, loc, vsend, vrecv):
        self.n_dp, self.blk, self.vecb, self.w, self.vecg = n_dp, blk, vecb, w, vecg
        self.send, self.recv, self.loc, self.vsend, self.vrecv = send, recv, loc, vsend, vrecv
        self.rows = blk.shape[1]
        self.nz = n_dp // 2
        self.d, self.t, self.x, self.z, self.y, self.c = positions()
        self.to_x = (self.d + 1 - 2 * self.x, self.t)
        self.to_y = (self.d, self.t + 2 - 4 * self.y)
        self.to_c = (self.d, self.t + 1 - 2 * self.c)
        self.u = self.t + 2 - 4 * self.y
        self.half = D // 2

    def dp_peers(self):
        return [(lax.rem(self.d + k, self.n_dp), self.t) for k in range(1, self.n_dp)]

    def at(self, m, t, block, lanes):
        return self.w.at[m, t, pl.ds(pl.multiple_of(block * self.rows, self.rows), self.rows), lanes]

    def copy(self, m, stage, src, dst, dev):
        pltpu.make_async_remote_copy(
            src_ref=src, dst_ref=dst, send_sem=self.send.at[m, stage], recv_sem=self.recv.at[m, stage],
            device_id=dev, device_id_type=MESH,
        ).start()

    def size(self, m, stage):
        if m == 2 and stage in (self.X0, self.Y1):
            return self.w.at[m, 0, pl.ds(0, self.rows), pl.ds(0, self.half)]
        if m == 2 and stage == self.Z:
            return self.w.at[m, 0, pl.ds(0, (self.nz - 1) * 2 * self.rows)]
        rows = (self.nz - 1) * self.rows if stage == self.Z else self.nz * self.rows
        if stage in (self.Y0, self.C, self.CU):
            rows = D
        lanes = self.half if stage in (self.X0, self.Y1, self.Y0, self.X1, self.X1U) else D
        return self.w.at[m, 0, pl.ds(0, rows), pl.ds(0, lanes)]

    def got(self, m, stage):
        wait_bytes(self.size(m, stage), self.recv.at[m, stage])

    def begin(self):
        barrier = pltpu.get_barrier_semaphore()
        peers = self.dp_peers() + [self.to_y, self.to_c]
        for dev in peers:
            pl.semaphore_signal(barrier, inc=1, device_id=dev, device_id_type=MESH)
        for m in range(3):
            pltpu.make_async_copy(self.blk.at[m], self.at(m, self.t, self.d, pl.ds(0, D)), self.loc.at[m]).start()
        pl.semaphore_wait(barrier, len(peers))
        for dev in self.dp_peers():
            pltpu.make_async_remote_copy(
                src_ref=self.vecb, dst_ref=self.vecg.at[self.d], send_sem=self.vsend, recv_sem=self.vrecv,
                device_id=dev, device_id_type=MESH,
            ).start()
        self.vecg[self.d] = self.vecb[...]
        self.along_z(0)
        own = self.blk.at[2]
        for stage, lanes, dev in (
            (self.X0, pl.ds(0, self.half), self.to_x), (self.Y1, pl.ds(self.half, self.half), self.to_y)
        ):
            self.copy(2, stage, own.at[:, lanes], self.at(2, self.t, self.d, lanes), dev)

    def middle(self):
        self.got(2, self.X0)
        self.got(2, self.Y1)
        wait_bytes(self.blk.at[2], self.loc.at[2])
        low, high = pl.ds(0, self.half), pl.ds(self.half, self.half)
        pair = pl.ds(pl.multiple_of(self.z * 2 * self.rows, 2 * self.rows), 2 * self.rows)
        for k in range(1, self.nz):
            dev = (lax.rem(self.d + 2 * k, self.n_dp), self.t)
            for ref in (
                self.w.at[2, self.t, pair, low], self.at(2, self.t, self.d, high), self.at(2, self.u, self.d, high)
            ):
                self.copy(2, self.Z, ref, ref, dev)

    def last(self):
        self.got(2, self.Z)
        ref = self.w.at[2, self.t, :, pl.ds(0, self.half)]
        self.copy(2, self.Y0, ref, ref, self.to_y)
        high = pl.ds(self.half, self.half)
        self.columns(2, self.X1, self.t, high, self.to_x)
        self.columns(2, self.X1U, self.u, high, self.to_x)

    def vectors(self):
        wait_bytes(self.vecg.at[pl.ds(0, self.n_dp - 1)], self.vrecv)
        width = D // self.n_dp
        lane = lax.broadcasted_iota(jnp.int32, (LANES, D), 0)
        col = lax.broadcasted_iota(jnp.int32, (LANES, D), 1)
        total = jnp.zeros((16, D), F32)
        for p in range(self.n_dp):
            pick = jnp.where((col == lane + p * width) & (lane < width), 1.0, 0.0).astype(BF)
            total += nn(self.vecg[p], pick)
        return total

    def along_z(self, m):
        for k in range(1, self.nz):
            dev = (lax.rem(self.d + 2 * k, self.n_dp), self.t)
            self.copy(m, self.Z, self.blk.at[m], self.at(m, self.t, self.d, pl.ds(0, D)), dev)

    def columns(self, m, stage, t, lanes, dev):
        for zz in range(self.nz):
            ref = self.at(m, t, 2 * zz + self.x, lanes)
            self.copy(m, stage, ref, ref, dev)

    def got_z(self, m):
        self.got(m, self.Z)
        wait_bytes(self.blk.at[m], self.loc.at[m])

    def spread(self, m):
        low, high = pl.ds(0, self.half), pl.ds(self.half, self.half)
        self.columns(m, self.Y1, self.t, high, self.to_y)
        self.columns(m, self.X0, self.t, low, self.to_x)

    def after_first(self, m):
        self.got(m, self.X0)
        ref = self.w.at[m, self.t, :, pl.ds(0, self.half)]
        self.copy(m, self.Y0, ref, ref, self.to_y)
        high = pl.ds(self.half, self.half)
        self.columns(m, self.X1, self.t, high, self.to_x)
        self.got(m, self.Y1)
        self.columns(m, self.X1U, self.u, high, self.to_x)

    def after_x1(self, m):
        self.got(m, self.X1)
        ref = self.w.at[m, self.t]
        self.copy(m, self.C, ref, ref, self.to_c)

    def after_last(self, m):
        self.got(m, self.Y0)
        self.got(m, self.X1U)
        ref = self.w.at[m, self.u]
        self.copy(m, self.CU, ref, ref, self.to_c)

    def finish(self):
        for m in range(3):
            for stage in range(8):
                wait_bytes(self.size(m, stage), self.send.at[m, stage])
        wait_bytes(self.vecg.at[pl.ds(0, self.n_dp - 1)], self.vsend)


def ln_parts(x):
    mean = jnp.mean(x, -1, keepdims=True)
    centred = x - mean
    inv = lax.rsqrt(jnp.mean(centred * centred, -1, keepdims=True) + 1e-05)
    return centred * inv, inv


def ln_back(e, u, inv):
    return inv * (
        e - jnp.mean(e, -1, keepdims=True) - u * jnp.mean(e * u, -1, keepdims=True)
    )


def group_tiles(rows, group):
    base = (group // 2) * 384
    low = lax.broadcasted_iota(jnp.int32, (rows.shape[0], LANES), 1) < HD
    first = rows[:, base : base + 128]
    second = rows[:, base + 128 : base + 256]
    third = rows[:, base + 256 : base + 384]
    if group % 2 == 0:
        return first, second
    second, third = pltpu.roll(second, HD, 1), pltpu.roll(third, HD, 1)
    return jnp.where(low, second, third), third


def ungroup_tiles(even, odd):
    low = lax.broadcasted_iota(jnp.int32, even[0].shape, 1) < HD
    pair = pltpu.roll(odd[0], HD, 1)
    single = pltpu.roll(odd[1], HD, 1)
    return even[0], jnp.where(low, even[1], pair), jnp.where(low, pair, single)


def fwd_kernel(
    n_dp, w_in, vec_in, tok_hbm, gcol, grow,
    w_hbm, vec_out, nrm_out, q_out, v_out, kT_out, ctx_out, mid_out, n2_out, act_out, slope_out, probs_out, inv_out, invT_out, out_out,
    xw, nrm, wa, wf, wp, qm, kt, vt, ktT, vtT, ctxT, ctx, mb, mid, n2, acc, act, slope, pst, vec_ref, sc, inv, invT, bias,
    in_sem, w_sem, out_sem, p_sem, *gather_refs,
):
    gather = Gather(n_dp, w_in, vec_in, w_hbm, *gather_refs) if n_dp else None
    if gather:
        gather.begin()
    else:
        w_hbm = w_in
    rank = lax.axis_index("tensor")
    own = xw.shape[0] - PREV
    start = jnp.maximum(rank * own - PREV, 0)
    cp_prev = pltpu.make_async_copy(tok_hbm.at[pl.ds(pl.multiple_of(start, 256), PREV)], xw.at[pl.ds(0, PREV)], in_sem.at[0])
    cp_own = pltpu.make_async_copy(tok_hbm.at[pl.ds(pl.multiple_of(rank * own, 256), own)], xw.at[pl.ds(PREV, own)], in_sem.at[1])
    cp_prev.start()
    cp_own.start()
    outs = []
    groups = [rank, rank + 1 - 2 * lax.rem(rank, 2)]
    groups += [lax.rem(k + 2, 4) for k in groups]

    def load(m, k, dst):
        g = groups[k]
        cp = pltpu.make_async_copy(w_hbm.at[m, g], dst.at[g], w_sem.at[m, k])
        cp.start()
        return cp

    def put(src, dst):
        cp = pltpu.make_async_copy(src, dst, out_sem.at[len(outs)])
        cp.start()
        outs.append(cp)

    for i in range(3):
        keys = gcol[pl.ds(i * BLK, 3 * BLK), :]
        same = keys == grow[0:1, pl.ds(i * BLK, BLK)]
        row = lax.broadcasted_iota(jnp.int32, (3 * BLK, BLK), 0)
        col = lax.broadcasted_iota(jnp.int32, (3 * BLK, BLK), 1)
        mb[i] = jnp.where(same & (row <= col + PREV), 0.0, -1e30).astype(F32)
    cp_prev.wait()
    cp_own.wait()
    vec = gather.vectors() if gather else vec_in[...]
    vec_ref[...] = vec
    put(vec_ref, vec_out)

    def ln_one(r, _):
        rows = pl.ds(pl.multiple_of(r * 128, 128), 128)
        u, _inv = ln_parts(xw[rows, :].astype(F32))
        nrm[rows, :] = (u * vec[0:1] + vec[1:2]).astype(BF)
        return 0

    lax.fori_loop(0, xw.shape[0] // 128, ln_one, 0)
    put(nrm, nrm_out)
    for g in range(4):
        pair, single = group_tiles(vec[0:8], g)
        bias[g, :, 0:128] = pair
        bias[g, :, 128:256] = single
        ctxT[2 * g + 1, 0:HD, :] = jnp.zeros((HD, own), BF)
    if gather:
        gather.got_z(0)
        gather.spread(0)
        gather.along_z(1)
        gather.after_first(0)
        gather.after_x1(0)
    low = lax.broadcasted_iota(jnp.int32, (BLK, LANES), 1) < HD

    def project(k):
        g = groups[k]
        bq_pair, bq_single = bias[g, 2:3, 0:128], bias[g, 2:3, 128:256]
        bv_pair, bv_single = bias[g, 3:4, 0:128], bias[g, 3:4, 128:256]

        def qkv(rc, _):
            rows = pl.ds(pl.multiple_of(rc * BLK, BLK), BLK)
            x = nrm[rows, :]
            one = nn(x, wa[g, :, 0:384])
            two = nn(x, wa[g, :, 512:768])
            k_pair = one[:, 128:256].astype(BF)
            v_pair = (one[:, 256:384] + bv_pair).astype(BF)
            kt[2 * g, rows, :] = k_pair
            vt[2 * g, rows, :] = v_pair
            ktT[2 * g, :, rows] = k_pair.T
            vtT[2 * g, :, rows] = v_pair.T
            qk, vo = two[:, 0:128], two[:, 128:256]
            k_single = jnp.where(low, pltpu.roll(qk, HD, 1), 0.0).astype(BF)
            v_single = jnp.where(low, vo + bv_single, 0.0)
            kt[2 * g + 1, rows, :] = k_single
            vt[2 * g + 1, rows, :] = pltpu.roll(v_single, HD, 1).astype(BF)
            ktT[2 * g + 1, :, rows] = k_single.T
            vtT[2 * g + 1, :, rows] = v_single.astype(BF).T

            @pl.when(rc >= PREV // BLK)
            def _():
                orows = pl.ds(pl.multiple_of(rc * BLK - PREV, BLK), BLK)
                q_pair = (one[:, 0:128] + bq_pair).astype(BF).astype(F32) * 0.125
                q_single = (qk + bq_single).astype(BF).astype(F32) * 0.125
                qm[3 * g, orows, :] = jnp.where(low, q_pair, 0.0).astype(BF)
                qm[3 * g + 1, orows, :] = jnp.where(low, 0.0, q_pair).astype(BF)
                qm[3 * g + 2, orows, :] = jnp.where(low, q_single, 0.0).astype(BF)

            return 0

        lax.fori_loop(0, nrm.shape[0] // BLK, qkv, 0)

    def probs_put(h, slot):
        return [
            pltpu.make_async_copy(
                pst.at[slot, i], probs_out.at[h, pl.ds(i * BLK, 3 * BLK), pl.ds(i * BLK, BLK)], p_sem.at[slot]
            )
            for i in range(3)
        ]

    def attend(g, k, pump):
        if k:
            for hh in range(3):
                wait_bytes(pst.at[hh], p_sem.at[hh])

        def score(n):
            hh, i = divmod(n, 3)
            keys = kt[2 * g + hh // 2, pl.ds(i * BLK, 3 * BLK), :]
            sc[i] = nt(keys, qm[3 * g + hh, pl.ds(i * BLK, BLK), :]) + mb[i]

        def soft(n):
            hh, i = divmod(n, 3)
            top = jnp.full((8, BLK), -1e30, F32)
            for c in range(0, 3 * BLK, 128):
                top = jnp.maximum(top, jnp.max(sc[i, c : c + 128, :].reshape(16, 8, BLK), 0))
            top = jnp.max(top, 0, keepdims=True)
            total = jnp.zeros((8, BLK), F32)
            for c in range(0, 3 * BLK, 128):
                p = jnp.exp(sc[i, c : c + 128, :] - top)
                total += jnp.sum(p.reshape(16, 8, BLK), 0)
                pst[hh, i, c : c + 128, :] = p.astype(BF)
            inv[pl.ds(3 * g + hh, 1), pl.ds(i * BLK, BLK)] = 1.0 / jnp.sum(total, 0, keepdims=True)

        def value(n):
            hh, i = divmod(n, 3)
            mine = pl.ds(i * BLK, BLK)
            tile, src, dst = 2 * g + hh // 2, HD * (hh == 1), HD * (hh != 0)
            o = nn(vtT[tile, src : src + HD, pl.ds(i * BLK, 3 * BLK)], pst[hh, i])
            ctxT[tile, dst : dst + HD, mine] = (o * inv[pl.ds(3 * g + hh, 1), mine]).astype(BF)
            if i == 2:
                for cp in probs_put(3 * g + hh, hh):
                    cp.start()

        score(0)
        for n in range(9):
            if gather:
                for name, *args in pump.get(n, ()):
                    getattr(gather, name)(*args)
            if n < 8:
                score(n + 1)
            soft(n)
            if n:
                value(n - 1)
        value(8)

    for k in range(4):
        if gather and k == 1:
            gather.got(0, gather.C)
        if gather and k == 3:
            gather.got(0, gather.CU)
        load(0, k, wa).wait()
        project(k)
        if gather and k == 0:
            gather.got_z(1)
            gather.middle()
        attend(groups[k], k, GATHER[k])
    put(qm, q_out)
    put(vt, v_out)
    put(ktT, kT_out)
    for t in range(8):
        ctx[t] = ctxT[t].T
    put(ctx, ctx_out)
    inv[12:, :] = jnp.zeros((LANES - 12, own), F32)
    invT[...] = inv[...].T
    put(inv.at[pl.ds(0, 16)], inv_out)
    put(invT, invT_out)

    def out_proj(rc, _):
        rows = pl.ds(pl.multiple_of(rc * BLK, BLK), BLK)
        total = xw[pl.ds(pl.multiple_of(rc * BLK + PREV, BLK), BLK), :].astype(F32) + vec[4:5]
        for g in range(4):
            total += nt(ctx[2 * g, rows, :], wa[g, :, 384:512])
            total += nt(ctx[2 * g + 1, rows, :], wa[g, :, 640:768])
        mid[rows, :] = total
        u, _inv = ln_parts(total)
        n2[rows, :] = (u * vec[5:6] + vec[6:7]).astype(BF)
        acc[rows, :] = total + vec[7:8]
        return 0

    lax.fori_loop(0, own // BLK, out_proj, 0)
    put(mid, mid_out)
    put(n2, n2_out)
    if gather:
        gather.got(1, gather.C)
        gather.got(1, gather.CU)
    fc_loads = [load(1, k, wf) for k in range(4)]
    proj_loads = [] if gather else [load(2, k, wp) for k in range(4)]
    for k in range(4):
        t = groups[k]
        fc_loads[k].wait()
        fc_bias = vec_ref[pl.ds(8 + t, 1), :]

        def mlp(rc, _):
            rows = pl.ds(pl.multiple_of(rc * BLK, BLK), BLK)
            z = nn(n2[rows, :], wf[t]) + fc_bias
            th = jnp.tanh(GELU_C * (z + 0.044715 * z * z * z))
            half = 0.5 * (1.0 + th)
            act[t, rows, :] = (z * half).astype(BF)
            slope[t, rows, :] = (
                half + 0.5 * z * (1.0 - th * th) * (GELU_C * (1.0 + 3 * 0.044715 * z * z))
            ).astype(BF)
            return 0

        lax.fori_loop(0, own // BLK, mlp, 0)
        put(act.at[t], act_out.at[t])
        put(slope.at[t], slope_out.at[t])
        if gather and k == 0:
            gather.after_x1(2)
            proj_loads.append(load(2, 0, wp))
    if gather:
        gather.after_last(2)
        proj_loads.append(load(2, 2, wp))
        gather.got(2, gather.C)
        proj_loads.append(load(2, 1, wp))
        gather.got(2, gather.CU)
        proj_loads.append(load(2, 3, wp))
    for k in (0, 2, 1, 3):
        t = groups[k]
        proj_loads[(0, 2, 1, 3).index(k)].wait()

        def mlp_out(rc, _):
            rows = pl.ds(pl.multiple_of(rc * BLK, BLK), BLK)
            acc[rows, :] += nt(act[t, rows, :], wp[t])
            return 0

        lax.fori_loop(0, own // BLK, mlp_out, 0)
    xw[0:own, :] = acc[...].astype(BF)
    put(xw.at[pl.ds(0, own)], out_out)
    for hh in range(3):
        wait_bytes(pst.at[hh], p_sem.at[hh])
    for cp in outs:
        cp.wait()
    if gather:
        gather.finish()


def forward(n_dp, w_in, vec, tokens, gcol, grow, own):
    win = own + PREV
    sds = jax.ShapeDtypeStruct
    out_shape = [
        sds((3, 4, D, D) if n_dp else (8, LANES), BF),
        sds((16, D), F32), sds((win, D), BF), sds((12, own, LANES), BF), sds((8, win, LANES), BF),
        sds((8, LANES, win), BF), sds((8, own, LANES), BF), sds((own, D), F32), sds((own, D), BF),
        sds((4, own, D), BF), sds((4, own, D), BF), sds((12, win, own), BF), sds((16, own), F32), sds((own, LANES), F32), sds((own, D), BF),
    ]
    scratch = [
        pltpu.VMEM((win, D), BF), pltpu.VMEM((win, D), BF),
        pltpu.VMEM((4, D, D), BF), pltpu.VMEM((4, D, D), BF), pltpu.VMEM((4, D, D), BF),
        pltpu.VMEM((12, own, LANES), BF), pltpu.VMEM((8, win, LANES), BF), pltpu.VMEM((8, win, LANES), BF),
        pltpu.VMEM((8, LANES, win), BF), pltpu.VMEM((8, LANES, win), BF),
        pltpu.VMEM((8, LANES, own), BF), pltpu.VMEM((8, own, LANES), BF),
        pltpu.VMEM((3, 3 * BLK, BLK), F32), pltpu.VMEM((own, D), F32), pltpu.VMEM((own, D), BF),
        pltpu.VMEM((own, D), F32), pltpu.VMEM((4, own, D), BF), pltpu.VMEM((4, own, D), BF),
        pltpu.VMEM((3, 3, 3 * BLK, BLK), BF), pltpu.VMEM((16, D), F32),
        pltpu.VMEM((3, 3 * BLK, BLK), F32), pltpu.VMEM((LANES, own), F32), pltpu.VMEM((own, LANES), F32),
        pltpu.VMEM((4, 8, 256), F32),
        pltpu.SemaphoreType.DMA((2,)), pltpu.SemaphoreType.DMA((3, 4)), pltpu.SemaphoreType.DMA((24,)),
        pltpu.SemaphoreType.DMA((3,)),
    ]
    params = {}
    if n_dp:
        scratch += [
            pltpu.VMEM((n_dp, 16, LANES), BF), pltpu.SemaphoreType.DMA((3, 8)), pltpu.SemaphoreType.DMA((3, 8)),
            pltpu.SemaphoreType.DMA((3,)), pltpu.SemaphoreType.DMA, pltpu.SemaphoreType.DMA,
        ]
        params = dict(collective_id=1, has_side_effects=True)
    return pl.pallas_call(
        functools.partial(fwd_kernel, n_dp),
        out_shape=out_shape,
        in_specs=[VM if n_dp else ANY, VM, ANY, VM, VM],
        out_specs=[ANY] * len(out_shape),
        scratch_shapes=scratch,
        compiler_params=pltpu.CompilerParams(vmem_limit_bytes=VMEM_LIMIT, **params),
        name="forward",
    )(w_in, vec, tokens, gcol, grow)


def pack_blocks(w_qkv, w_out, w_fc, w_proj):
    q, k, v, o = w_qkv[:, 0], w_qkv[:, 1], w_qkv[:, 2], w_out.T
    pairs = [a[:, :128] for a in (q, k, v, o)]
    singles = [a[:, 128:] for a in (q, k, v, o)]
    return jnp.stack([jnp.concatenate(pairs + singles, 1), w_fc, w_proj.T]).astype(BF)


def doc_inputs(documents, own):
    rank = lax.axis_index("tensor")
    rows = documents.shape[0]
    gid = (documents + 8 * jnp.arange(rows, dtype=jnp.int32)[:, None]).reshape(-1)
    padded = jnp.concatenate([jnp.full((PREV,), -1, jnp.int32), gid])
    win = lax.dynamic_slice_in_dim(padded, rank * own, own + PREV)
    mine = lax.dynamic_slice_in_dim(gid, rank * own, own)
    return win[:, None], jnp.broadcast_to(mine[None], (8, own))


SCHEDULE = {
    ("p", 1): [("along_x", 0)],
    ("f", 1): [("after_x", 0), ("along_x", 1)],
    "start": [("forward",), ("after_x", 1), ("along_x", 2), ("after_z", 0)],
    ("h", 0): [],
    ("a", 0): [("after_x", 2), ("along_x", 3), ("after_z", 1)],
    ("a", 1): [],
    ("h", 2): [("after_x", 3), ("along_x", 4), ("after_z", 2)],
    ("h", 3): [("after_x", 4), ("after_z", 3)],
    ("w", 3): [("along_x", 5)],
    "end": [("after_z", 4), ("after_x", 5)],
}


class Reduce:
    def __init__(self, n_dp, sb, rc, su, rx, rz, ry, ys, fin, sems):
        self.n_dp, self.nz, self.rows = n_dp, n_dp // 2, D // n_dp
        self.sb, self.rc, self.su, self.rx, self.rz, self.ry, self.ys, self.fin = sb, rc, su, rx, rz, ry, ys, fin
        self.cs, self.cr, self.xs, self.xr, self.zs, self.zr, self.ysem, self.yr = sems
        self.d, self.t, self.x, self.z, self.y, self.c = positions()
        self.to_x = (self.d + 1 - 2 * self.x, self.t)
        self.to_y = (self.d, self.t + 2 - 4 * self.y)
        self.to_c = (self.d, self.t + 1 - 2 * self.c)

    def block(self, ref, index):
        return ref.at[pl.ds(pl.multiple_of(index * self.rows, self.rows), self.rows)]

    def send(self, src, dst, ssem, rsem, dev):
        pltpu.make_async_remote_copy(
            src_ref=src, dst_ref=dst, send_sem=ssem, recv_sem=rsem, device_id=dev, device_id_type=MESH
        ).start()

    def to_core(self, u):
        self.send(self.sb.at[u % 2], self.rc.at[u], self.cs.at[u], self.cr.at[u], self.to_c)

    def core_sent(self, u):
        wait_bytes(self.sb.at[u % 2], self.cs.at[u])

    def core_got(self, u):
        wait_bytes(self.rc.at[u], self.cr.at[u])

    def slot(self, u):
        return u % 4

    def along_x(self, u):
        for zz in range(self.nz):
            src = self.block(self.su.at[self.slot(u)], 2 * zz + 1 - self.x)
            self.send(src, self.rx.at[u, pl.ds(zz * self.rows, self.rows)], self.xs.at[u], self.xr.at[u], self.to_x)

    def after_x(self, u):
        wait_bytes(self.rx.at[u], self.xr.at[u])
        tile = self.su.at[self.slot(u)]
        for zz in range(self.nz):
            mine = self.block(tile, 2 * zz + self.x)
            got = self.rx[u, pl.ds(zz * self.rows, self.rows), :]
            mine[...] = (mine[...].astype(F32) + got.astype(F32)).astype(BF)
        for k in range(1, self.nz):
            zz = lax.rem(self.z + k, self.nz)
            src = self.block(tile, 2 * zz + self.x)
            dev = (2 * zz + self.x, self.t)
            self.send(src, self.rz.at[u, k - 1], self.zs.at[u], self.zr.at[u], dev)

    def after_z(self, u):
        m, yy = 2 - u // 2, u % 2
        wait_bytes(self.rz.at[u], self.zr.at[u])
        total = self.block(self.su.at[self.slot(u)], 2 * self.z + self.x)[...].astype(F32)
        for k in range(self.nz - 1):
            total += self.rz[u, k].astype(F32)

        @pl.when(self.y == yy)
        def _():
            self.fin[m] = total

        @pl.when(self.y != yy)
        def _():
            self.ys[m] = total.astype(BF)
            self.send(self.ys.at[m], self.ry.at[m], self.ysem.at[m], self.yr.at[m], self.to_y)

    def sent(self, u):
        wait_bytes(self.rx.at[u], self.xs.at[u])
        wait_bytes(self.rz.at[u], self.zs.at[u])

    def finish(self, m):
        wait_bytes(self.ry.at[m], self.yr.at[m])
        self.fin[m] += self.ry[m].astype(F32)
        wait_bytes(self.ys.at[m], self.ysem.at[m])


def bwd_kernel(
    n_dp, w_hbm, vec_hbm, tok_hbm, cot_hbm, nrm_hbm, q_hbm, v_hbm, kT_hbm, ctx_hbm, mid_hbm, n2_hbm,
    act_hbm, slope_hbm, probs_hbm, inv_hbm, invT_hbm, own_out_hbm,
    *rest,
):
    if n_dp:
        fin_out, vgrad_out, ss_out, igr_out, prev_out, all_out = rest[:6]
        rest = rest[6:]
    else:
        tiles_out, vgrad_out, igr_out, prev_out = rest[:4]
        rest = rest[4:]
    (cot, cotT, shared, gm, w4, pool, gn1, vs, kTs, qs, ctxs, pbuf, gctx, dk, dv, dqT, gj, vec_ref, vg, cs_ref,
     sb, dps, inv, invT, in_sem, tile_sem, ct_sem, p_sem, out_sem) = rest[:29]
    rest = rest[29:]
    n2T, gp, dsT = shared.at[pl.ds(0, D)], shared.at[pl.ds(D, D)], shared.at[pl.ds(0, D + PREV)]
    d, t, x, z, y, c = positions()
    own = cot.shape[0]
    own_rows = pl.ds(pl.multiple_of(t * own, 256), own)
    red = None
    if n_dp:
        (rc, su, rx, rz, ry, ys, fin, comb, vgx, ssx, *sems) = rest
        red = Reduce(n_dp, sb, rc, su, rx, rz, ry, ys, fin, sems[:8])
        o_send, o_recv, v_send, v_recv, s_send, s_recv = sems[8:]
        to_c, to_y = red.to_c, red.to_y
        diag = (d, t + 2 - 4 * y + 1 - 2 * c)
        dp_peers = [(lax.rem(d + k, n_dp), t) for k in range(1, n_dp)]
        barrier = pltpu.get_barrier_semaphore()
        peers = dp_peers + [to_y, to_c, diag]
        for dev in peers:
            pl.semaphore_signal(barrier, inc=1, device_id=dev, device_id_type=MESH)

    def fetch(src, dst, sem):
        cp = pltpu.make_async_copy(src, dst, sem)
        cp.start()
        return cp

    order = [1 - c, c, 3 - c, 2 + c]

    def fetch_tile(j):
        s = j % 2
        return [
            fetch(w_hbm.at[2, order[j]], w4.at[s], tile_sem.at[j, 0]),
            fetch(w_hbm.at[1, order[j]], w4.at[2 + s], tile_sem.at[j, 1]),
        ]

    def fetch_slope(j):
        return fetch(slope_hbm.at[order[j]], pool.at[j], tile_sem.at[j, 3])

    cp_cot = fetch(cot_hbm.at[own_rows], cot, in_sem.at[0])
    acts = [fetch(act_hbm.at[order[j]], pool.at[j], tile_sem.at[j, 2]) for j in range(4)]
    cp_n2 = fetch(n2_hbm, gp, in_sem.at[1])
    tiles = {0: fetch_tile(0), 1: fetch_tile(1)}
    cp_vec = fetch(vec_hbm, vec_ref, in_sem.at[2])
    cp_mid = fetch(mid_hbm, gn1.at[pl.ds(0, own)], in_sem.at[3])
    local_out = []
    if n_dp:
        cp_out = fetch(own_out_hbm, sb.at[1], out_sem.at[0])
        pl.semaphore_wait(barrier, len(peers))
        red.send(own_out_hbm, all_out.at[t], o_send.at[0], o_recv.at[0], to_y)
        red.send(own_out_hbm, all_out.at[t], o_send.at[1], o_recv.at[1], to_c)
        cp_out.wait()
        cp_out = fetch(sb.at[1], all_out.at[t], out_sem.at[0])
    vg[...] = jnp.zeros_like(vg)
    ones = jnp.ones((16, own), BF)
    cp_cot.wait()
    cotT[...] = cot[...].T

    def emit(u, keep, rows, lanes, value):
        if not n_dp or not keep:
            sb[u % 2, rows, lanes] = value.astype(BF)
        else:
            su[red.slot(u), rows, lanes] = (value + rc[u, rows, lanes].astype(F32)).astype(BF)

    def chunk(r, size=BLK):
        return pl.ds(pl.multiple_of(r * size, size), size)

    pending = set()

    def before(u, keep):
        if n_dp:
            if keep:
                red.core_got(u)
                if u >= 4:
                    red.sent(u - 4)
            elif u >= 2:
                red.core_sent(u - 2)
        elif u % 2 in pending:
            wait_bytes(sb.at[u % 2], tile_sem.at[4, u % 2])

    def after(u, keep, m, which):
        if n_dp:
            if not keep:
                red.to_core(u)
        else:
            pending.add(u % 2)
            pltpu.make_async_copy(sb.at[u % 2], tiles_out.at[m, which], tile_sem.at[4, u % 2]).start()

    def pump(point):
        if not n_dp:
            return
        for name, *args in SCHEDULE.get(point, ()):
            if name == "forward":
                wait_bytes(all_out.at[t], o_recv.at[0])
                there = all_out.at[t + 2 - 4 * y]
                red.send(there, there, o_send.at[2], o_recv.at[2], to_c)
            else:
                getattr(red, name)(*args)

    slopes = {}
    for j in (0, 2, 1, 3):
        yy, keep = j // 2, j % 2 == 1
        acts[j].wait()
        if n_dp and j == 2:
            cp_out.wait()
        before(yy, keep)

        def grad_p(r, _):
            emit(yy, keep, chunk(r), slice(None), nn(cotT[chunk(r), :], pool[j]))
            return 0

        lax.fori_loop(0, D // BLK, grad_p, 0)
        after(yy, keep, 2, order[j])
        slopes[j] = fetch_slope(j)
        pump(("p", j))
    cp_n2.wait()
    n2T[...] = gp[...].T
    for j in range(4):
        yy, keep = j // 2, j % 2 == 1
        s = j % 2
        which = order[j]
        u_f = 2 + yy
        for cp in tiles[j] + [slopes[j]]:
            cp.wait()

        def grads(r, _):
            rows = chunk(r)
            ga = nn(cot[rows, :], w4[s]).astype(BF).astype(F32)
            g = (ga * pool[j, rows, :].astype(F32)).astype(BF)
            gp[rows, :] = g
            back = nt(g, w4[2 + s])
            if j == 0:
                gm[rows, :] = back
            else:
                gm[rows, :] += back
            return 0

        lax.fori_loop(0, own // BLK, grads, 0)
        if j < 2:
            tiles[j + 2] = fetch_tile(j + 2)
        vg[pl.ds(8 + which, 1), :] = nn(ones, gp[...])[0:1]
        before(u_f, keep)

        def grad_f(r, _):
            emit(u_f, keep, chunk(r), slice(None), nn(n2T[chunk(r), :], gp[...]))
            return 0

        lax.fori_loop(0, D // BLK, grad_f, 0)
        after(u_f, keep, 1, which)
        pump(("f", j))
    cp_vec.wait()
    cp_mid.wait()
    wa_cps = [fetch(w_hbm.at[0, k], w4.at[k], ct_sem.at[0, k]) for k in range(4)]
    cp_nrm_own = fetch(nrm_hbm.at[pl.ds(PREV, own)], pool.at[0], in_sem.at[1])
    cp_nrm_prev = fetch(nrm_hbm.at[pl.ds(0, PREV)], pool.at[1, pl.ds(0, PREV)], in_sem.at[3])

    def fetch_heads(j):
        s, g = j % 2, order[j]
        return [
            fetch(v_hbm.at[pl.ds(2 * g, 2)], vs.at[s], ct_sem.at[1 + j, 0]),
            fetch(kT_hbm.at[pl.ds(2 * g, 2)], kTs.at[s], ct_sem.at[1 + j, 1]),
            fetch(q_hbm.at[pl.ds(3 * g, 3)], qs.at[s], ct_sem.at[1 + j, 2]),
            fetch(ctx_hbm.at[pl.ds(2 * g, 2)], ctxs.at[s], ct_sem.at[1 + j, 3]),
        ]

    heads = {0: fetch_heads(0), 1: fetch_heads(1)}

    def probs_get(g, hh, slot):
        for i in range(3):
            at = (pl.ds(i * BLK, 3 * BLK), pl.ds(i * BLK, BLK))
            pltpu.make_async_copy(probs_hbm.at[3 * g + hh].at[at], pbuf.at[slot].at[at], p_sem.at[slot]).start()

    probs_get(order[0], 0, 0)
    probs_get(order[0], 1, 1)
    cp_inv = [fetch(inv_hbm, inv, in_sem.at[4]), fetch(invT_hbm, invT, in_sem.at[5])]

    def ln_two(r, sums):
        rows = chunk(r, 128)
        u, inv = ln_parts(gn1[rows, :])
        g = gm[rows, :]
        co = cot[rows, :].astype(F32)
        total = co + ln_back(g * vec_ref[5:6, :], u, inv)
        gm[rows, :] = total
        cot[rows, :] = total.astype(BF)
        new = [jnp.sum(v, 0, keepdims=True) for v in (total, g * u, g, co)]
        return tuple(a + b for a, b in zip(sums, new))

    zero = jnp.zeros((1, D), F32)
    sums = lax.fori_loop(0, own // 128, ln_two, (zero,) * 4)
    for k in range(4):
        vg[4 + k : 5 + k, :] = sums[k]
    gattn, gattnT = cot, cotT
    gattnT[...] = gattn[...].T
    cp_nrm_own.wait()
    cp_nrm_prev.wait()
    nrmT, nrmT_prev = pool.at[2], pool.at[3]
    nrmT[...] = pool[0].T
    nrmT_prev[:, 0:PREV] = pool[1, 0:PREV, :].T
    cp_tok_own = fetch(tok_hbm.at[own_rows], pool.at[0], in_sem.at[0])
    tok_start = pl.multiple_of(jnp.maximum(t * own - PREV, 0), 256)
    cp_tok_prev = fetch(tok_hbm.at[pl.ds(tok_start, PREV)], pool.at[1, pl.ds(0, PREV)], in_sem.at[2])
    for cp in wa_cps + cp_inv:
        cp.wait()
    pump("start")
    win = own + PREV
    low = lax.broadcasted_iota(jnp.int32, (BLK, LANES), 1) < HD
    ones_win = jnp.ones((16, win), BF)
    for j in range(4):
        yy, keep = j // 2, j % 2 == 1
        s, g = j % 2, order[j]
        u = 4 + yy
        for cp in heads[j]:
            cp.wait()

        def grad_ctx(r, _):
            rows = chunk(r)
            both = nn(gattn[rows, :], jnp.concatenate([w4[g, :, 384:512], w4[g, :, 640:768]], 1))
            lane = lax.broadcasted_iota(jnp.int32, (BLK, LANES), 1)
            for hh in range(3):
                scale = jnp.sum(jnp.where(lane == 3 * g + hh, invT[rows, :], 0.0), 1, keepdims=True)
                part = both[:, 128:256] if hh == 2 else both[:, 0:128]
                part = part * scale
                gctx[hh, rows, :] = (jnp.where(low, part, 0.0) if hh == 0 else jnp.where(low, 0.0, part)).astype(BF)
            return 0

        lax.fori_loop(0, own // BLK, grad_ctx, 0)
        dqT[1, HD:, :] = jnp.zeros((HD, own), F32)

        def weigh(n):
            hh, i = divmod(n, 3)
            if i == 0:
                slot = (3 * j + hh) % 2
                wait_bytes(pbuf.at[slot, pl.ds(0, 3 * BLK)], p_sem.at[slot])
            dps[i] = nt(vs[s, hh // 2, pl.ds(i * BLK, 3 * BLK), :], gctx[hh, pl.ds(i * BLK, BLK), :])

        def soft(n):
            hh, i = divmod(n, 3)
            slot = (3 * j + hh) % 2
            mine = pl.ds(i * BLK, BLK)
            centre = jnp.zeros((8, BLK), F32)
            for a in range(0, 3 * BLK, 128):
                p = pbuf[slot, pl.ds(i * BLK + a, 128), mine].astype(F32)
                centre += jnp.sum((p * dps[i, a : a + 128, :]).reshape(16, 8, BLK), 0)
            centre = jnp.sum(centre, 0, keepdims=True) * inv[pl.ds(3 * g + hh, 1), mine]
            for a in range(0, 3 * BLK, 128):
                rows = pl.ds(i * BLK + a, 128)
                p = pbuf[slot, rows, mine].astype(F32)
                dsT[rows, mine] = (p * (dps[i, a : a + 128, :] - centre)).astype(BF)

        def query(n):
            hh, i = divmod(n, 3)
            mine, keys = pl.ds(i * BLK, BLK), pl.ds(i * BLK, 3 * BLK)
            half = HD * (hh == 1)
            dqT[hh // 2, half : half + HD, mine] = nn(kTs[s, hh // 2, half : half + HD, keys], dsT[keys, mine])
            if i < 2:
                return
            slot = (3 * j + hh) % 2
            for b in range(5):
                rows = pl.ds(b * BLK, BLK)
                lo, hi = max(0, b - 2) * BLK, (min(2, b) + 1) * BLK
                one = nn(pbuf[slot, rows, lo:hi], gctx[hh, lo:hi, :])
                two = nn(dsT[rows, lo:hi], qs[s, hh, lo:hi, :])
                if hh == 1:
                    one, two = one + dv[0, rows, :], two + dk[0, rows, :]
                dv[hh // 2, rows, :] = one
                dk[hh // 2, rows, :] = two
            if 3 * j + hh < 10:
                probs_get(order[j + (hh + 2) // 3], (hh + 2) % 3, slot)

        weigh(0)
        for n in range(9):
            if n < 8:
                weigh(n + 1)
            soft(n)
            if n % 3:
                query(n - 1)
            if n % 3 == 2:
                query(n)
        pump(("h", j))
        for r in range(win // BLK):
            rows = pl.ds(r * BLK, BLK)
            k_single = pltpu.roll(dk[1, rows, :], HD, 1)
            if r >= PREV // BLK:
                orows = pl.ds(r * BLK - PREV, BLK)
                gj[rows, 0:128] = (dqT[0, :, orows].T * 0.125).astype(BF)
                k_single += dqT[1, :, orows].T * 0.125
            else:
                gj[rows, 0:128] = jnp.zeros((BLK, LANES), BF)
            gj[rows, 128:256] = dk[0, rows, :].astype(BF)
            gj[rows, 256:384] = dv[0, rows, :].astype(BF)
            gj[rows, 384:512] = k_single.astype(BF)
            gj[rows, 512:640] = pltpu.roll(dv[1, rows, :], HD, 1).astype(BF)
        cs_ref[g] = nn(ones_win, gj[...])[0:8]
        before(u, keep)

        def grad_a(r, _):
            rows = chunk(r)
            a_own, a_prev, b = nrmT[rows, :], nrmT_prev[rows, 0:PREV], gattnT[rows, :]
            emit(u, keep, rows, slice(0, 384), nn(a_own, gj[PREV:, 0:384]) + nn(a_prev, gj[0:PREV, 0:384]))
            emit(u, keep, rows, slice(384, 512), nn(b, ctxs[s, 0]))
            last = nn(a_own, gj[PREV:, 384:640]) + nn(a_prev, gj[0:PREV, 384:640])
            emit(u, keep, rows, slice(512, 640), last[:, 0:128])
            emit(u, keep, rows, slice(640, 768), last[:, 128:256] + nn(b, ctxs[s, 1]))
            return 0

        lax.fori_loop(0, D // BLK, grad_a, 0)
        after(u, keep, 0, g)
        pump(("w", j))

        def grad_n1(r, _):
            rows = chunk(r)
            back = nt(gj[rows, 0:384], w4[g, :, 0:384]) + nt(gj[rows, 384:640], w4[g, :, 512:768])
            if j == 0:
                gn1[rows, :] = back
            else:
                gn1[rows, :] += back
            return 0

        lax.fori_loop(0, win // BLK, grad_n1, 0)
        if j < 2:
            heads[j + 2] = fetch_heads(j + 2)
        pump(("a", j))
    cp_tok_own.wait()
    cp_tok_prev.wait()
    igr, prev = w4.at[0], w4.at[1]

    def ln_one(base, src, tokens, dst, add):
        def step(r, sums):
            rows = chunk(r, 128)
            g = gn1[pl.ds(pl.multiple_of(base + r * 128, 128), 128), :]
            u, inv = ln_parts(tokens[rows, :].astype(F32))
            total = ln_back(g * vec_ref[0:1, :], u, inv)
            if add:
                total += gm[rows, :]
            dst[rows, :] = total.astype(BF)
            return (sums[0] + jnp.sum(g * u, 0, keepdims=True), sums[1] + jnp.sum(g, 0, keepdims=True))

        return lax.fori_loop(0, src // 128, step, (zero, zero))

    sp = ln_one(0, PREV, pool.at[1], prev, False)
    if n_dp:

        @pl.when(c == 1)
        def _():
            red.send(prev.at[pl.ds(0, PREV)], comb, o_send.at[3], o_recv.at[3], to_c)

    so = ln_one(PREV, own, pool.at[0], igr, True)
    vg[0:1, :] = sp[0] + so[0]
    vg[1:2, :] = sp[1] + so[1]
    for g in (0, 2):
        for row, (a, b) in ((2, (0, 384)), (3, (256, 512))):
            even = (cs_ref[g, :, a : a + 128], cs_ref[g, :, b : b + 128])
            odd = (cs_ref[g + 1, :, a : a + 128], cs_ref[g + 1, :, b : b + 128])
            for k, part in enumerate(ungroup_tiles(even, odd)):
                col = (g // 2) * 384 + 128 * k
                vg[row : row + 1, col : col + 128] = part[0:1]
    if not n_dp:
        last = [fetch(igr, igr_out, out_sem.at[0]), fetch(prev.at[pl.ds(0, PREV)], prev_out, out_sem.at[1]),
                fetch(vg, vgrad_out, out_sem.at[2])]
        for cp in last:
            cp.wait()
        for k in range(2):
            wait_bytes(sb.at[k], tile_sem.at[4, k])
        return

    @pl.when(c == 0)
    def _():
        wait_bytes(comb, o_recv.at[3])
        igr[own - PREV :, :] = (igr[own - PREV :, :].astype(F32) + comb[...].astype(F32)).astype(BF)

    @pl.when(c == 1)
    def _():
        wait_bytes(comb, o_send.at[3])

    there = t + 2 - 4 * y
    local_out.append(fetch(igr, igr_out.at[t], out_sem.at[1]))
    part_rows = own // PARTS

    def part(which, q):
        return igr_out.at[which, pl.ds(q * part_rows, part_rows)]

    def across(q):
        red.send(igr.at[pl.ds(q * part_rows, part_rows)], part(t, q), o_send.at[9 + q], o_recv.at[9 + q], to_y)

    def part_sent(q):
        wait_bytes(part(t, q), o_send.at[9 + q])

    def pass_on(q):
        wait_bytes(part(t, q), o_recv.at[9 + q])
        red.send(part(there, q), part(there, q), o_send.at[9 + PARTS + q], o_recv.at[9 + PARTS + q], to_c)

    across(0)
    across(1)
    red.send(igr, igr_out.at[t], o_send.at[5], o_recv.at[5], to_c)
    prev_rows = prev.at[pl.ds(0, PREV)]

    def exchange(buf, own_slot, devs, ssem, rsem):
        for dev in devs:
            red.send(buf.at[own_slot], buf.at[own_slot], ssem, rsem, dev)

    def add_up(buf, count):
        total = buf[0]
        for k in range(1, count):
            total += buf[k]
        return total

    tensor_peers = (to_y, to_c, diag)
    vgx[0, d] = vg[...]
    exchange(vgx.at[0], d, dp_peers, v_send.at[0], v_recv.at[0])
    pump("end")
    wait_bytes(vgx.at[0, pl.ds(0, n_dp - 1)], v_recv.at[0])
    vgx[1, t] = add_up(vgx.at[0], n_dp)
    exchange(vgx.at[1], t, tensor_peers, v_send.at[1], v_recv.at[1])
    part_sent(0)
    across(2)
    red.after_z(5)
    part_sent(1)
    across(3)

    @pl.when(t == 2)
    def _():
        red.send(prev_rows, prev_out, o_send.at[6], o_recv.at[6], to_y)
        red.send(prev_rows, prev_out, o_send.at[7], o_recv.at[7], to_c)
        fetch(prev_rows, prev_out, out_sem.at[2]).wait()

    for m in range(3):
        red.finish(m)
    squares = jnp.zeros((8, LANES), F32)
    for m in range(3):
        sq = fin[m] * fin[m]
        cols = sq[:, 0:LANES]
        for k in range(1, D // LANES):
            cols += sq[:, k * LANES : (k + 1) * LANES]
        squares += jnp.sum(cols.reshape(-1, 8, LANES), 0)
    ssx[0, d] = squares
    exchange(ssx.at[0], d, dp_peers, s_send.at[0], s_recv.at[0])
    fin_cp = fetch(fin, fin_out, in_sem.at[0])
    wait_bytes(ssx.at[0, pl.ds(0, n_dp - 1)], s_recv.at[0])
    ssx[1, t] = add_up(ssx.at[0], n_dp)
    exchange(ssx.at[1], t, tensor_peers, s_send.at[1], s_recv.at[1])
    wait_bytes(vgx.at[1, pl.ds(0, 3)], v_recv.at[1])
    vg[...] = add_up(vgx.at[1], 4)
    vg_cp = fetch(vg, vgrad_out, in_sem.at[1])
    for q in range(PARTS):
        pass_on(q)

    @pl.when(t == 0)
    def _():
        wait_bytes(prev_out, o_recv.at[6])
        red.send(prev_out, prev_out, o_send.at[7], o_recv.at[7], to_c)

    wait_bytes(ssx.at[1, pl.ds(0, 3)], s_recv.at[1])
    part_ref = ssx.at[2, 0]
    part_ref[...] = add_up(ssx.at[1], 4)
    ss_cp = fetch(part_ref, ss_out, in_sem.at[2])
    for k in (1, 2, 5):
        wait_bytes(all_out.at[t], o_recv.at[k])

    @pl.when(c == 1)
    def _():
        wait_bytes(prev_out, o_recv.at[7])

    for k in (0, 1, 2, 5):
        wait_bytes(all_out.at[t], o_send.at[k])
    for q in range(PARTS):
        wait_bytes(part(t, q), o_recv.at[9 + PARTS + q])
        wait_bytes(part(t, q), o_send.at[9 + PARTS + q])
    part_sent(2)
    part_sent(3)

    @pl.when(t == 2)
    def _():
        wait_bytes(prev_out, o_send.at[6])

    @pl.when(c == 0)
    def _():
        wait_bytes(prev_out, o_send.at[7])

    for u in range(2, 6):
        red.sent(u)
    for u in (4, 5):
        red.core_sent(u)
    wait_bytes(vgx.at[0, pl.ds(0, n_dp - 1)], v_send.at[0])
    wait_bytes(vgx.at[1, pl.ds(0, 3)], v_send.at[1])
    wait_bytes(ssx.at[0, pl.ds(0, n_dp - 1)], s_send.at[0])
    wait_bytes(ssx.at[1, pl.ds(0, 3)], s_send.at[1])
    for cp in local_out + [fin_cp, vg_cp, ss_cp]:
        cp.wait()


def backward(n_dp, w_full, vec, tokens, cot, saved, own_out, own):
    nrm, q, v, kT, ctx, mid, n2, act, slope, probs, inv, invT = saved
    win = own + PREV
    sds = jax.ShapeDtypeStruct
    dma = pltpu.SemaphoreType.DMA
    vm = pltpu.VMEM
    scratch = [
        vm((own, D), BF), vm((D, own), BF), vm((D + own, D), BF), vm((own, D), F32),
        vm((4, D, D), BF), vm((4, own, D), BF), vm((win, D), F32),
        vm((2, 2, win, LANES), BF), vm((2, 2, LANES, win), BF), vm((2, 3, own, LANES), BF), vm((2, 2, own, LANES), BF),
        vm((2, win, own), BF), vm((3, own, LANES), BF),
        vm((2, win, LANES), F32), vm((2, win, LANES), F32), vm((2, LANES, own), F32), vm((win, 640), BF),
        vm((16, D), F32), vm((16, D), F32), vm((4, 8, 640), F32), vm((2, D, D), BF),
        vm((3, 3 * BLK, BLK), F32), vm((16, own), F32), vm((own, LANES), F32),
        dma((6,)), dma((5, 4)), dma((5, 4)), dma((2,)), dma((4,)),
    ]
    params = {}
    if n_dp:
        rows = D // n_dp
        out_shape = [
            sds((3, rows, D), F32), sds((16, D), F32), sds((8, LANES), F32),
            sds((4, own, D), BF), sds((PREV, D), BF), sds((4, own, D), BF),
        ]
        scratch += [
            vm((6, D, D), BF), vm((4, D, D), BF), vm((6, D // 2, D), BF), vm((6, n_dp // 2 - 1, rows, D), BF),
            vm((3, rows, D), BF), vm((3, rows, D), BF), vm((3, rows, D), F32), vm((PREV, D), BF),
            vm((2, n_dp, 16, D), F32), vm((3, n_dp, 8, LANES), F32),
            dma((6,)), dma((6,)), dma((6,)), dma((6,)), dma((6,)), dma((6,)), dma((3,)), dma((3,)),
            dma((9 + 2 * PARTS,)), dma((9 + 2 * PARTS,)), dma((2,)), dma((2,)), dma((2,)), dma((2,)),
        ]
        params = dict(collective_id=2, has_side_effects=True)
    else:
        out_shape = [sds((3, 4, D, D), BF), sds((16, D), F32), sds((own, D), BF), sds((PREV, D), BF)]
    return pl.pallas_call(
        functools.partial(bwd_kernel, n_dp),
        out_shape=out_shape,
        in_specs=[ANY] * 17,
        out_specs=[ANY] * len(out_shape),
        scratch_shapes=scratch,
        compiler_params=pltpu.CompilerParams(vmem_limit_bytes=VMEM_LIMIT, **params),
        name="backward",
    )(w_full, vec, tokens, cot, nrm, q, v, kT, ctx, mid, n2, act, slope, probs, inv, invT, own_out)


def adam_step(weight, gradient, first, second, rate, decay):
    first = beta_one * first + (1.0 - beta_one) * gradient
    second = beta_two * second + (1.0 - beta_two) * gradient * gradient
    first_hat = first / (1.0 - beta_one**STEP)
    second_hat = second / (1.0 - beta_two**STEP)
    weight = weight - rate * (first_hat / (jnp.sqrt(second_hat) + epsilon) + decay * weight)
    return (weight, first, second)


def adam_kernel(direct, squares, vgrad, fin, gvec, *refs):
    n = 2 if direct else 0
    if direct:
        own_grads, prev, all_out = refs[:3]
        refs = refs[3:]
    ins, refs = refs[:15], refs[15:]
    if direct:
        out_ref, igr_ref = refs[:2]
    norm_ref, outs, refs = refs[n], refs[n + 1 : n + 16], refs[n + 16 :]
    if direct:
        rows_ref, prev_ref, sem = refs
        own = all_out.shape[1]
        loads = [pltpu.make_async_copy(own_grads.at[k], rows_ref.at[k], sem.at[k]) for k in range(4)]
        loads += [pltpu.make_async_copy(all_out.at[k], rows_ref.at[4 + k], sem.at[4 + k]) for k in range(4)]
        loads.append(pltpu.make_async_copy(prev, prev_ref, sem.at[8]))
        for cp in loads:
            cp.start()
    vg = vgrad[0:12, :]
    norm = jnp.sqrt(jnp.sum(squares[...], keepdims=True) + jnp.sum(vg * vg, keepdims=True))
    norm_ref[...] = jnp.broadcast_to(norm, norm_ref.shape)
    clip = max_norm / jnp.maximum(norm, max_norm)

    def update(k, at, grad, rate, decay):
        new = adam_step(ins[k][at], grad * clip, ins[5 + k][at], ins[10 + k][at], rate, decay)
        for j in range(3):
            outs[5 * j + k][at] = new[j]

    def single(j):
        tile = fin[0, :, 512 + 128 * (j // 2) : 640 + 128 * (j // 2)]
        return (pltpu.roll(tile, HD, 1) if j % 2 else tile)

    every = slice(None)
    for j in range(3):
        update(0, (j, every, slice(0, 128)), fin[0, :, 128 * j : 128 * j + 128], rate_qkv, decay_rate)
        update(0, (j, every, slice(128, 192)), single(j)[:, 0:HD], rate_qkv, decay_rate)
    update(1, (slice(0, 128), every), fin[0, :, 384:512].T, rate_out, decay_rate)
    update(1, (slice(128, 192), every), single(3).T[0:HD, :], rate_out, decay_rate)
    update(2, (every, every), fin[1], rate_fc, decay_rate)
    update(3, (every, every), fin[2], rate_proj, decay_rate)
    update(4, (every, every), gvec[...], rate_vec, 0.0)
    if direct:
        stores = []
        for k in (8, 0, 2, 3, 1, 4, 5, 6, 7):
            loads[k].wait()
            if k == 8:
                continue
            if k == 1:
                tail = pl.ds(own - PREV, PREV)
                rows_ref[1, tail, :] = (rows_ref[1, tail, :].astype(F32) + prev_ref[...].astype(F32)).astype(BF)
            dst = igr_ref if k < 4 else out_ref
            cp = pltpu.make_async_copy(rows_ref.at[k], dst.at[pl.ds(k % 4 * own, own)], sem.at[k])
            cp.start()
            stores.append(cp)
        for cp in stores:
            cp.wait()


def optimizer(squares, vgrad, fin, gvec, moved, states):
    direct = moved is not None
    sds = jax.ShapeDtypeStruct
    out_shape = [sds((8, LANES), F32)] + [sds(a.shape, F32) for a in states]
    out_specs = [VM] * len(out_shape)
    in_specs = [VM] * 4
    scratch = []
    args = (squares, vgrad, fin, gvec)
    if direct:
        own = moved[2].shape[1]
        out_shape = [sds((4 * own, D), BF)] * 2 + out_shape
        out_specs = [ANY, ANY] + out_specs
        in_specs += [ANY] * 3
        args += tuple(moved)
        scratch = [pltpu.VMEM((8, own, D), BF), pltpu.VMEM((PREV, D), BF), pltpu.SemaphoreType.DMA((9,))]
    return pl.pallas_call(
        functools.partial(adam_kernel, direct),
        out_shape=out_shape, in_specs=in_specs + [VM] * 15, out_specs=out_specs, scratch_shapes=scratch,
        compiler_params=pltpu.CompilerParams(vmem_limit_bytes=VMEM_LIMIT),
        name="optimizer",
    )(*args, *states)


def body(
    tokens, cotangent, documents, w_qkv, w_out, w_fc, w_proj, vectors,
    first_qkv, first_out, first_fc, first_proj, first_vec,
    second_qkv, second_out, second_fc, second_proj, second_vec,
):
    n_dp = lax.axis_size("dp")
    n_t = lax.axis_size("tensor")
    own = tokens.shape[0] // n_t
    rows = D // n_dp
    d = lax.axis_index("dp")
    direct = rows % 16 == 0
    kernel_dp = n_dp if direct else 0
    blk = pack_blocks(w_qkv, w_out, w_fc, w_proj)
    gcol, grow = doc_inputs(documents, own)
    if direct:
        w_in = blk
        vec_in = jnp.pad(vectors.astype(BF), ((0, 4), (0, LANES - rows)))
    else:
        w_in = lax.all_gather(blk, ("dp", "tensor"), axis=0).reshape(n_dp, n_t, 3, rows, D)
        w_in = w_in.transpose(2, 1, 0, 3, 4).reshape(3, n_t, D, D)
        vec_in = jnp.pad(lax.all_gather(vectors.astype(BF), "dp", axis=1, tiled=True).astype(F32), ((0, 4), (0, 0)))
    w_full, vec, *saved, own_out = forward(kernel_dp, w_in, vec_in, tokens, gcol, grow, own)
    if not direct:
        w_full = w_in
    grads = backward(kernel_dp, w_full, vec, tokens, cotangent, saved, own_out, own)
    if direct:
        fin, vgrad, squares, own_grads, prev, all_out = grads
        moved = (own_grads, prev, all_out)
    else:
        tiles, vgrad, own_grad, prev = grads
        output = lax.all_gather(own_out, "tensor", axis=0, tiled=True)
        whole = lax.all_gather(own_grad, "tensor", axis=0, tiled=True).astype(F32)
        prevs = lax.all_gather(prev, "tensor", axis=0).astype(F32)
        for k in range(1, n_t):
            whole = whole.at[k * own - PREV : k * own].add(prevs[k])
        input_grad = whole.astype(BF)
        fin = tiles.reshape(3, n_t, n_dp, rows, D).transpose(2, 1, 0, 3, 4).reshape(-1, D)
        fin = lax.psum_scatter(fin, ("dp", "tensor"), scatter_dimension=0, tiled=True)
        fin = fin.reshape(3, rows, D).astype(F32)
        vgrad = lax.psum(vgrad, ("dp", "tensor"))
        squares = lax.psum(jnp.sum(fin * fin), ("dp", "tensor"))
        squares = jnp.pad(squares.reshape(1, 1), ((0, 7), (0, LANES - 1)))
        moved = None
    g_vec = lax.dynamic_slice_in_dim(vgrad[0:12], d * rows, rows, 1)
    states = []
    for qkv, out, fc, proj, vec in (
        (w_qkv, w_out, w_fc, w_proj, vectors),
        (first_qkv, first_out, first_fc, first_proj, first_vec),
        (second_qkv, second_out, second_fc, second_proj, second_vec),
    ):
        states += [qkv.transpose(1, 0, 2), out, fc, proj.T, vec]
    outs = optimizer(squares, vgrad, fin, g_vec, moved, states)
    if direct:
        output, input_grad, *outs = outs
    norm, *states = outs
    for k in (0, 5, 10):
        states[k] = states[k].transpose(1, 0, 2)
        states[k + 3] = states[k + 3].T
    return (output, input_grad, norm[0, 0], *states)


def solution(mesh):
    rows = P("dp", None)
    weights = (P("dp", None, "tensor"), P("tensor", "dp"), P("dp", "tensor"), P("tensor", "dp"), P(None, "dp"))
    return jax.shard_map(
        body, mesh=mesh, in_specs=(rows, rows, rows) + weights * 3,
        out_specs=(rows, rows, P()) + weights * 3, check_vma=False,
    )
```

```python
import functools
import math

import jax
import jax.numpy as jnp
from jax import lax
from jax.experimental import pallas as pl
from jax.experimental.pallas import tpu as pltpu
from jax.sharding import PartitionSpec as P

D = 768
HD = 64
FF = 3072
STEP = 10
PREV = 512
BLK = 256
LANES = 128
PARTS = 4

beta_one = 0.9
beta_two = 0.999
rate_qkv = 0.03
rate_out = 0.08
rate_fc = 0.03
rate_proj = 0.02
rate_vec = 0.6
decay_rate = 0.01
epsilon = 1e-08
max_norm = 1.0

BF = jnp.bfloat16
F32 = jnp.float32
VMEM_LIMIT = 62 * 2**20
ANY = pl.BlockSpec(memory_space=pl.ANY)
VM = pl.BlockSpec(memory_space=pltpu.VMEM)
GELU_C = math.sqrt(2.0 / math.pi)


def nn(a, b):
    return lax.dot_general(a, b, (((1,), (0,)), ((), ())), preferred_element_type=F32)


def nt(a, b):
    return lax.dot_general(a, b, (((1,), (1,)), ((), ())), preferred_element_type=F32)


MESH = pl.DeviceIdType.MESH


def wait_bytes(ref, sem):
    pltpu.make_async_copy(ref, ref, sem).wait()


def positions():
    d, t = lax.axis_index("dp"), lax.axis_index("tensor")
    return d, t, lax.rem(d, 2), d // 2, t // 2, lax.rem(t, 2)


GATHER = (
    {6: [("after_last", 0), ("spread", 1)]},
    {5: [("after_first", 1)]},
    {3: [("after_x1", 1)]},
    {3: [("after_last", 1), ("last",)]},
)


class Gather:
    Z, X0, Y1, Y0, X1, X1U, C, CU = range(8)

    def __init__(self, n_dp, blk, vecb, w, vecg, send, recv, loc, vsend, vrecv):
        self.n_dp, self.blk, self.vecb, self.w, self.vecg = n_dp, blk, vecb, w, vecg
        self.send, self.recv, self.loc, self.vsend, self.vrecv = send, recv, loc, vsend, vrecv
        self.rows = blk.shape[1]
        self.nz = n_dp // 2
        self.d, self.t, self.x, self.z, self.y, self.c = positions()
        self.to_x = (self.d + 1 - 2 * self.x, self.t)
        self.to_y = (self.d, self.t + 2 - 4 * self.y)
        self.to_c = (self.d, self.t + 1 - 2 * self.c)
        self.u = self.t + 2 - 4 * self.y
        self.half = D // 2

    def dp_peers(self):
        return [(lax.rem(self.d + k, self.n_dp), self.t) for k in range(1, self.n_dp)]

    def at(self, m, t, block, lanes):
        return self.w.at[m, t, pl.ds(pl.multiple_of(block * self.rows, self.rows), self.rows), lanes]

    def copy(self, m, stage, src, dst, dev):
        pltpu.make_async_remote_copy(
            src_ref=src, dst_ref=dst, send_sem=self.send.at[m, stage], recv_sem=self.recv.at[m, stage],
            device_id=dev, device_id_type=MESH,
        ).start()

    def size(self, m, stage):
        if m == 2 and stage in (self.X0, self.Y1):
            return self.w.at[m, 0, pl.ds(0, self.rows), pl.ds(0, self.half)]
        if m == 2 and stage == self.Z:
            return self.w.at[m, 0, pl.ds(0, (self.nz - 1) * 2 * self.rows)]
        rows = (self.nz - 1) * self.rows if stage == self.Z else self.nz * self.rows
        if stage in (self.Y0, self.C, self.CU):
            rows = D
        lanes = self.half if stage in (self.X0, self.Y1, self.Y0, self.X1, self.X1U) else D
        return self.w.at[m, 0, pl.ds(0, rows), pl.ds(0, lanes)]

    def got(self, m, stage):
        wait_bytes(self.size(m, stage), self.recv.at[m, stage])

    def greet(self):
        for dev in self.dp_peers() + [self.to_y, self.to_c]:
            pl.semaphore_signal(pltpu.get_barrier_semaphore(), inc=1, device_id=dev, device_id_type=MESH)

    def begin(self):
        for m in range(3):
            pltpu.make_async_copy(self.blk.at[m], self.at(m, self.t, self.d, pl.ds(0, D)), self.loc.at[m]).start()
        pl.semaphore_wait(pltpu.get_barrier_semaphore(), self.n_dp + 1)
        for dev in self.dp_peers():
            pltpu.make_async_remote_copy(
                src_ref=self.vecb, dst_ref=self.vecg.at[self.d], send_sem=self.vsend, recv_sem=self.vrecv,
                device_id=dev, device_id_type=MESH,
            ).start()
        self.vecg[self.d] = self.vecb[...]
        self.along_z(0)
        own = self.blk.at[2]
        for stage, lanes, dev in (
            (self.X0, pl.ds(0, self.half), self.to_x), (self.Y1, pl.ds(self.half, self.half), self.to_y)
        ):
            self.copy(2, stage, own.at[:, lanes], self.at(2, self.t, self.d, lanes), dev)

    def middle(self):
        self.got(2, self.X0)
        self.got(2, self.Y1)
        wait_bytes(self.blk.at[2], self.loc.at[2])
        low, high = pl.ds(0, self.half), pl.ds(self.half, self.half)
        pair = pl.ds(pl.multiple_of(self.z * 2 * self.rows, 2 * self.rows), 2 * self.rows)
        for k in range(1, self.nz):
            dev = (lax.rem(self.d + 2 * k, self.n_dp), self.t)
            for ref in (
                self.w.at[2, self.t, pair, low], self.at(2, self.t, self.d, high), self.at(2, self.u, self.d, high)
            ):
                self.copy(2, self.Z, ref, ref, dev)

    def last(self):
        self.got(2, self.Z)
        ref = self.w.at[2, self.t, :, pl.ds(0, self.half)]
        self.copy(2, self.Y0, ref, ref, self.to_y)
        high = pl.ds(self.half, self.half)
        self.columns(2, self.X1, self.t, high, self.to_x)
        self.columns(2, self.X1U, self.u, high, self.to_x)

    def vectors(self):
        wait_bytes(self.vecg.at[pl.ds(0, self.n_dp - 1)], self.vrecv)
        width = D // self.n_dp
        lane = lax.broadcasted_iota(jnp.int32, (LANES, D), 0)
        col = lax.broadcasted_iota(jnp.int32, (LANES, D), 1)
        total = jnp.zeros((16, D), F32)
        for p in range(self.n_dp):
            pick = jnp.where((col == lane + p * width) & (lane < width), 1.0, 0.0).astype(BF)
            total += nn(self.vecg[p], pick)
        return total

    def along_z(self, m):
        for k in range(1, self.nz):
            dev = (lax.rem(self.d + 2 * k, self.n_dp), self.t)
            self.copy(m, self.Z, self.blk.at[m], self.at(m, self.t, self.d, pl.ds(0, D)), dev)

    def columns(self, m, stage, t, lanes, dev):
        for zz in range(self.nz):
            ref = self.at(m, t, 2 * zz + self.x, lanes)
            self.copy(m, stage, ref, ref, dev)

    def got_z(self, m):
        self.got(m, self.Z)
        wait_bytes(self.blk.at[m], self.loc.at[m])

    def spread(self, m):
        low, high = pl.ds(0, self.half), pl.ds(self.half, self.half)
        self.columns(m, self.Y1, self.t, high, self.to_y)
        self.columns(m, self.X0, self.t, low, self.to_x)

    def after_first(self, m):
        self.got(m, self.X0)
        ref = self.w.at[m, self.t, :, pl.ds(0, self.half)]
        self.copy(m, self.Y0, ref, ref, self.to_y)
        high = pl.ds(self.half, self.half)
        self.columns(m, self.X1, self.t, high, self.to_x)
        self.got(m, self.Y1)
        self.columns(m, self.X1U, self.u, high, self.to_x)

    def after_x1(self, m):
        self.got(m, self.X1)
        ref = self.w.at[m, self.t]
        self.copy(m, self.C, ref, ref, self.to_c)

    def after_last(self, m):
        self.got(m, self.Y0)
        self.got(m, self.X1U)
        ref = self.w.at[m, self.u]
        self.copy(m, self.CU, ref, ref, self.to_c)

    def finish(self):
        for m in range(3):
            for stage in range(8):
                wait_bytes(self.size(m, stage), self.send.at[m, stage])
        wait_bytes(self.vecg.at[pl.ds(0, self.n_dp - 1)], self.vsend)


def ln_parts(x):
    mean = jnp.mean(x, -1, keepdims=True)
    centred = x - mean
    inv = lax.rsqrt(jnp.mean(centred * centred, -1, keepdims=True) + 1e-05)
    return centred * inv, inv


def ln_back(e, u, inv):
    return inv * (
        e - jnp.mean(e, -1, keepdims=True) - u * jnp.mean(e * u, -1, keepdims=True)
    )


def group_tiles(rows, group):
    base = (group // 2) * 384
    low = lax.broadcasted_iota(jnp.int32, (rows.shape[0], LANES), 1) < HD
    first = rows[:, base : base + 128]
    second = rows[:, base + 128 : base + 256]
    third = rows[:, base + 256 : base + 384]
    if group % 2 == 0:
        return first, second
    second, third = pltpu.roll(second, HD, 1), pltpu.roll(third, HD, 1)
    return jnp.where(low, second, third), third


def ungroup_tiles(even, odd):
    low = lax.broadcasted_iota(jnp.int32, even[0].shape, 1) < HD
    pair = pltpu.roll(odd[0], HD, 1)
    single = pltpu.roll(odd[1], HD, 1)
    return even[0], jnp.where(low, even[1], pair), jnp.where(low, pair, single)


def pack(blk, vecb, wide, w_qkv, w_out, w_fc, w_proj, vectors):
    out = w_out[...].T
    for k in range(3):
        blk[0, :, 128 * k : 128 * k + 128] = w_qkv[k, :, 0:128].astype(BF)
    blk[0, :, 384:512] = out[:, 0:128].astype(BF)
    for k, pair in enumerate(((w_qkv[0, :, 128:192], w_qkv[1, :, 128:192]), (w_qkv[2, :, 128:192], out[:, 128:192]))):
        blk[0, :, 512 + 128 * k : 640 + 128 * k] = jnp.concatenate(pair, 1).astype(BF)
    blk[1] = w_fc[...].astype(BF)
    blk[2] = w_proj[...].astype(BF)
    wide[...] = jnp.zeros_like(wide)
    wide[0 : vectors.shape[0], 0 : vectors.shape[1]] = vectors[...]
    vecb[...] = wide[...].astype(BF)


def fwd_kernel(
    n_dp, n_in, *refs,
):
    ins, refs = refs[:n_in], refs[n_in:]
    tok_hbm, docs = ins[-2:]
    fwd_body(n_dp, ins[:-2], tok_hbm, docs, *refs)


def fwd_body(
    n_dp, weights, tok_hbm, docs,
    w_hbm, vec_out, nrm_out, q_out, v_out, kT_out, ctx_out, mid_out, n2_out, act_out, slope_out, probs_out, inv_out, invT_out, out_out,
    xw, nrm, wa, wf, wp, qm, kt, vt, ktT, vtT, ctxT, ctx, mb, mid, n2, acc, act, slope, pst, vec_ref, sc, inv, invT, bias,
    in_sem, w_sem, out_sem, p_sem, *gather_refs,
):
    gather = None
    if n_dp:
        blk, vecb, wide, *gather_refs = gather_refs
        gather = Gather(n_dp, blk, vecb, w_hbm, *gather_refs)
        gather.greet()
        pack(blk, vecb, wide, *weights)
        gather.begin()
    else:
        w_hbm, vec_in = weights
    rank = lax.axis_index("tensor")
    own = xw.shape[0] - PREV
    start = jnp.maximum(rank * own - PREV, 0)
    cp_prev = pltpu.make_async_copy(tok_hbm.at[pl.ds(pl.multiple_of(start, 256), PREV)], xw.at[pl.ds(0, PREV)], in_sem.at[0])
    cp_own = pltpu.make_async_copy(tok_hbm.at[pl.ds(pl.multiple_of(rank * own, 256), own)], xw.at[pl.ds(PREV, own)], in_sem.at[1])
    cp_prev.start()
    cp_own.start()
    outs = []
    groups = [rank, rank + 1 - 2 * lax.rem(rank, 2)]
    groups += [lax.rem(k + 2, 4) for k in groups]

    def load(m, k, dst):
        g = groups[k]
        cp = pltpu.make_async_copy(w_hbm.at[m, g], dst.at[g], w_sem.at[m, k])
        cp.start()
        return cp

    def put(src, dst):
        cp = pltpu.make_async_copy(src, dst, out_sem.at[len(outs)])
        cp.start()
        outs.append(cp)

    per_row = docs.shape[1] // BLK

    def doc_block(k):
        index = rank * (own // BLK) - PREV // BLK + k
        safe = jnp.maximum(index, 0)
        row = safe // per_row
        col = pl.multiple_of(lax.rem(safe, per_row) * BLK, BLK)
        ids = (docs[pl.ds(row, 1), pl.ds(col, BLK)] + 8 * row).astype(F32)
        return jnp.where(index < 0, -1.0, ids)

    for k in range(5):
        keys = jnp.broadcast_to(doc_block(k), (BLK, BLK)).T
        for i in range(max(0, k - 2), min(2, k) + 1):
            same = keys == doc_block(2 + i)
            key_at = lax.broadcasted_iota(jnp.int32, (BLK, BLK), 0) + (k - i) * BLK
            query_at = lax.broadcasted_iota(jnp.int32, (BLK, BLK), 1) + PREV
            mb[i, (k - i) * BLK : (k - i + 1) * BLK, :] = jnp.where(same & (key_at <= query_at), 0.0, -1e30).astype(F32)
    cp_prev.wait()
    cp_own.wait()
    vec = gather.vectors() if gather else vec_in[...]
    vec_ref[...] = vec
    put(vec_ref, vec_out)

    def ln_one(r, _):
        rows = pl.ds(pl.multiple_of(r * 128, 128), 128)
        u, _inv = ln_parts(xw[rows, :].astype(F32))
        nrm[rows, :] = (u * vec[0:1] + vec[1:2]).astype(BF)
        return 0

    lax.fori_loop(0, xw.shape[0] // 128, ln_one, 0)
    put(nrm, nrm_out)
    for g in range(4):
        pair, single = group_tiles(vec[0:8], g)
        bias[g, :, 0:128] = pair
        bias[g, :, 128:256] = single
        ctxT[2 * g + 1, 0:HD, :] = jnp.zeros((HD, own), BF)
    if gather:
        gather.got_z(0)
        gather.spread(0)
        gather.along_z(1)
        gather.after_first(0)
        gather.after_x1(0)
    low = lax.broadcasted_iota(jnp.int32, (BLK, LANES), 1) < HD

    def project(k):
        g = groups[k]
        bq_pair, bq_single = bias[g, 2:3, 0:128], bias[g, 2:3, 128:256]
        bv_pair, bv_single = bias[g, 3:4, 0:128], bias[g, 3:4, 128:256]

        def qkv(rc, _):
            rows = pl.ds(pl.multiple_of(rc * BLK, BLK), BLK)
            x = nrm[rows, :]
            one = nn(x, wa[g, :, 0:384])
            two = nn(x, wa[g, :, 512:768])
            k_pair = one[:, 128:256].astype(BF)
            v_pair = (one[:, 256:384] + bv_pair).astype(BF)
            kt[2 * g, rows, :] = k_pair
            vt[2 * g, rows, :] = v_pair
            ktT[2 * g, :, rows] = k_pair.T
            vtT[2 * g, :, rows] = v_pair.T
            qk, vo = two[:, 0:128], two[:, 128:256]
            k_single = jnp.where(low, pltpu.roll(qk, HD, 1), 0.0).astype(BF)
            v_single = jnp.where(low, vo + bv_single, 0.0)
            kt[2 * g + 1, rows, :] = k_single
            vt[2 * g + 1, rows, :] = pltpu.roll(v_single, HD, 1).astype(BF)
            ktT[2 * g + 1, :, rows] = k_single.T
            vtT[2 * g + 1, :, rows] = v_single.astype(BF).T

            @pl.when(rc >= PREV // BLK)
            def _():
                orows = pl.ds(pl.multiple_of(rc * BLK - PREV, BLK), BLK)
                q_pair = (one[:, 0:128] + bq_pair).astype(BF).astype(F32) * 0.125
                q_single = (qk + bq_single).astype(BF).astype(F32) * 0.125
                qm[3 * g, orows, :] = jnp.where(low, q_pair, 0.0).astype(BF)
                qm[3 * g + 1, orows, :] = jnp.where(low, 0.0, q_pair).astype(BF)
                qm[3 * g + 2, orows, :] = jnp.where(low, q_single, 0.0).astype(BF)

            return 0

        lax.fori_loop(0, nrm.shape[0] // BLK, qkv, 0)

    def probs_put(h, slot):
        return [
            pltpu.make_async_copy(
                pst.at[slot, i], probs_out.at[h, pl.ds(i * BLK, 3 * BLK), pl.ds(i * BLK, BLK)], p_sem.at[slot]
            )
            for i in range(3)
        ]

    def attend(g, k, pump):
        if k:
            for hh in range(3):
                wait_bytes(pst.at[hh], p_sem.at[hh])

        def score(n):
            hh, i = divmod(n, 3)
            keys = kt[2 * g + hh // 2, pl.ds(i * BLK, 3 * BLK), :]
            sc[i] = nt(keys, qm[3 * g + hh, pl.ds(i * BLK, BLK), :]) + mb[i]

        def soft(n):
            hh, i = divmod(n, 3)
            top = jnp.full((8, BLK), -1e30, F32)
            for c in range(0, 3 * BLK, 128):
                top = jnp.maximum(top, jnp.max(sc[i, c : c + 128, :].reshape(16, 8, BLK), 0))
            top = jnp.max(top, 0, keepdims=True)
            total = jnp.zeros((8, BLK), F32)
            for c in range(0, 3 * BLK, 128):
                p = jnp.exp(sc[i, c : c + 128, :] - top)
                total += jnp.sum(p.reshape(16, 8, BLK), 0)
                pst[hh, i, c : c + 128, :] = p.astype(BF)
            inv[pl.ds(3 * g + hh, 1), pl.ds(i * BLK, BLK)] = 1.0 / jnp.sum(total, 0, keepdims=True)

        def value(n):
            hh, i = divmod(n, 3)
            mine = pl.ds(i * BLK, BLK)
            tile, src, dst = 2 * g + hh // 2, HD * (hh == 1), HD * (hh != 0)
            o = nn(vtT[tile, src : src + HD, pl.ds(i * BLK, 3 * BLK)], pst[hh, i])
            ctxT[tile, dst : dst + HD, mine] = (o * inv[pl.ds(3 * g + hh, 1), mine]).astype(BF)
            if i == 2:
                for cp in probs_put(3 * g + hh, hh):
                    cp.start()

        score(0)
        for n in range(9):
            if gather:
                for name, *args in pump.get(n, ()):
                    getattr(gather, name)(*args)
            if n < 8:
                score(n + 1)
            soft(n)
            if n:
                value(n - 1)
        value(8)

    for k in range(4):
        if gather and k == 1:
            gather.got(0, gather.C)
        if gather and k == 3:
            gather.got(0, gather.CU)
        load(0, k, wa).wait()
        project(k)
        if gather and k == 0:
            gather.got_z(1)
            gather.middle()
        attend(groups[k], k, GATHER[k])
    put(qm, q_out)
    put(vt, v_out)
    put(ktT, kT_out)
    for t in range(8):
        ctx[t] = ctxT[t].T
    put(ctx, ctx_out)
    inv[12:, :] = jnp.zeros((LANES - 12, own), F32)
    invT[...] = inv[...].T
    put(inv.at[pl.ds(0, 16)], inv_out)
    put(invT, invT_out)

    def out_proj(rc, _):
        rows = pl.ds(pl.multiple_of(rc * BLK, BLK), BLK)
        total = xw[pl.ds(pl.multiple_of(rc * BLK + PREV, BLK), BLK), :].astype(F32) + vec[4:5]
        for g in range(4):
            total += nt(ctx[2 * g, rows, :], wa[g, :, 384:512])
            total += nt(ctx[2 * g + 1, rows, :], wa[g, :, 640:768])
        mid[rows, :] = total
        u, _inv = ln_parts(total)
        n2[rows, :] = (u * vec[5:6] + vec[6:7]).astype(BF)
        acc[rows, :] = total + vec[7:8]
        return 0

    lax.fori_loop(0, own // BLK, out_proj, 0)
    put(mid, mid_out)
    put(n2, n2_out)
    if gather:
        gather.got(1, gather.C)
        gather.got(1, gather.CU)
    fc_loads = [load(1, k, wf) for k in range(4)]
    proj_loads = [] if gather else [load(2, k, wp) for k in range(4)]
    for k in range(4):
        t = groups[k]
        fc_loads[k].wait()
        fc_bias = vec_ref[pl.ds(8 + t, 1), :]

        def mlp(rc, _):
            rows = pl.ds(pl.multiple_of(rc * BLK, BLK), BLK)
            z = nn(n2[rows, :], wf[t]) + fc_bias
            th = jnp.tanh(GELU_C * (z + 0.044715 * z * z * z))
            half = 0.5 * (1.0 + th)
            act[t, rows, :] = (z * half).astype(BF)
            slope[t, rows, :] = (
                half + 0.5 * z * (1.0 - th * th) * (GELU_C * (1.0 + 3 * 0.044715 * z * z))
            ).astype(BF)
            return 0

        lax.fori_loop(0, own // BLK, mlp, 0)
        put(act.at[t], act_out.at[t])
        put(slope.at[t], slope_out.at[t])
        if gather and k == 0:
            gather.after_x1(2)
            proj_loads.append(load(2, 0, wp))
    if gather:
        gather.after_last(2)
        proj_loads.append(load(2, 2, wp))
        gather.got(2, gather.C)
        proj_loads.append(load(2, 1, wp))
        gather.got(2, gather.CU)
        proj_loads.append(load(2, 3, wp))
    for k in (0, 2, 1, 3):
        t = groups[k]
        proj_loads[(0, 2, 1, 3).index(k)].wait()

        def mlp_out(rc, _):
            rows = pl.ds(pl.multiple_of(rc * BLK, BLK), BLK)
            acc[rows, :] += nt(act[t, rows, :], wp[t])
            return 0

        lax.fori_loop(0, own // BLK, mlp_out, 0)
    xw[0:own, :] = acc[...].astype(BF)
    put(xw.at[pl.ds(0, own)], out_out)
    for hh in range(3):
        wait_bytes(pst.at[hh], p_sem.at[hh])
    for cp in outs:
        cp.wait()
    if gather:
        gather.finish()


def forward(n_dp, weights, tokens, documents, own):
    win = own + PREV
    sds = jax.ShapeDtypeStruct
    out_shape = [
        sds((3, 4, D, D) if n_dp else (8, LANES), BF),
        sds((16, D), F32), sds((win, D), BF), sds((12, own, LANES), BF), sds((8, win, LANES), BF),
        sds((8, LANES, win), BF), sds((8, own, LANES), BF), sds((own, D), F32), sds((own, D), BF),
        sds((4, own, D), BF), sds((4, own, D), BF), sds((12, win, own), BF), sds((16, own), F32), sds((own, LANES), F32), sds((own, D), BF),
    ]
    scratch = [
        pltpu.VMEM((win, D), BF), pltpu.VMEM((win, D), BF),
        pltpu.VMEM((4, D, D), BF), pltpu.VMEM((4, D, D), BF), pltpu.VMEM((4, D, D), BF),
        pltpu.VMEM((12, own, LANES), BF), pltpu.VMEM((8, win, LANES), BF), pltpu.VMEM((8, win, LANES), BF),
        pltpu.VMEM((8, LANES, win), BF), pltpu.VMEM((8, LANES, win), BF),
        pltpu.VMEM((8, LANES, own), BF), pltpu.VMEM((8, own, LANES), BF),
        pltpu.VMEM((3, 3 * BLK, BLK), F32), pltpu.VMEM((own, D), F32), pltpu.VMEM((own, D), BF),
        pltpu.VMEM((own, D), F32), pltpu.VMEM((4, own, D), BF), pltpu.VMEM((4, own, D), BF),
        pltpu.VMEM((3, 3, 3 * BLK, BLK), BF), pltpu.VMEM((16, D), F32),
        pltpu.VMEM((3, 3 * BLK, BLK), F32), pltpu.VMEM((LANES, own), F32), pltpu.VMEM((own, LANES), F32),
        pltpu.VMEM((4, 8, 256), F32),
        pltpu.SemaphoreType.DMA((2,)), pltpu.SemaphoreType.DMA((3, 4)), pltpu.SemaphoreType.DMA((24,)),
        pltpu.SemaphoreType.DMA((3,)),
    ]
    params = {}
    if n_dp:
        scratch += [
            pltpu.VMEM((3, D // n_dp, D), BF), pltpu.VMEM((16, LANES), BF), pltpu.VMEM((16, LANES), F32),
            pltpu.VMEM((n_dp, 16, LANES), BF), pltpu.SemaphoreType.DMA((3, 8)), pltpu.SemaphoreType.DMA((3, 8)),
            pltpu.SemaphoreType.DMA((3,)), pltpu.SemaphoreType.DMA, pltpu.SemaphoreType.DMA,
        ]
        params = dict(collective_id=1, has_side_effects=True)
    return pl.pallas_call(
        functools.partial(fwd_kernel, n_dp, len(weights) + 2),
        out_shape=out_shape,
        in_specs=([VM] * 5 if n_dp else [ANY, VM]) + [ANY, VM],
        out_specs=[ANY] * len(out_shape),
        scratch_shapes=scratch,
        compiler_params=pltpu.CompilerParams(vmem_limit_bytes=VMEM_LIMIT, **params),
        name="forward",
    )(*weights, tokens, documents)


def pack_blocks(w_qkv, w_out, w_fc, w_proj):
    q, k, v, o = w_qkv[:, 0], w_qkv[:, 1], w_qkv[:, 2], w_out.T
    pairs = [a[:, :128] for a in (q, k, v, o)]
    singles = [a[:, 128:] for a in (q, k, v, o)]
    return jnp.stack([jnp.concatenate(pairs + singles, 1), w_fc, w_proj.T]).astype(BF)


SCHEDULE = {
    ("p", 1): [("along_x", 0)],
    ("f", 1): [("after_x", 0), ("along_x", 1)],
    "start": [("forward",), ("after_x", 1), ("along_x", 2), ("after_z", 0)],
    ("h", 0): [],
    ("a", 0): [("after_x", 2), ("along_x", 3), ("after_z", 1)],
    ("a", 1): [],
    ("h", 2): [("after_x", 3), ("along_x", 4), ("after_z", 2)],
    ("h", 3): [("after_x", 4), ("after_z", 3)],
    ("w", 3): [("along_x", 5)],
    "end": [("after_z", 4), ("after_x", 5)],
}


class Reduce:
    def __init__(self, n_dp, sb, rc, su, rx, rz, ry, ys, fin, sems):
        self.n_dp, self.nz, self.rows = n_dp, n_dp // 2, D // n_dp
        self.sb, self.rc, self.su, self.rx, self.rz, self.ry, self.ys, self.fin = sb, rc, su, rx, rz, ry, ys, fin
        self.cs, self.cr, self.xs, self.xr, self.zs, self.zr, self.ysem, self.yr = sems
        self.d, self.t, self.x, self.z, self.y, self.c = positions()
        self.to_x = (self.d + 1 - 2 * self.x, self.t)
        self.to_y = (self.d, self.t + 2 - 4 * self.y)
        self.to_c = (self.d, self.t + 1 - 2 * self.c)

    def block(self, ref, index):
        return ref.at[pl.ds(pl.multiple_of(index * self.rows, self.rows), self.rows)]

    def send(self, src, dst, ssem, rsem, dev):
        pltpu.make_async_remote_copy(
            src_ref=src, dst_ref=dst, send_sem=ssem, recv_sem=rsem, device_id=dev, device_id_type=MESH
        ).start()

    def to_core(self, u):
        self.send(self.sb.at[u % 2], self.rc.at[u], self.cs.at[u], self.cr.at[u], self.to_c)

    def core_sent(self, u):
        wait_bytes(self.sb.at[u % 2], self.cs.at[u])

    def core_got(self, u):
        wait_bytes(self.rc.at[u], self.cr.at[u])

    def slot(self, u):
        return u % 4

    def along_x(self, u):
        for k in range(1, self.nz + 1):
            zz = lax.rem(self.z + k, self.nz)
            src = self.block(self.su.at[self.slot(u)], 2 * zz + 1 - self.x)
            sem = self.xr.at[u + k] if u == 5 else self.xr.at[u]
            self.send(src, self.block(self.rx.at[u], zz), self.xs.at[u], sem, self.to_x)

    def after_x(self, u):
        if u < 5:
            wait_bytes(self.rx.at[u], self.xr.at[u])
        tile = self.su.at[self.slot(u)]
        for k in range(1, self.nz + 1):
            zz = lax.rem(self.z + k, self.nz)
            got = self.block(self.rx.at[u], zz)
            if u == 5:
                wait_bytes(got, self.xr.at[u + k])
            mine = self.block(tile, 2 * zz + self.x)
            mine[...] = (mine[...].astype(F32) + got[...].astype(F32)).astype(BF)
            if k < self.nz:
                dev = (2 * zz + self.x, self.t)
                self.send(mine, self.rz.at[u, k - 1], self.zs.at[u], self.zr.at[u], dev)

    def after_z(self, u):
        m, yy = 2 - u // 2, u % 2
        wait_bytes(self.rz.at[u], self.zr.at[u])
        total = self.block(self.su.at[self.slot(u)], 2 * self.z + self.x)[...].astype(F32)
        for k in range(self.nz - 1):
            total += self.rz[u, k].astype(F32)

        @pl.when(self.y == yy)
        def _():
            self.fin[m] = total

        @pl.when(self.y != yy)
        def _():
            self.ys[m] = total.astype(BF)
            self.send(self.ys.at[m], self.ry.at[m], self.ysem.at[m], self.yr.at[m], self.to_y)

    def sent(self, u):
        wait_bytes(self.rx.at[u], self.xs.at[u])
        wait_bytes(self.rz.at[u], self.zs.at[u])

    def finish(self, m):
        wait_bytes(self.ry.at[m], self.yr.at[m])
        self.fin[m] += self.ry[m].astype(F32)
        wait_bytes(self.ys.at[m], self.ysem.at[m])


def bwd_kernel(
    n_dp, w_hbm, vec_hbm, tok_hbm, cot_hbm, nrm_hbm, q_hbm, v_hbm, kT_hbm, ctx_hbm, mid_hbm, n2_hbm,
    act_hbm, slope_hbm, probs_hbm, inv_hbm, invT_hbm, own_out_hbm,
    *rest,
):
    if n_dp:
        fin_out, vgrad_out, ss_out, igr_out, prev_out, all_out = rest[:6]
        rest = rest[6:]
    else:
        tiles_out, vgrad_out, igr_out, prev_out = rest[:4]
        rest = rest[4:]
    (cot, cotT, shared, gm, w4, pool, gn1, vs, kTs, qs, ctxs, pbuf, gctx, dk, dv, dqT, gj, vec_ref, vg, cs_ref,
     sb, dps, inv, invT, in_sem, tile_sem, ct_sem, p_sem, out_sem) = rest[:29]
    rest = rest[29:]
    n2T, gp, dsT = shared.at[pl.ds(0, D)], shared.at[pl.ds(D, D)], shared.at[pl.ds(0, D + PREV)]
    d, t, x, z, y, c = positions()
    own = cot.shape[0]
    own_rows = pl.ds(pl.multiple_of(t * own, 256), own)
    red = None
    if n_dp:
        (rc, su, rx, rz, ry, ys, fin, comb, vgx, ssx, *sems) = rest
        red = Reduce(n_dp, sb, rc, su, rx, rz, ry, ys, fin, sems[:8])
        o_send, o_recv, v_send, v_recv, s_send, s_recv = sems[8:]
        to_c, to_y = red.to_c, red.to_y
        diag = (d, t + 2 - 4 * y + 1 - 2 * c)
        dp_peers = [(lax.rem(d + k, n_dp), t) for k in range(1, n_dp)]
        barrier = pltpu.get_barrier_semaphore()
        peers = dp_peers + [to_y, to_c, diag]
        for dev in peers:
            pl.semaphore_signal(barrier, inc=1, device_id=dev, device_id_type=MESH)

    def fetch(src, dst, sem):
        cp = pltpu.make_async_copy(src, dst, sem)
        cp.start()
        return cp

    order = [1 - c, c, 3 - c, 2 + c]

    def fetch_tile(j):
        s = j % 2
        return [
            fetch(w_hbm.at[2, order[j]], w4.at[s], tile_sem.at[j, 0]),
            fetch(w_hbm.at[1, order[j]], w4.at[2 + s], tile_sem.at[j, 1]),
        ]

    def fetch_slope(j):
        return fetch(slope_hbm.at[order[j]], pool.at[j], tile_sem.at[j, 3])

    cp_cot = fetch(cot_hbm.at[own_rows], cot, in_sem.at[0])
    acts = [fetch(act_hbm.at[order[j]], pool.at[j], tile_sem.at[j, 2]) for j in range(4)]
    cp_n2 = fetch(n2_hbm, gp, in_sem.at[1])
    tiles = {0: fetch_tile(0), 1: fetch_tile(1)}
    cp_vec = fetch(vec_hbm, vec_ref, in_sem.at[2])
    cp_mid = fetch(mid_hbm, gn1.at[pl.ds(0, own)], in_sem.at[3])
    local_out = []
    if n_dp:
        cp_out = fetch(own_out_hbm, sb.at[1], out_sem.at[0])
        pl.semaphore_wait(barrier, len(peers))
        red.send(own_out_hbm, all_out.at[t], o_send.at[0], o_recv.at[0], to_y)
        red.send(own_out_hbm, all_out.at[t], o_send.at[1], o_recv.at[1], to_c)
        cp_out.wait()
        cp_out = fetch(sb.at[1], all_out.at[t], out_sem.at[0])
    vg[...] = jnp.zeros_like(vg)
    ones = jnp.ones((16, own), BF)
    cp_cot.wait()
    cotT[...] = cot[...].T

    def emit(u, keep, rows, lanes, value):
        if not n_dp or not keep:
            sb[u % 2, rows, lanes] = value.astype(BF)
        else:
            su[red.slot(u), rows, lanes] = (value + rc[u, rows, lanes].astype(F32)).astype(BF)

    def chunk(r, size=BLK):
        return pl.ds(pl.multiple_of(r * size, size), size)

    pending = set()

    def before(u, keep):
        if n_dp:
            if keep:
                red.core_got(u)
                if u >= 4:
                    red.sent(u - 4)
            elif u >= 2:
                red.core_sent(u - 2)
        elif u % 2 in pending:
            wait_bytes(sb.at[u % 2], tile_sem.at[4, u % 2])

    def after(u, keep, m, which):
        if n_dp:
            if not keep:
                red.to_core(u)
        else:
            pending.add(u % 2)
            pltpu.make_async_copy(sb.at[u % 2], tiles_out.at[m, which], tile_sem.at[4, u % 2]).start()

    def pump(point):
        if not n_dp:
            return
        for name, *args in SCHEDULE.get(point, ()):
            if name == "forward":
                wait_bytes(all_out.at[t], o_recv.at[0])
                there = all_out.at[t + 2 - 4 * y]
                red.send(there, there, o_send.at[2], o_recv.at[2], to_c)
            else:
                getattr(red, name)(*args)

    slopes = {}
    for j in (0, 2, 1, 3):
        yy, keep = j // 2, j % 2 == 1
        acts[j].wait()
        if n_dp and j == 2:
            cp_out.wait()
        before(yy, keep)

        def grad_p(r, _):
            emit(yy, keep, chunk(r), slice(None), nn(cotT[chunk(r), :], pool[j]))
            return 0

        lax.fori_loop(0, D // BLK, grad_p, 0)
        after(yy, keep, 2, order[j])
        slopes[j] = fetch_slope(j)
        pump(("p", j))
    cp_n2.wait()
    n2T[...] = gp[...].T
    for j in range(4):
        yy, keep = j // 2, j % 2 == 1
        s = j % 2
        which = order[j]
        u_f = 2 + yy
        for cp in tiles[j] + [slopes[j]]:
            cp.wait()

        def grads(r, _):
            rows = chunk(r)
            ga = nn(cot[rows, :], w4[s]).astype(BF).astype(F32)
            g = (ga * pool[j, rows, :].astype(F32)).astype(BF)
            gp[rows, :] = g
            back = nt(g, w4[2 + s])
            if j == 0:
                gm[rows, :] = back
            else:
                gm[rows, :] += back
            return 0

        lax.fori_loop(0, own // BLK, grads, 0)
        if j < 2:
            tiles[j + 2] = fetch_tile(j + 2)
        vg[pl.ds(8 + which, 1), :] = nn(ones, gp[...])[0:1]
        before(u_f, keep)

        def grad_f(r, _):
            emit(u_f, keep, chunk(r), slice(None), nn(n2T[chunk(r), :], gp[...]))
            return 0

        lax.fori_loop(0, D // BLK, grad_f, 0)
        after(u_f, keep, 1, which)
        pump(("f", j))
    cp_vec.wait()
    cp_mid.wait()
    wa_cps = [fetch(w_hbm.at[0, k], w4.at[k], ct_sem.at[0, k]) for k in range(4)]
    cp_nrm_own = fetch(nrm_hbm.at[pl.ds(PREV, own)], pool.at[0], in_sem.at[1])
    cp_nrm_prev = fetch(nrm_hbm.at[pl.ds(0, PREV)], pool.at[1, pl.ds(0, PREV)], in_sem.at[3])

    def fetch_heads(j):
        s, g = j % 2, order[j]
        return [
            fetch(v_hbm.at[pl.ds(2 * g, 2)], vs.at[s], ct_sem.at[1 + j, 0]),
            fetch(kT_hbm.at[pl.ds(2 * g, 2)], kTs.at[s], ct_sem.at[1 + j, 1]),
            fetch(q_hbm.at[pl.ds(3 * g, 3)], qs.at[s], ct_sem.at[1 + j, 2]),
            fetch(ctx_hbm.at[pl.ds(2 * g, 2)], ctxs.at[s], ct_sem.at[1 + j, 3]),
        ]

    heads = {0: fetch_heads(0), 1: fetch_heads(1)}

    def probs_get(g, hh, slot):
        for i in range(3):
            at = (pl.ds(i * BLK, 3 * BLK), pl.ds(i * BLK, BLK))
            pltpu.make_async_copy(probs_hbm.at[3 * g + hh].at[at], pbuf.at[slot].at[at], p_sem.at[slot]).start()

    probs_get(order[0], 0, 0)
    probs_get(order[0], 1, 1)
    cp_inv = [fetch(inv_hbm, inv, in_sem.at[4]), fetch(invT_hbm, invT, in_sem.at[5])]

    def ln_two(r, sums):
        rows = chunk(r, 128)
        u, inv = ln_parts(gn1[rows, :])
        g = gm[rows, :]
        co = cot[rows, :].astype(F32)
        total = co + ln_back(g * vec_ref[5:6, :], u, inv)
        gm[rows, :] = total
        cot[rows, :] = total.astype(BF)
        new = [jnp.sum(v, 0, keepdims=True) for v in (total, g * u, g, co)]
        return tuple(a + b for a, b in zip(sums, new))

    zero = jnp.zeros((1, D), F32)
    sums = lax.fori_loop(0, own // 128, ln_two, (zero,) * 4)
    for k in range(4):
        vg[4 + k : 5 + k, :] = sums[k]
    gattn, gattnT = cot, cotT
    gattnT[...] = gattn[...].T
    cp_nrm_own.wait()
    cp_nrm_prev.wait()
    nrmT, nrmT_prev = pool.at[2], pool.at[3]
    nrmT[...] = pool[0].T
    nrmT_prev[:, 0:PREV] = pool[1, 0:PREV, :].T
    cp_tok_own = fetch(tok_hbm.at[own_rows], pool.at[0], in_sem.at[0])
    tok_start = pl.multiple_of(jnp.maximum(t * own - PREV, 0), 256)
    cp_tok_prev = fetch(tok_hbm.at[pl.ds(tok_start, PREV)], pool.at[1, pl.ds(0, PREV)], in_sem.at[2])
    for cp in wa_cps + cp_inv:
        cp.wait()
    pump("start")
    win = own + PREV
    low = lax.broadcasted_iota(jnp.int32, (BLK, LANES), 1) < HD
    ones_win = jnp.ones((16, win), BF)
    for j in range(4):
        yy, keep = j // 2, j % 2 == 1
        s, g = j % 2, order[j]
        u = 4 + yy
        for cp in heads[j]:
            cp.wait()

        def grad_ctx(r, _):
            rows = chunk(r)
            both = nn(gattn[rows, :], jnp.concatenate([w4[g, :, 384:512], w4[g, :, 640:768]], 1))
            lane = lax.broadcasted_iota(jnp.int32, (BLK, LANES), 1)
            for hh in range(3):
                scale = jnp.sum(jnp.where(lane == 3 * g + hh, invT[rows, :], 0.0), 1, keepdims=True)
                part = both[:, 128:256] if hh == 2 else both[:, 0:128]
                part = part * scale
                gctx[hh, rows, :] = (jnp.where(low, part, 0.0) if hh == 0 else jnp.where(low, 0.0, part)).astype(BF)
            return 0

        lax.fori_loop(0, own // BLK, grad_ctx, 0)
        dqT[1, HD:, :] = jnp.zeros((HD, own), F32)

        def weigh(n):
            hh, i = divmod(n, 3)
            if i == 0:
                slot = (3 * j + hh) % 2
                wait_bytes(pbuf.at[slot, pl.ds(0, 3 * BLK)], p_sem.at[slot])
            dps[i] = nt(vs[s, hh // 2, pl.ds(i * BLK, 3 * BLK), :], gctx[hh, pl.ds(i * BLK, BLK), :])

        def soft(n):
            hh, i = divmod(n, 3)
            slot = (3 * j + hh) % 2
            mine = pl.ds(i * BLK, BLK)
            centre = jnp.zeros((8, BLK), F32)
            for a in range(0, 3 * BLK, 128):
                p = pbuf[slot, pl.ds(i * BLK + a, 128), mine].astype(F32)
                centre += jnp.sum((p * dps[i, a : a + 128, :]).reshape(16, 8, BLK), 0)
            centre = jnp.sum(centre, 0, keepdims=True) * inv[pl.ds(3 * g + hh, 1), mine]
            for a in range(0, 3 * BLK, 128):
                rows = pl.ds(i * BLK + a, 128)
                p = pbuf[slot, rows, mine].astype(F32)
                dsT[rows, mine] = (p * (dps[i, a : a + 128, :] - centre)).astype(BF)

        def query(n):
            hh, i = divmod(n, 3)
            mine, keys = pl.ds(i * BLK, BLK), pl.ds(i * BLK, 3 * BLK)
            half = HD * (hh == 1)
            dqT[hh // 2, half : half + HD, mine] = nn(kTs[s, hh // 2, half : half + HD, keys], dsT[keys, mine])
            if i < 2:
                return
            slot = (3 * j + hh) % 2
            for b in range(5):
                rows = pl.ds(b * BLK, BLK)
                lo, hi = max(0, b - 2) * BLK, (min(2, b) + 1) * BLK
                one = nn(pbuf[slot, rows, lo:hi], gctx[hh, lo:hi, :])
                two = nn(dsT[rows, lo:hi], qs[s, hh, lo:hi, :])
                if hh == 1:
                    one, two = one + dv[0, rows, :], two + dk[0, rows, :]
                dv[hh // 2, rows, :] = one
                dk[hh // 2, rows, :] = two
            if 3 * j + hh < 10:
                probs_get(order[j + (hh + 2) // 3], (hh + 2) % 3, slot)

        weigh(0)
        for n in range(9):
            if n < 8:
                weigh(n + 1)
            soft(n)
            if n % 3:
                query(n - 1)
            if n % 3 == 2:
                query(n)
        pump(("h", j))
        for r in range(win // BLK):
            rows = pl.ds(r * BLK, BLK)
            k_single = pltpu.roll(dk[1, rows, :], HD, 1)
            if r >= PREV // BLK:
                orows = pl.ds(r * BLK - PREV, BLK)
                gj[rows, 0:128] = (dqT[0, :, orows].T * 0.125).astype(BF)
                k_single += dqT[1, :, orows].T * 0.125
            else:
                gj[rows, 0:128] = jnp.zeros((BLK, LANES), BF)
            gj[rows, 128:256] = dk[0, rows, :].astype(BF)
            gj[rows, 256:384] = dv[0, rows, :].astype(BF)
            gj[rows, 384:512] = k_single.astype(BF)
            gj[rows, 512:640] = pltpu.roll(dv[1, rows, :], HD, 1).astype(BF)
        cs_ref[g] = nn(ones_win, gj[...])[0:8]
        before(u, keep)

        def grad_a(r, _):
            rows = chunk(r)
            a_own, a_prev, b = nrmT[rows, :], nrmT_prev[rows, 0:PREV], gattnT[rows, :]
            emit(u, keep, rows, slice(0, 384), nn(a_own, gj[PREV:, 0:384]) + nn(a_prev, gj[0:PREV, 0:384]))
            emit(u, keep, rows, slice(384, 512), nn(b, ctxs[s, 0]))
            last = nn(a_own, gj[PREV:, 384:640]) + nn(a_prev, gj[0:PREV, 384:640])
            emit(u, keep, rows, slice(512, 640), last[:, 0:128])
            emit(u, keep, rows, slice(640, 768), last[:, 128:256] + nn(b, ctxs[s, 1]))
            return 0

        lax.fori_loop(0, D // BLK, grad_a, 0)
        after(u, keep, 0, g)
        pump(("w", j))

        def grad_n1(r, _):
            rows = chunk(r)
            back = nt(gj[rows, 0:384], w4[g, :, 0:384]) + nt(gj[rows, 384:640], w4[g, :, 512:768])
            if j == 0:
                gn1[rows, :] = back
            else:
                gn1[rows, :] += back
            return 0

        lax.fori_loop(0, win // BLK, grad_n1, 0)
        if j < 2:
            heads[j + 2] = fetch_heads(j + 2)
        pump(("a", j))
    cp_tok_own.wait()
    cp_tok_prev.wait()
    igr, prev = w4.at[0], w4.at[1]

    def ln_one(base, src, tokens, dst, add):
        def step(r, sums):
            rows = chunk(r, 128)
            g = gn1[pl.ds(pl.multiple_of(base + r * 128, 128), 128), :]
            u, inv = ln_parts(tokens[rows, :].astype(F32))
            total = ln_back(g * vec_ref[0:1, :], u, inv)
            if add:
                total += gm[rows, :]
            dst[rows, :] = total.astype(BF)
            return (sums[0] + jnp.sum(g * u, 0, keepdims=True), sums[1] + jnp.sum(g, 0, keepdims=True))

        return lax.fori_loop(0, src // 128, step, (zero, zero))

    sp = ln_one(0, PREV, pool.at[1], prev, False)
    if n_dp:

        @pl.when(c == 1)
        def _():
            red.send(prev.at[pl.ds(0, PREV)], comb, o_send.at[3], o_recv.at[3], to_c)

    so = ln_one(PREV, own, pool.at[0], igr, True)
    vg[0:1, :] = sp[0] + so[0]
    vg[1:2, :] = sp[1] + so[1]
    for g in (0, 2):
        for row, (a, b) in ((2, (0, 384)), (3, (256, 512))):
            even = (cs_ref[g, :, a : a + 128], cs_ref[g, :, b : b + 128])
            odd = (cs_ref[g + 1, :, a : a + 128], cs_ref[g + 1, :, b : b + 128])
            for k, part in enumerate(ungroup_tiles(even, odd)):
                col = (g // 2) * 384 + 128 * k
                vg[row : row + 1, col : col + 128] = part[0:1]
    if not n_dp:
        last = [fetch(igr, igr_out, out_sem.at[0]), fetch(prev.at[pl.ds(0, PREV)], prev_out, out_sem.at[1]),
                fetch(vg, vgrad_out, out_sem.at[2])]
        for cp in last:
            cp.wait()
        for k in range(2):
            wait_bytes(sb.at[k], tile_sem.at[4, k])
        return

    @pl.when(c == 0)
    def _():
        wait_bytes(comb, o_recv.at[3])
        igr[own - PREV :, :] = (igr[own - PREV :, :].astype(F32) + comb[...].astype(F32)).astype(BF)

    @pl.when(c == 1)
    def _():
        wait_bytes(comb, o_send.at[3])

    there = t + 2 - 4 * y
    local_out.append(fetch(igr, igr_out.at[t], out_sem.at[1]))
    part_rows = own // PARTS

    def part(which, q):
        return igr_out.at[which, pl.ds(q * part_rows, part_rows)]

    def across(q):
        red.send(igr.at[pl.ds(q * part_rows, part_rows)], part(t, q), o_send.at[9 + q], o_recv.at[9 + q], to_y)

    def part_sent(q):
        wait_bytes(part(t, q), o_send.at[9 + q])

    def pass_on(q):
        wait_bytes(part(t, q), o_recv.at[9 + q])
        red.send(part(there, q), part(there, q), o_send.at[9 + PARTS + q], o_recv.at[9 + PARTS + q], to_c)

    across(0)
    across(1)
    red.send(igr, igr_out.at[t], o_send.at[5], o_recv.at[5], to_c)
    prev_rows = prev.at[pl.ds(0, PREV)]

    def exchange(buf, own_slot, devs, ssem, rsem):
        for dev in devs:
            red.send(buf.at[own_slot], buf.at[own_slot], ssem, rsem, dev)

    def add_up(buf, count):
        total = buf[0]
        for k in range(1, count):
            total += buf[k]
        return total

    tensor_peers = (to_y, to_c, diag)
    vgx[0, d] = vg[...]
    exchange(vgx.at[0], d, dp_peers, v_send.at[0], v_recv.at[0])
    pump("end")
    wait_bytes(vgx.at[0, pl.ds(0, n_dp - 1)], v_recv.at[0])
    vgx[1, t] = add_up(vgx.at[0], n_dp)
    exchange(vgx.at[1], t, tensor_peers, v_send.at[1], v_recv.at[1])
    part_sent(0)
    across(2)
    red.after_z(5)
    part_sent(1)
    across(3)

    @pl.when(t == 2)
    def _():
        red.send(prev_rows, prev_out, o_send.at[6], o_recv.at[6], to_y)
        red.send(prev_rows, prev_out, o_send.at[7], o_recv.at[7], to_c)
        fetch(prev_rows, prev_out, out_sem.at[2]).wait()

    for m in range(3):
        red.finish(m)
    squares = jnp.zeros((8, LANES), F32)
    for m in range(3):
        sq = fin[m] * fin[m]
        cols = sq[:, 0:LANES]
        for k in range(1, D // LANES):
            cols += sq[:, k * LANES : (k + 1) * LANES]
        squares += jnp.sum(cols.reshape(-1, 8, LANES), 0)
    ssx[0, d] = squares
    exchange(ssx.at[0], d, dp_peers, s_send.at[0], s_recv.at[0])
    fin_cp = fetch(fin, fin_out, in_sem.at[0])
    wait_bytes(ssx.at[0, pl.ds(0, n_dp - 1)], s_recv.at[0])
    ssx[1, t] = add_up(ssx.at[0], n_dp)
    exchange(ssx.at[1], t, tensor_peers, s_send.at[1], s_recv.at[1])
    wait_bytes(vgx.at[1, pl.ds(0, 3)], v_recv.at[1])
    vg[...] = add_up(vgx.at[1], 4)
    vg_cp = fetch(vg, vgrad_out, in_sem.at[1])
    for q in range(PARTS):
        pass_on(q)

    @pl.when(t == 0)
    def _():
        wait_bytes(prev_out, o_recv.at[6])
        red.send(prev_out, prev_out, o_send.at[7], o_recv.at[7], to_c)

    wait_bytes(ssx.at[1, pl.ds(0, 3)], s_recv.at[1])
    part_ref = ssx.at[2, 0]
    part_ref[...] = add_up(ssx.at[1], 4)
    ss_cp = fetch(part_ref, ss_out, in_sem.at[2])
    for k in (1, 2, 5):
        wait_bytes(all_out.at[t], o_recv.at[k])

    @pl.when(c == 1)
    def _():
        wait_bytes(prev_out, o_recv.at[7])

    for k in (0, 1, 2, 5):
        wait_bytes(all_out.at[t], o_send.at[k])
    for q in range(PARTS):
        wait_bytes(part(t, q), o_recv.at[9 + PARTS + q])
        wait_bytes(part(t, q), o_send.at[9 + PARTS + q])
    part_sent(2)
    part_sent(3)

    @pl.when(t == 2)
    def _():
        wait_bytes(prev_out, o_send.at[6])

    @pl.when(c == 0)
    def _():
        wait_bytes(prev_out, o_send.at[7])

    for u in range(2, 6):
        red.sent(u)
    for u in (4, 5):
        red.core_sent(u)
    wait_bytes(vgx.at[0, pl.ds(0, n_dp - 1)], v_send.at[0])
    wait_bytes(vgx.at[1, pl.ds(0, 3)], v_send.at[1])
    wait_bytes(ssx.at[0, pl.ds(0, n_dp - 1)], s_send.at[0])
    wait_bytes(ssx.at[1, pl.ds(0, 3)], s_send.at[1])
    for cp in local_out + [fin_cp, vg_cp, ss_cp]:
        cp.wait()


def backward(n_dp, w_full, vec, tokens, cot, saved, own_out, own):
    nrm, q, v, kT, ctx, mid, n2, act, slope, probs, inv, invT = saved
    win = own + PREV
    sds = jax.ShapeDtypeStruct
    dma = pltpu.SemaphoreType.DMA
    vm = pltpu.VMEM
    scratch = [
        vm((own, D), BF), vm((D, own), BF), vm((D + own, D), BF), vm((own, D), F32),
        vm((4, D, D), BF), vm((4, own, D), BF), vm((win, D), F32),
        vm((2, 2, win, LANES), BF), vm((2, 2, LANES, win), BF), vm((2, 3, own, LANES), BF), vm((2, 2, own, LANES), BF),
        vm((2, win, own), BF), vm((3, own, LANES), BF),
        vm((2, win, LANES), F32), vm((2, win, LANES), F32), vm((2, LANES, own), F32), vm((win, 640), BF),
        vm((16, D), F32), vm((16, D), F32), vm((4, 8, 640), F32), vm((2, D, D), BF),
        vm((3, 3 * BLK, BLK), F32), vm((16, own), F32), vm((own, LANES), F32),
        dma((6,)), dma((5, 4)), dma((5, 4)), dma((2,)), dma((4,)),
    ]
    params = {}
    if n_dp:
        rows = D // n_dp
        out_shape = [
            sds((3, rows, D), F32), sds((16, D), F32), sds((8, LANES), F32),
            sds((4, own, D), BF), sds((PREV, D), BF), sds((4, own, D), BF),
        ]
        scratch += [
            vm((6, D, D), BF), vm((4, D, D), BF), vm((6, D // 2, D), BF), vm((6, n_dp // 2 - 1, rows, D), BF),
            vm((3, rows, D), BF), vm((3, rows, D), BF), vm((3, rows, D), F32), vm((PREV, D), BF),
            vm((2, n_dp, 16, D), F32), vm((3, n_dp, 8, LANES), F32),
            dma((6,)), dma((6,)), dma((6,)), dma((6 + n_dp // 2,)), dma((6,)), dma((6,)), dma((3,)), dma((3,)),
            dma((9 + 2 * PARTS,)), dma((9 + 2 * PARTS,)), dma((2,)), dma((2,)), dma((2,)), dma((2,)),
        ]
        params = dict(collective_id=2, has_side_effects=True)
    else:
        out_shape = [sds((3, 4, D, D), BF), sds((16, D), F32), sds((own, D), BF), sds((PREV, D), BF)]
    return pl.pallas_call(
        functools.partial(bwd_kernel, n_dp),
        out_shape=out_shape,
        in_specs=[ANY] * 17,
        out_specs=[ANY] * len(out_shape),
        scratch_shapes=scratch,
        compiler_params=pltpu.CompilerParams(vmem_limit_bytes=VMEM_LIMIT, **params),
        name="backward",
    )(w_full, vec, tokens, cot, nrm, q, v, kT, ctx, mid, n2, act, slope, probs, inv, invT, own_out)


def adam_step(weight, gradient, first, second, rate, decay):
    first = beta_one * first + (1.0 - beta_one) * gradient
    second = beta_two * second + (1.0 - beta_two) * gradient * gradient
    first_hat = first / (1.0 - beta_one**STEP)
    second_hat = second / (1.0 - beta_two**STEP)
    weight = weight - rate * (first_hat / (jnp.sqrt(second_hat) + epsilon) + decay * weight)
    return (weight, first, second)


def adam_kernel(direct, squares, vgrad, fin, *refs):
    if direct:
        own_grads, prev, all_out = refs[:3]
        refs = refs[3:]
    in_hbm, refs = refs[:15], refs[15:]
    if direct:
        out_ref, igr_ref = refs[:2]
        refs = refs[2:]
    norm_ref, out_hbm, ins, outs, refs = refs[0], refs[1:16], refs[16:31], refs[31:46], refs[46:]
    in_sem, out_sem = refs[:2]
    state_loads = [pltpu.make_async_copy(in_hbm[k], ins[k], in_sem.at[k]) for k in range(15)]
    for cp in state_loads:
        cp.start()
    if direct:
        rows_ref, prev_ref, sem = refs[2:]
        own = all_out.shape[1]
        loads = [pltpu.make_async_copy(own_grads.at[k], rows_ref.at[k], sem.at[k]) for k in range(4)]
        loads += [pltpu.make_async_copy(all_out.at[k], rows_ref.at[4 + k], sem.at[4 + k]) for k in range(4)]
        loads.append(pltpu.make_async_copy(prev, prev_ref, sem.at[8]))
        for k in (8, 0, 1, 2, 3, 4, 5, 6, 7):
            loads[k].start()
        stores = []
        for k in (8, 0, 2, 3, 1, 4, 5, 6, 7):
            loads[k].wait()
            if k == 8:
                continue
            if k == 1:
                tail = pl.ds(own - PREV, PREV)
                rows_ref[1, tail, :] = (rows_ref[1, tail, :].astype(F32) + prev_ref[...].astype(F32)).astype(BF)
            dst = igr_ref if k < 4 else out_ref
            cp = pltpu.make_async_copy(rows_ref.at[k], dst.at[pl.ds(k % 4 * own, own)], sem.at[k])
            cp.start()
            stores.append(cp)
    for cp in state_loads:
        cp.wait()
    vg = vgrad[0:12, :]
    norm = jnp.sqrt(jnp.sum(squares[...], keepdims=True) + jnp.sum(vg * vg, keepdims=True))
    norm_ref[0, 0] = norm[0, 0]
    clip = max_norm / jnp.maximum(norm, max_norm)

    def update(k, at, grad, rate, decay):
        new = adam_step(ins[k][at], grad * clip, ins[5 + k][at], ins[10 + k][at], rate, decay)
        for j in range(3):
            outs[5 * j + k][at] = new[j]

    def single(j):
        tile = fin[0, :, 512 + 128 * (j // 2) : 640 + 128 * (j // 2)]
        return (pltpu.roll(tile, HD, 1) if j % 2 else tile)

    every = slice(None)
    for j in range(3):
        update(0, (j, every, slice(0, 128)), fin[0, :, 128 * j : 128 * j + 128], rate_qkv, decay_rate)
        update(0, (j, every, slice(128, 192)), single(j)[:, 0:HD], rate_qkv, decay_rate)
    update(1, (slice(0, 128), every), fin[0, :, 384:512].T, rate_out, decay_rate)
    update(1, (slice(128, 192), every), single(3).T[0:HD, :], rate_out, decay_rate)
    update(2, (every, every), fin[1], rate_fc, decay_rate)
    update(3, (every, every), fin[2], rate_proj, decay_rate)
    width = fin.shape[1]
    shift = D - lax.axis_index("dp") * width
    update(4, (every, every), pltpu.roll(vgrad[...], shift, 1)[0:12, 0:width], rate_vec, 0.0)
    state_stores = [pltpu.make_async_copy(outs[k], out_hbm[k], out_sem.at[k]) for k in range(15)]
    for cp in state_stores:
        cp.start()
    for cp in state_stores:
        cp.wait()
    if direct:
        for cp in stores:
            cp.wait()


def optimizer(squares, vgrad, fin, moved, states):
    direct = moved is not None
    sds = jax.ShapeDtypeStruct
    dma = pltpu.SemaphoreType.DMA
    out_shape = [sds((1, 1), F32)] + [sds(a.shape, F32) for a in states]
    out_specs = [pl.BlockSpec(memory_space=pltpu.SMEM)] + [ANY] * 15
    in_specs = [VM] * 3
    scratch = [pltpu.VMEM(a.shape, F32) for a in states] * 2 + [dma((15,)), dma((15,))]
    args = (squares, vgrad, fin)
    if direct:
        own = moved[2].shape[1]
        out_shape = [sds((4 * own, D), BF)] * 2 + out_shape
        out_specs = [ANY, ANY] + out_specs
        in_specs += [ANY] * 3
        args += tuple(moved)
        scratch += [pltpu.VMEM((8, own, D), BF), pltpu.VMEM((PREV, D), BF), dma((9,))]
    return pl.pallas_call(
        functools.partial(adam_kernel, direct),
        out_shape=out_shape, in_specs=in_specs + [ANY] * 15, out_specs=out_specs, scratch_shapes=scratch,
        compiler_params=pltpu.CompilerParams(vmem_limit_bytes=VMEM_LIMIT),
        name="optimizer",
    )(*args, *states)


def body(
    tokens, cotangent, documents, w_qkv, w_out, w_fc, w_proj, vectors,
    first_qkv, first_out, first_fc, first_proj, first_vec,
    second_qkv, second_out, second_fc, second_proj, second_vec,
):
    n_dp = lax.axis_size("dp")
    n_t = lax.axis_size("tensor")
    own = tokens.shape[0] // n_t
    rows = D // n_dp
    direct = rows % 16 == 0
    kernel_dp = n_dp if direct else 0
    if direct:
        weights = (w_qkv.transpose(1, 0, 2), w_out, w_fc, w_proj.T, vectors)
    else:
        blk = pack_blocks(w_qkv, w_out, w_fc, w_proj)
        w_in = lax.all_gather(blk, ("dp", "tensor"), axis=0).reshape(n_dp, n_t, 3, rows, D)
        w_in = w_in.transpose(2, 1, 0, 3, 4).reshape(3, n_t, D, D)
        vec_in = lax.all_gather(vectors.astype(BF), "dp", axis=1, tiled=True).astype(F32)
        weights = (w_in, jnp.pad(vec_in, ((0, 4), (0, 0))))
    w_full, vec, *saved, own_out = forward(kernel_dp, weights, tokens, documents, own)
    if not direct:
        w_full = w_in
    grads = backward(kernel_dp, w_full, vec, tokens, cotangent, saved, own_out, own)
    if direct:
        fin, vgrad, squares, own_grads, prev, all_out = grads
        moved = (own_grads, prev, all_out)
    else:
        tiles, vgrad, own_grad, prev = grads
        output = lax.all_gather(own_out, "tensor", axis=0, tiled=True)
        whole = lax.all_gather(own_grad, "tensor", axis=0, tiled=True).astype(F32)
        prevs = lax.all_gather(prev, "tensor", axis=0).astype(F32)
        for k in range(1, n_t):
            whole = whole.at[k * own - PREV : k * own].add(prevs[k])
        input_grad = whole.astype(BF)
        fin = tiles.reshape(3, n_t, n_dp, rows, D).transpose(2, 1, 0, 3, 4).reshape(-1, D)
        fin = lax.psum_scatter(fin, ("dp", "tensor"), scatter_dimension=0, tiled=True)
        fin = fin.reshape(3, rows, D).astype(F32)
        vgrad = lax.psum(vgrad, ("dp", "tensor"))
        squares = lax.psum(jnp.sum(fin * fin), ("dp", "tensor"))
        squares = jnp.pad(squares.reshape(1, 1), ((0, 7), (0, LANES - 1)))
        moved = None
    states = []
    for qkv, out, fc, proj, vec in (
        (w_qkv, w_out, w_fc, w_proj, vectors),
        (first_qkv, first_out, first_fc, first_proj, first_vec),
        (second_qkv, second_out, second_fc, second_proj, second_vec),
    ):
        states += [qkv.transpose(1, 0, 2), out, fc, proj.T, vec]
    outs = optimizer(squares, vgrad, fin, moved, states)
    if direct:
        output, input_grad, *outs = outs
    norm, *states = outs
    for k in (0, 5, 10):
        states[k] = states[k].transpose(1, 0, 2)
        states[k + 3] = states[k + 3].T
    return (output, input_grad, norm.reshape(()), *states)


def solution(mesh):
    rows = P("dp", None)
    weights = (P("dp", None, "tensor"), P("tensor", "dp"), P("dp", "tensor"), P("tensor", "dp"), P(None, "dp"))
    return jax.shard_map(
        body, mesh=mesh, in_specs=(rows, rows, rows) + weights * 3,
        out_specs=(rows, rows, P()) + weights * 3, check_vma=False,
    )
```
